256 devices in a mesh: dp: 128 (over y, z_hi, x, core), tensor: 2 (over z_lo).
Axes of the slice: x: 4, y: 4, z: 8 (z_hi: 4, z_lo: 2; z = z_hi * 2 + z_lo), core: 2. Of those that a mesh axis runs over, the one named last changes fastest.
Arguments:
- tokens: bfloat16 [256, 197, 384], P(('dp', 'tensor')), may hold values from -6 to 6
- attn_gain: float32 [384], replicated, may hold values from 0.5 to 1.5
- attn_shift: float32 [384], replicated, may hold values from -0.625 to 0.625
- w_qkv: bfloat16 [384, 6, 192], P(None, 'tensor'), may hold values from -0.3125 to 0.3125
- qv_bias: bfloat16 [6, 128], P('tensor'), may hold values from -0.3125 to 0.3125
- w_out: bfloat16 [6, 64, 384], P('tensor'), may hold values from -2 to 2
- out_bias: bfloat16 [384], replicated, may hold values from -1.25 to 1.25
- moe_gain: float32 [384], replicated, may hold values from 0.5 to 1.5
- moe_shift: float32 [384], replicated, may hold values from -0.625 to 0.625
- router: bfloat16 [384, 3], replicated, may hold values from -0.21875 to 0.21875
- w_in: bfloat16 [3, 384, 1536], P(None, None, 'tensor'), may hold values from -0.3125 to 0.3125
- in_bias: bfloat16 [3, 1536], P(None, 'tensor'), may hold values from -1.25 to 1.25
- w_exp: bfloat16 [3, 1536, 384], P(None, 'tensor'), may hold values from -0.4375 to 0.4375
- exp_bias: bfloat16 [3, 384], replicated, may hold values from -1.25 to 1.25
- routes: int32 [256, 197, 2], P('dp'), may hold values from 0 to 2, all different within a row
- cotangent: bfloat16 [256, 197, 384], P(('dp', 'tensor')), may hold values from -6 to 6
Outputs:
- block_out: bfloat16 [256, 197, 384], P(('dp', 'tensor'))
- grad_tokens: bfloat16 [256, 197, 384], P(('dp', 'tensor'))
- grad_attn_gain: float32 [384], replicated
- grad_attn_shift: float32 [384], replicated
- grad_w_qkv: float32 [384, 6, 192], P(None, 'tensor')
- grad_qv_bias: float32 [6, 128], P('tensor')
- grad_w_out: float32 [6, 64, 384], P('tensor')
- grad_out_bias: float32 [384], replicated
- grad_moe_gain: float32 [384], replicated
- grad_moe_shift: float32 [384], replicated
- grad_router: float32 [384, 3], replicated
- grad_w_in: float32 [3, 384, 1536], P(None, None, 'tensor')
- grad_in_bias: float32 [3, 1536], P(None, 'tensor')
- grad_w_exp: float32 [3, 1536, 384], P(None, 'tensor')
- grad_exp_bias: float32 [3, 384], replicated
The draws below stay inside these ranges and needn't reach their ends.
Inputs may be any that keep to these rules, and one draw needn't show every extreme that they name: `routes`: each token names 2 different experts.
All inputs are finite; a program needn't handle non-finite values.
Results may differ from the reference program's by a relative error of at most 0.019.
Values may be sent and summed in bfloat16 or wider, within the bound.
A program may use at most 128 MiB of HBM per device.

```python
import math
import jax
import jax.numpy as jnp
from jax import lax

D = 384
HEADS = 6
HD = 64
FF = 1536
EXPERTS = 3
TOPK = 2
SEQ = 197
CAP = 128
IMAGES = 256


def block_levels(own_key, extent, split, smallest, high):
    factor_of, own = 1.0, jax.random.fold_in(own_key, 6)
    for dim, shards_of in split:
        heights = jnp.exp(jax.random.uniform(jax.random.fold_in(own, dim), (shards_of,), jnp.float32, smallest / len(split), high / len(split)))
        factor_of = factor_of * jnp.repeat(heights, extent[dim] // shards_of).reshape([-1 if axis == dim else 1 for axis in range(len(extent))])
    return factor_of


def distinct(key, rows, amount, top, lift):
    ranking = jax.random.permutation(jax.random.fold_in(key, 1), amount)
    favour = ranking
    for power in range(3):
        favour = favour * favour // amount
    favour = favour * lift // amount
    lots = jax.random.randint(jax.random.fold_in(key, 2), (rows, amount), 0, 4096) + favour
    fixed_rows = jax.random.permutation(jax.random.fold_in(key, 3), rows)[jnp.arange(amount) % rows]
    lots = jnp.where(jnp.arange(rows)[:, None] == fixed_rows[None, :], 1 << 14, lots)
    merit = lots * amount + jnp.arange(amount)
    return lax.top_k(merit.astype(jnp.int32), top)[1].astype(jnp.int32)


def normal_values(stream_key, dims, width, limit, cuts=(), kind=jnp.bfloat16):
    level = block_levels(stream_key, dims, cuts, -0.22, 0.18) if cuts else 1.0
    array = jax.random.normal(stream_key, dims, jnp.float32) * width * level
    return jnp.minimum(jnp.maximum(array, -limit), limit).astype(kind)


def setup_inputs(seed: int = 0) -> dict:
    key_list = jax.random.split(jax.random.key(seed), 17)
    tokens = normal_values(key_list[0], (IMAGES, SEQ, D), 1.0, 6.0, ((0, 256),))
    attn_gain = jnp.clip(1.0 + 0.1 * jax.random.normal(key_list[1], (D,), jnp.float32), 0.5, 1.5)
    attn_shift = normal_values(key_list[2], (D,), 0.1, 0.625, (), jnp.float32)
    w_qkv = normal_values(key_list[3], (D, HEADS, 3 * HD), D ** -0.5, 0.3125, ((1, 2),))
    qv_bias = normal_values(key_list[4], (HEADS, 2 * HD), 0.05, 0.3125, ((0, 2),))
    w_out = normal_values(key_list[5], (HEADS, HD, D), (max(D // 48, 1)) ** -0.5, 2.0, ((0, 2),))
    out_bias = normal_values(key_list[6], (D,), 0.2, 1.25)
    moe_gain = jnp.clip(1.0 + 0.1 * jax.random.normal(key_list[7], (D,), jnp.float32), 0.5, 1.5)
    moe_shift = normal_values(key_list[8], (D,), 0.1, 0.625, (), jnp.float32)
    router = normal_values(key_list[9], (D, EXPERTS), (2 * D) ** -0.5, 0.21875)
    w_in = normal_values(key_list[10], (EXPERTS, D, FF), D ** -0.5, 0.3125, ((2, 2),))
    in_bias = normal_values(key_list[11], (EXPERTS, FF), 0.2, 1.25, ((1, 2),))
    w_exp = normal_values(key_list[12], (EXPERTS, FF, D), (FF // 8) ** -0.5, 0.4375, ((1, 2),))
    exp_bias = normal_values(key_list[13], (EXPERTS, D), 0.2, 1.25)
    routes = distinct(key_list[14], IMAGES * SEQ, EXPERTS, TOPK, 5461).reshape((IMAGES, SEQ, TOPK))
    cotangent = normal_values(key_list[15], (IMAGES, SEQ, D), 1.0, 6.0, ((0, 256),))
    return {"tokens": tokens, "attn_gain": attn_gain, "attn_shift": attn_shift, "w_qkv": w_qkv, "qv_bias": qv_bias, "w_out": w_out, "out_bias": out_bias, "moe_gain": moe_gain, "moe_shift": moe_shift, "router": router, "w_in": w_in, "in_bias": in_bias, "w_exp": w_exp, "exp_bias": exp_bias, "routes": routes, "cotangent": cotangent}


@jax.custom_vjp
def low(v):
    return lax.optimization_barrier(v.astype(jnp.bfloat16)).astype(jnp.float32)

@jax.custom_vjp
def low_back(v):
    return v

def low_keep(v):
    return (low(v), None)

def low_pass(kept, grad):
    return (grad,)

def back_keep(v):
    return (v, None)

def back_low(kept, grad):
    return (low(grad),)
low.defvjp(low_keep, low_pass)
low_back.defvjp(back_keep, back_low)
highest = lax.Precision.HIGHEST

def layer_norm(values, gain_vec, shift_vec):
    centre = values - lax.optimization_barrier(jnp.mean(values, axis=-1, keepdims=True))
    spread = lax.optimization_barrier(jnp.mean(centre * centre, axis=-1, keepdims=True))
    return centre * lax.rsqrt(spread + 1e-06) * gain_vec + shift_vec

def routing_tables(routes, capacity, experts):
    images, length, pick_count = routes.shape
    expert_ids = jnp.arange(experts, dtype=jnp.int32)
    chosen = (routes[..., None] == expert_ids).astype(jnp.int32)
    ordered = jnp.transpose(chosen, (0, 2, 1, 3)).reshape(images, pick_count * length, experts)
    earlier = jnp.cumsum(ordered, axis=1).astype(jnp.int32) - ordered
    slot_pos = lax.optimization_barrier(jnp.sum(earlier * ordered, axis=-1)).astype(jnp.int32).reshape(images, pick_count, length)
    slot_pos = jnp.transpose(slot_pos, (0, 2, 1))
    kept_mask = slot_pos < capacity
    target = jnp.where(kept_mask, routes * capacity + slot_pos, experts * capacity).astype(jnp.int32)
    return (chosen, kept_mask, target)

def softmax_last(values):
    row_top = lax.optimization_barrier(jnp.max(values, axis=-1, keepdims=True))
    weights = jnp.exp(values - row_top)
    return weights / lax.optimization_barrier(jnp.sum(weights, axis=-1, keepdims=True))

def forward_group(params, tok_piece, route_piece):
    attn_gain, attn_shift, w_qkv, qv_bias, w_out, out_bias, moe_gain, moe_shift, router, w_in, in_bias, w_exp, exp_bias = params
    images = tok_piece.shape[0]
    normed = low(layer_norm(tok_piece, attn_gain, attn_shift))
    project = jnp.einsum('gsd,dhc->gshc', normed, w_qkv, precision=highest)
    queries = low_back(low(project[..., :HD] + qv_bias[:, :HD]))
    key_rows = low_back(low(project[..., HD:2 * HD]))
    value_rows = low_back(low(project[..., 2 * HD:] + qv_bias[:, HD:]))
    raw_scores = low_back(jnp.einsum('gqhc,gkhc->ghqk', queries, key_rows, precision=highest))
    attn_probs = softmax_last(raw_scores * (1.0 / math.sqrt(HD)))
    context = low_back(low(jnp.einsum('ghqk,gkhc->gqhc', low(attn_probs), value_rows, precision=highest)))
    attended = low_back(jnp.einsum('gqhc,hcd->gqd', context, w_out, precision=highest))
    hidden_in = tok_piece + attended + out_bias
    moe_in = low(layer_norm(hidden_in, moe_gain, moe_shift))
    logits = jnp.einsum('gsd,de->gse', moe_in, router, precision=highest)
    gate_probs = softmax_last(logits)
    chosen, kept_mask, target = routing_tables(route_piece, CAP, EXPERTS)
    gate_pick = lax.optimization_barrier(jnp.sum(gate_probs[:, :, None, :] * chosen.astype(jnp.float32), axis=-1))
    combine_pick = jnp.where(kept_mask, gate_pick, jnp.zeros_like(gate_pick))
    onehot = (target[..., None] == jnp.arange(EXPERTS * CAP, dtype=jnp.int32)).astype(jnp.float32)
    dispatch = lax.optimization_barrier(jnp.sum(onehot, axis=2))
    combine = lax.optimization_barrier(jnp.sum(onehot * combine_pick[..., None], axis=2))
    slot_in = jnp.einsum('gst,gsd->gtd', dispatch, moe_in, precision=highest).reshape(images, EXPERTS, CAP, D)
    pre_act = low_back(jnp.einsum('gecd,edf->gecf', slot_in, w_in, precision=highest) + in_bias[None, :, None, :])
    activated = low(jax.nn.gelu(pre_act, approximate=False))
    slot_out = low_back(jnp.einsum('gecf,efd->gecd', activated, w_exp, precision=highest)) + exp_bias[None, :, None, :]
    moe_out = jnp.einsum('gst,gtd->gsd', combine, slot_out.reshape(images, EXPERTS * CAP, D), precision=highest)
    return hidden_in + moe_out

def to_float(array_in):
    return array_in.astype(jnp.float32)

def reference(tokens, attn_gain, attn_shift, w_qkv, qv_bias, w_out, out_bias, moe_gain, moe_shift, router, w_in, in_bias, w_exp, exp_bias, routes, cotangent):
    params = jax.tree.map(to_float, (attn_gain, attn_shift, w_qkv, qv_bias, w_out, out_bias, moe_gain, moe_shift, router, w_in, in_bias, w_exp, exp_bias))
    image_total = tokens.shape[0]
    group_size = math.gcd(image_total, 16)
    group_count = image_total // group_size
    tok_groups = tokens.astype(jnp.float32).reshape(group_count, group_size, SEQ, D)
    route_groups = routes.reshape(group_count, group_size, SEQ, TOPK)
    cot_groups = cotangent.astype(jnp.float32).reshape(group_count, group_size, SEQ, D)

    def one_group(running, pieces):
        tok_piece, route_piece, cot_piece = pieces

        def local_forward(param_set, tok_in):
            return forward_group(param_set, tok_in, route_piece)
        block_piece, pullback = jax.vjp(local_forward, params, tok_piece)
        grad_params, grad_piece = pullback(cot_piece)
        running = jax.tree.map(jnp.add, running, grad_params)
        return (running, (block_piece.astype(jnp.bfloat16), grad_piece.astype(jnp.bfloat16)))
    zero_grads = jax.tree.map(jnp.zeros_like, params)
    grad_totals, (block_out, grad_tokens) = lax.scan(one_group, zero_grads, (tok_groups, route_groups, cot_groups))
    return (block_out.reshape(image_total, SEQ, D), grad_tokens.reshape(image_total, SEQ, D), grad_totals[0], grad_totals[1], grad_totals[2], grad_totals[3], grad_totals[4], grad_totals[5], grad_totals[6], grad_totals[7], grad_totals[8], grad_totals[9], grad_totals[10], grad_totals[11], grad_totals[12])
```

```python
import functools
import math

import jax
import jax.numpy as jnp
from jax import lax
from jax.experimental import pallas as pl
from jax.experimental.pallas import tpu as pltpu
from jax.sharding import PartitionSpec as P

CAP = 128
MESH = pl.DeviceIdType.MESH
RING = 4
TILE_ROWS = 16
LANES = 128
CHAIN_ORDERS = (
    ("xa", "xb", "ya", "yb", "za", "zb"),
    ("xb", "xa", "yb", "ya", "zb", "za"),
    ("ya", "yb", "xa", "xb", "za", "zb"),
    ("yb", "ya", "xb", "xa", "zb", "za"),
)
HALVINGS = 5
STEPS = 7
SMALL_ROWS = 24
SHARED_ROWS = 16


def partners():
    me = lax.axis_index("dp")
    core = me % 2
    x = (me // 2) % RING
    z = (me // (2 * RING)) % RING
    y = me // (2 * RING * RING)

    def dp_index(y, z, x, core):
        return ((y * RING + z) * RING + x) * 2 + core

    def swap(v):
        return v + 1 - 2 * (v % 2)

    return {
        "core": ({"dp": dp_index(y, z, x, 1 - core)}, core),
        "xa": ({"dp": dp_index(y, z, swap(x), core)}, (x + 1) // 2 % 2),
        "xb": ({"dp": dp_index(y, z, RING - 1 - x, core)}, x // 2),
        "ya": ({"dp": dp_index(swap(y), z, x, core)}, (y + 1) // 2 % 2),
        "yb": ({"dp": dp_index(RING - 1 - y, z, x, core)}, y // 2),
        "za": ({"dp": dp_index(y, swap(z), x, core)}, (z + 1) // 2 % 2),
        "zb": ({"dp": dp_index(y, RING - 1 - z, x, core)}, z // 2),
        "pair": ({"tensor": 1 - lax.axis_index("tensor")}, lax.axis_index("tensor")),
    }


def add_tiles(dst, dst_at, left, left_at, right, right_at, count):
    step = max(k for k in range(1, 17) if count % k == 0)

    @pl.loop(0, count // step)
    def _(i):
        total = left[pl.ds(left_at + i * step, step)].astype(jnp.float32) + right[
            pl.ds(right_at + i * step, step)
        ].astype(jnp.float32)
        dst[pl.ds(dst_at + i * step, step)] = total.astype(dst.dtype)


def reduce_kernel(
    chains,
    grad_ref,
    small_ref,
    out_ref,
    small_out,
    held,
    landing,
    small_held,
    small_landing,
    send_sem,
    recv_sem,
    back_send,
    back_recv,
    small_send,
    small_recv,
):
    who = partners()
    barrier = pltpu.get_barrier_semaphore()
    for device, _ in who.values():
        pl.semaphore_signal(barrier, inc=1, device_id=device, device_id_type=MESH)
    pl.semaphore_wait(barrier, len(who))

    def remote(src, dst, send, recv, name):
        return pltpu.make_async_remote_copy(
            src_ref=src,
            dst_ref=dst,
            send_sem=send,
            recv_sem=recv,
            device_id=who[name][0],
            device_id_type=MESH,
        )

    count = len(chains)
    orders = [("core",) + CHAIN_ORDERS[c] for c in range(count)]
    base, size, landing_at = [], [], []
    start = 0
    for chain in chains:
        base.append(start)
        size.append(chain)
        start += chain
    spot = 0

    def send_step(c, k):
        nonlocal spot
        name = orders[c][k]
        source = grad_ref if k == 0 else held
        if k < HALVINGS:
            half = size[c] // 2
            bit = who[name][1]
            give = base[c] + (1 - bit) * half
            base[c] = base[c] + bit * half
            size[c] = half
        else:
            give = base[c]
        n = size[c]
        copy = remote(
            source.at[pl.ds(give, n)],
            landing.at[pl.ds(spot, n)],
            send_sem.at[c, k],
            recv_sem.at[c, k],
            name,
        )
        copy.start()
        landing_at.append(spot)
        spot += n
        return copy, landing_at[-1]

    small_order = ("pair", "core", "xa", "xb", "ya", "yb", "za", "zb")

    def small_step(k):
        rows = SHARED_ROWS if k == 0 else SMALL_ROWS
        copy = remote(
            small_ref.at[pl.ds(0, rows)] if k == 0 else small_held.at[k - 1],
            small_landing.at[k, pl.ds(0, rows)] if k == 0 else small_landing.at[k],
            small_send.at[k],
            small_recv.at[k],
            small_order[k],
        )
        copy.start()
        return copy

    unsent = []
    pending = [send_step(c, 0) for c in range(count)]
    small_pending = small_step(0)
    unsent.append(small_pending)
    for k in range(STEPS):
        for c in range(count):
            copy, where = pending[c]
            copy.wait_recv()
            if k >= HALVINGS:
                copy.wait_send()
            else:
                unsent.append(copy)
            add_tiles(
                held, base[c], grad_ref if k == 0 else held, base[c], landing, where, size[c]
            )
            if k + 1 < STEPS:
                pending[c] = send_step(c, k + 1)
        small_pending.wait_recv()
        if k == 0:
            small_held[0, :SHARED_ROWS] = small_ref[:SHARED_ROWS] + small_landing[0, :SHARED_ROWS]
            small_held[0, SHARED_ROWS:] = small_ref[SHARED_ROWS:]
        else:
            small_held[k] = small_held[k - 1] + small_landing[k]
        small_pending = small_step(k + 1)
        unsent.append(small_pending)

    def back_step(c, k):
        part = out_ref.at[pl.ds(base[c], size[c])]
        copy = remote(part, part, back_send.at[c, k], back_recv.at[c, k], orders[c][k])
        copy.start()
        unsent.append(copy)
        return copy

    back = []
    for c in range(count):
        step = max(k for k in range(1, 17) if size[c] % k == 0)

        @pl.loop(0, size[c] // step)
        def _(i, c=c, step=step):
            rows = pl.ds(base[c] + i * step, step)
            out_ref[rows] = held[rows]

        back.append(back_step(c, HALVINGS - 1))
    small_pending.wait_recv()
    small_out[...] = small_held[STEPS - 1] + small_landing[STEPS]
    for k in reversed(range(HALVINGS)):
        for c in range(count):
            back[c].wait_recv()
            base[c] = base[c] - who[orders[c][k]][1] * size[c]
            size[c] = size[c] * 2
            if k:
                back[c] = back_step(c, k - 1)
    for copy in unsent:
        copy.wait_send()


def reduce_all(grads, small, chains):
    tiles = sum(chains)
    landing = sum(
        c // 2 + c // 4 + c // 8 + c // 16 + 3 * (c // 32) for c in chains
    )
    count = len(chains)
    return pl.pallas_call(
        functools.partial(reduce_kernel, chains),
        out_shape=(
            jax.ShapeDtypeStruct((tiles, TILE_ROWS, LANES), jnp.bfloat16),
            jax.ShapeDtypeStruct((SMALL_ROWS, small.shape[1]), jnp.float32),
        ),
        in_specs=[pl.BlockSpec(memory_space=pltpu.VMEM)] * 2,
        out_specs=[pl.BlockSpec(memory_space=pltpu.VMEM)] * 2,
        scratch_shapes=[
            pltpu.VMEM((tiles, TILE_ROWS, LANES), jnp.bfloat16),
            pltpu.VMEM((landing, TILE_ROWS, LANES), jnp.bfloat16),
            pltpu.VMEM((STEPS, SMALL_ROWS, small.shape[1]), jnp.float32),
            pltpu.VMEM((STEPS + 1, SMALL_ROWS, small.shape[1]), jnp.float32),
            pltpu.SemaphoreType.DMA((count, STEPS)),
            pltpu.SemaphoreType.DMA((count, STEPS)),
            pltpu.SemaphoreType.DMA((count, HALVINGS)),
            pltpu.SemaphoreType.DMA((count, HALVINGS)),
            pltpu.SemaphoreType.DMA((STEPS + 1,)),
            pltpu.SemaphoreType.DMA((STEPS + 1,)),
        ],
        compiler_params=pltpu.CompilerParams(
            collective_id=0, has_side_effects=True, vmem_limit_bytes=48 * 1024 * 1024
        ),
    )(grads, small)


highest = lax.Precision.HIGHEST


def layer_norm(values, gain_vec, shift_vec):
    centre = values - jnp.mean(values, axis=-1, keepdims=True)
    spread = jnp.mean(centre * centre, axis=-1, keepdims=True)
    return centre * lax.rsqrt(spread + 1e-06) * gain_vec + shift_vec


def gelu_slope(values):
    return 0.5 * (1.0 + lax.erf(values * (1.0 / math.sqrt(2.0)))) + values * jnp.exp(
        -0.5 * values * values
    ) * (1.0 / math.sqrt(2.0 * math.pi))


def routing_tables(routes, capacity, experts):
    images, length, pick_count = routes.shape
    expert_ids = jnp.arange(experts, dtype=jnp.int32)
    chosen = (routes[..., None] == expert_ids).astype(jnp.int32)
    ordered = jnp.transpose(chosen, (0, 2, 1, 3)).reshape(images, pick_count * length, experts)
    earlier = jnp.cumsum(ordered, axis=1) - ordered
    slot_pos = jnp.sum(earlier * ordered, axis=-1).reshape(images, pick_count, length)
    slot_pos = jnp.transpose(slot_pos, (0, 2, 1))
    kept_mask = slot_pos < capacity
    target = jnp.where(kept_mask, routes * capacity + slot_pos, experts * capacity)
    return (chosen, kept_mask, target)


def on_device(
    tokens,
    attn_gain,
    attn_shift,
    w_qkv,
    qv_bias,
    w_out,
    out_bias,
    moe_gain,
    moe_shift,
    router,
    w_in,
    in_bias,
    w_exp,
    exp_bias,
    routes,
    cotangent,
):
    own_images, length, model_width = tokens.shape
    group_images = routes.shape[0]
    pick_count = routes.shape[2]
    experts = w_in.shape[0]
    local_heads = w_qkv.shape[1]
    head_dim = w_qkv.shape[2] // 3
    own_rows = own_images * length
    all_rows = group_images * length
    slot_count = experts * CAP
    score_scale = 1.0 / math.sqrt(head_dim)
    own_start = lax.axis_index("tensor") * own_images
    tok_flat = tokens.reshape(own_rows, model_width).astype(jnp.float32)
    normed_own, attn_norm_back = jax.vjp(layer_norm, tok_flat, attn_gain, attn_shift)
    normed_all = lax.all_gather(
        normed_own.astype(jnp.bfloat16).reshape(own_images, length, model_width),
        "tensor",
        axis=0,
        tiled=True,
    ).reshape(all_rows, model_width)
    w_qkv_flat = w_qkv.reshape(model_width, local_heads * 3 * head_dim)
    project = jnp.dot(normed_all, w_qkv_flat, preferred_element_type=jnp.float32).reshape(
        group_images, length, local_heads, 3 * head_dim
    )
    bias_float = qv_bias.astype(jnp.float32)
    queries = (project[..., :head_dim] + bias_float[:, :head_dim]).astype(jnp.bfloat16)
    key_rows = project[..., head_dim : 2 * head_dim].astype(jnp.bfloat16)
    value_rows = (project[..., 2 * head_dim :] + bias_float[:, head_dim:]).astype(jnp.bfloat16)
    scores = (
        jnp.einsum("gqhc,gkhc->ghqk", queries, key_rows, preferred_element_type=jnp.float32)
        * score_scale
    )
    row_top = jnp.max(scores, axis=-1, keepdims=True)
    weights = jnp.exp(scores - row_top)
    totals = jnp.sum(weights, axis=-1, keepdims=True)
    log_total = row_top + jnp.log(totals)
    attn_probs = weights / totals
    context = jnp.einsum(
        "ghqk,gkhc->gqhc",
        attn_probs.astype(jnp.bfloat16),
        value_rows,
        preferred_element_type=jnp.float32,
    ).astype(jnp.bfloat16)
    context_flat = context.reshape(all_rows, local_heads * head_dim)
    w_out_flat = w_out.reshape(local_heads * head_dim, model_width)
    row_part = context_flat
    attended = lax.psum_scatter(
        jnp.dot(row_part, w_out_flat, preferred_element_type=jnp.float32).astype(jnp.bfloat16),
        "tensor",
        scatter_dimension=0,
        tiled=True,
    ).astype(jnp.float32)
    hidden_in = tok_flat + attended + out_bias.astype(jnp.float32)
    moe_own, moe_norm_back = jax.vjp(layer_norm, hidden_in, moe_gain, moe_shift)
    moe_low = moe_own.astype(jnp.bfloat16)
    moe_all = lax.all_gather(
        moe_low.reshape(own_images, length, model_width), "tensor", axis=0, tiled=True
    )
    logits = jnp.dot(
        moe_all.reshape(all_rows, model_width), router, preferred_element_type=jnp.float32
    ).reshape(group_images, length, experts)
    logit_top = jnp.max(logits, axis=-1, keepdims=True)
    gate_exp = jnp.exp(logits - logit_top)
    gate_probs = gate_exp / jnp.sum(gate_exp, axis=-1, keepdims=True)
    chosen, kept_mask, target = routing_tables(routes, CAP, experts)
    chosen_float = chosen.astype(jnp.float32)
    kept_float = kept_mask.astype(jnp.float32)
    gate_pick = jnp.sum(gate_probs[:, :, None, :] * chosen_float, axis=-1)
    combine_pick = gate_pick * kept_float
    slot_ids = jnp.arange(slot_count, dtype=jnp.int32)
    onehot = (target[..., None] == slot_ids).astype(jnp.bfloat16)
    dispatch = jnp.sum(onehot, axis=2).reshape(group_images, length, experts, CAP)
    slot_in = jnp.einsum(
        "gsec,gsd->egcd", dispatch, moe_all, preferred_element_type=jnp.float32
    ).astype(jnp.bfloat16)
    pre_act = (
        jnp.einsum("egcd,edf->egcf", slot_in, w_in, preferred_element_type=jnp.float32)
        + in_bias.astype(jnp.float32)[:, None, None, :]
    )
    activated = jax.nn.gelu(pre_act, approximate=False).astype(jnp.bfloat16)
    expert_part = jnp.einsum(
        "egcf,efd->gecd", activated, w_exp, preferred_element_type=jnp.float32
    ).reshape(group_images, slot_count, model_width)
    safe_target = jnp.minimum(target, slot_count - 1).reshape(group_images, length * pick_count)
    picked = jnp.take_along_axis(expert_part, safe_target[:, :, None], axis=1).reshape(
        group_images, length, pick_count, model_width
    )
    mixed_part = jnp.sum(picked * combine_pick[..., None], axis=2).reshape(all_rows, model_width)
    moe_sum = lax.psum_scatter(
        mixed_part.astype(jnp.bfloat16), "tensor", scatter_dimension=0, tiled=True
    ).astype(jnp.float32)
    own_weight = lax.dynamic_slice_in_dim(combine_pick, own_start, own_images, 0).reshape(
        own_rows, pick_count
    )
    own_chosen = lax.dynamic_slice_in_dim(chosen_float, own_start, own_images, 0).reshape(
        own_rows, pick_count, experts
    )
    own_kept = lax.dynamic_slice_in_dim(kept_float, own_start, own_images, 0).reshape(
        own_rows, pick_count
    )
    own_gates = lax.dynamic_slice_in_dim(gate_probs, own_start, own_images, 0).reshape(
        own_rows, experts
    )
    own_share = jnp.sum(own_weight[..., None] * own_chosen, axis=1)
    exp_bias_float = exp_bias.astype(jnp.float32)
    block_out = hidden_in + moe_sum + jnp.dot(own_share, exp_bias_float, precision=highest)
    cot_own = cotangent.reshape(own_rows, model_width).astype(jnp.float32)
    cot_all = lax.all_gather(cotangent, "tensor", axis=0, tiled=True).astype(jnp.float32)
    scaled = (combine_pick[..., None] * cot_all[:, :, None, :]).astype(jnp.bfloat16)
    grad_slot = (
        jnp.einsum("gskt,gskd->gtd", onehot, scaled, preferred_element_type=jnp.float32)
        .astype(jnp.bfloat16)
        .reshape(group_images, experts, CAP, model_width)
    )
    grad_w_exp = jnp.einsum(
        "egcf,gecd->efd", activated, grad_slot, preferred_element_type=jnp.float32
    )
    grad_act = jnp.einsum("gecd,efd->egcf", grad_slot, w_exp, preferred_element_type=jnp.float32)
    grad_pre = (grad_act * gelu_slope(pre_act)).astype(jnp.bfloat16)
    grad_w_in = jnp.einsum("egcd,egcf->edf", slot_in, grad_pre, preferred_element_type=jnp.float32)
    grad_in_bias = jnp.sum(grad_pre.astype(jnp.float32), axis=(1, 2))
    grad_slot_in = jnp.einsum(
        "egcf,edf->gecd", grad_pre, w_in, preferred_element_type=jnp.float32
    ).reshape(group_images, slot_count, model_width)
    back_picked = jnp.take_along_axis(grad_slot_in, safe_target[:, :, None], axis=1).reshape(
        group_images, length, pick_count, model_width
    )
    grad_moe_part = jnp.sum(back_picked * kept_float[..., None], axis=2).reshape(
        all_rows, model_width
    )
    grad_pick_part = jnp.sum(picked * cot_all[:, :, None, :], axis=-1).reshape(all_rows, pick_count)
    grad_moe_own, grad_pick_own = (
        lax.psum_scatter(
            grad_moe_part.astype(jnp.bfloat16), "tensor", scatter_dimension=0, tiled=True
        ).astype(jnp.float32),
        lax.psum_scatter(
            grad_pick_part.astype(jnp.bfloat16), "tensor", scatter_dimension=0, tiled=True
        ).astype(jnp.float32),
    )
    cot_bias = jnp.dot(cot_own, exp_bias_float.T, precision=highest)
    pick_bias = jnp.sum(own_chosen * cot_bias[:, None, :], axis=-1)
    grad_gate_pick = (grad_pick_own + pick_bias) * own_kept
    grad_gates = jnp.sum(grad_gate_pick[..., None] * own_chosen, axis=1)
    grad_logits = own_gates * (grad_gates - jnp.sum(own_gates * grad_gates, axis=-1, keepdims=True))
    grad_router = jnp.einsum(
        "sd,se->de", moe_low.astype(jnp.float32), grad_logits, precision=highest
    )
    grad_moe_total = grad_moe_own + jnp.dot(
        grad_logits, router.astype(jnp.float32).T, precision=highest
    )
    grad_hidden_norm, grad_moe_gain, grad_moe_shift = moe_norm_back(grad_moe_total)
    grad_hidden = cot_own + grad_hidden_norm
    grad_out_bias = jnp.sum(grad_hidden, axis=0)
    grad_exp_bias = jnp.einsum("se,sd->ed", own_share, cot_own, precision=highest)
    grad_hidden_all = lax.all_gather(
        grad_hidden.astype(jnp.bfloat16).reshape(own_images, length, model_width),
        "tensor",
        axis=0,
        tiled=True,
    ).reshape(all_rows, model_width)
    grad_w_out = jnp.einsum(
        "rc,rd->cd", context_flat, grad_hidden_all, preferred_element_type=jnp.float32
    ).reshape(local_heads, head_dim, model_width)
    grad_context = (
        lax.dot_general(
            grad_hidden_all,
            w_out_flat,
            (((1,), (1,)), ((), ())),
            preferred_element_type=jnp.float32,
        )
        .astype(jnp.bfloat16)
        .reshape(group_images, length, local_heads, head_dim)
    )
    scores_again = (
        jnp.einsum("gqhc,gkhc->ghqk", queries, key_rows, preferred_element_type=jnp.float32)
        * score_scale
    )
    probs_again = jnp.exp(scores_again - log_total)
    grad_probs = jnp.einsum(
        "gqhc,gkhc->ghqk", grad_context, value_rows, preferred_element_type=jnp.float32
    )
    row_dot = jnp.sum(grad_probs * probs_again, axis=-1, keepdims=True)
    grad_raw = (probs_again * (grad_probs - row_dot) * score_scale).astype(jnp.bfloat16)
    grad_queries = jnp.einsum(
        "ghqk,gkhc->gqhc", grad_raw, key_rows, preferred_element_type=jnp.float32
    ).astype(jnp.bfloat16)
    grad_keys = jnp.einsum(
        "ghqk,gqhc->gkhc", grad_raw, queries, preferred_element_type=jnp.float32
    ).astype(jnp.bfloat16)
    grad_values = jnp.einsum(
        "ghqk,gqhc->gkhc",
        probs_again.astype(jnp.bfloat16),
        grad_context,
        preferred_element_type=jnp.float32,
    ).astype(jnp.bfloat16)
    grad_project = jnp.concatenate([grad_queries, grad_keys, grad_values], axis=-1).reshape(
        all_rows, local_heads * 3 * head_dim
    )
    grad_w_qkv = jnp.einsum(
        "rd,rc->dc", normed_all, grad_project, preferred_element_type=jnp.float32
    ).reshape(model_width, local_heads, 3 * head_dim)
    grad_qv_bias = jnp.concatenate(
        [
            jnp.sum(grad_queries.astype(jnp.float32), axis=(0, 1)),
            jnp.sum(grad_values.astype(jnp.float32), axis=(0, 1)),
        ],
        axis=-1,
    )
    row_part = grad_project
    grad_normed = lax.psum_scatter(
        lax.dot_general(
            row_part, w_qkv_flat, (((1,), (1,)), ((), ())), preferred_element_type=jnp.float32
        ).astype(jnp.bfloat16),
        "tensor",
        scatter_dimension=0,
        tiled=True,
    ).astype(jnp.float32)
    grad_tok_norm, grad_attn_gain, grad_attn_shift = attn_norm_back(grad_normed)
    grad_tokens = grad_hidden + grad_tok_norm
    big = [grad_w_in, grad_w_exp, grad_w_qkv, grad_w_out]
    sizes = [leaf.size for leaf in big]
    chains = (256, 256, 256, 256)
    total = sum(chains) * TILE_ROWS * LANES
    packed = jnp.concatenate(
        [leaf.astype(jnp.bfloat16).reshape(-1) for leaf in big]
        + [jnp.zeros((total - sum(sizes),), jnp.bfloat16)]
    ).reshape(-1, TILE_ROWS, LANES)
    small = jnp.concatenate(
        [
            jnp.stack([grad_attn_gain, grad_attn_shift, grad_out_bias, grad_moe_gain, grad_moe_shift]),
            grad_router.T,
            grad_exp_bias,
            jnp.zeros((5, model_width), jnp.float32),
            grad_in_bias.reshape(-1, model_width),
            grad_qv_bias.reshape(-1, model_width),
            jnp.zeros((1, model_width), jnp.float32),
        ]
    )
    summed, small = reduce_all(packed, small, chains)
    flat = summed.reshape(-1)
    parts, at = [], 0
    for leaf in big:
        parts.append(flat[at : at + leaf.size].astype(jnp.float32).reshape(leaf.shape))
        at += leaf.size
    grad_w_in, grad_w_exp, grad_w_qkv, grad_w_out = parts
    grad_attn_gain, grad_attn_shift, grad_out_bias, grad_moe_gain, grad_moe_shift = small[:5]
    grad_router = small[5:8].T
    grad_exp_bias = small[8:11]
    grad_in_bias = small[16:22].reshape(grad_in_bias.shape)
    grad_qv_bias = small[22:23].reshape(grad_qv_bias.shape)
    return (
        block_out.astype(jnp.bfloat16).reshape(own_images, length, model_width),
        grad_tokens.astype(jnp.bfloat16).reshape(own_images, length, model_width),
        grad_attn_gain,
        grad_attn_shift,
        grad_w_qkv,
        grad_qv_bias,
        grad_w_out,
        grad_out_bias,
        grad_moe_gain,
        grad_moe_shift,
        grad_router,
        grad_w_in,
        grad_in_bias,
        grad_w_exp,
        grad_exp_bias,
    )


def solution(mesh):
    placed = (
        P(("dp", "tensor"), None, None),
        P(),
        P(),
        P(None, "tensor", None),
        P("tensor", None),
        P("tensor", None, None),
        P(),
        P(),
        P(),
        P(),
        P(None, None, "tensor"),
        P(None, "tensor"),
        P(None, "tensor", None),
        P(),
        P("dp", None, None),
        P(("dp", "tensor"), None, None),
    )
    return jax.shard_map(
        on_device,
        mesh=mesh,
        in_specs=placed,
        out_specs=(
            P(("dp", "tensor"), None, None),
            P(("dp", "tensor"), None, None),
            P(),
            P(),
            P(None, "tensor", None),
            P("tensor", None),
            P("tensor", None, None),
            P(),
            P(),
            P(),
            P(),
            P(None, None, "tensor"),
            P(None, "tensor"),
            P(None, "tensor", None),
            P(),
        ),
        check_vma=False,
    )
```

```python
import functools
import math

import jax
import jax.numpy as jnp
from jax import lax
from jax.experimental import pallas as pl
from jax.experimental.pallas import tpu as pltpu
from jax.sharding import PartitionSpec as P

MESH = pl.DeviceIdType.MESH
RING = 4
D, SEQ, HEADS, HD, FF, EXPERTS, CAP = 384, 197, 3, 64, 768, 3, 128
ROWS = 208
QKV = 3 * HEADS * HD
TILE_ROWS = 16
LANES = 128
QKV_LANES = 640
IN_TILES = (D // TILE_ROWS) * (FF // LANES)
EXP_TILES = (FF // TILE_ROWS) * (D // LANES)
MOE_TILES = EXPERTS * (IN_TILES + EXP_TILES)
QKV_TILES = (D // TILE_ROWS) * (QKV_LANES // LANES)
OUT_TILES = (HEADS * HD // TILE_ROWS) * (D // LANES)
MOE_CHAINS = (224, 224, 224, 192)
ATTN_CHAINS = (64, 32, 32, 32)
CHAINS = MOE_CHAINS + ATTN_CHAINS
TILES = sum(CHAINS)
ORDERS = (
    ("core", "xa", "xb", "ya", "yb", "za", "zb"),
    ("core", "xb", "xa", "yb", "ya", "zb", "za"),
    ("core", "ya", "yb", "xa", "xb", "za", "zb"),
    ("core", "yb", "ya", "xb", "xa", "zb", "za"),
)
HALVINGS = 5
STEPS = 7
LANDING = sum(c // 2 + c // 4 + c // 8 + c // 16 + 3 * (c // 32) for c in CHAINS)
SMALL_ORDER = ("pair", "core", "xa", "xb", "ya", "yb", "za", "zb")
SMALL_ROWS = 24
SHARED_ROWS = 16
F32 = jnp.float32
BF16 = jnp.bfloat16
HIGHEST = lax.Precision.HIGHEST


def partners():
    me = lax.axis_index("dp")
    core = me % 2
    x = (me // 2) % RING
    z = (me // (2 * RING)) % RING
    y = me // (2 * RING * RING)

    def dp_index(y, z, x, core):
        return ((y * RING + z) * RING + x) * 2 + core

    def swap(v):
        return v + 1 - 2 * (v % 2)

    return {
        "core": ({"dp": dp_index(y, z, x, 1 - core)}, core),
        "xa": ({"dp": dp_index(y, z, swap(x), core)}, (x + 1) // 2 % 2),
        "xb": ({"dp": dp_index(y, z, RING - 1 - x, core)}, x // 2),
        "ya": ({"dp": dp_index(swap(y), z, x, core)}, (y + 1) // 2 % 2),
        "yb": ({"dp": dp_index(RING - 1 - y, z, x, core)}, y // 2),
        "za": ({"dp": dp_index(y, swap(z), x, core)}, (z + 1) // 2 % 2),
        "zb": ({"dp": dp_index(y, RING - 1 - z, x, core)}, z // 2),
        "pair": ({"tensor": 1 - lax.axis_index("tensor")}, lax.axis_index("tensor")),
    }


def dot(a, b, dims=((1,), (0,)), precision=None):
    return lax.dot_general(
        a, b, (dims, ((), ())), precision=precision, preferred_element_type=F32
    )


LAST = ((1,), (1,))
FIRST = ((0,), (0,))


def normalize(v):
    centre = v - jnp.mean(v, axis=-1, keepdims=True)
    r = lax.rsqrt(jnp.mean(centre * centre, axis=-1, keepdims=True) + 1e-06)
    return centre * r, r


def norm_back(grad, xhat, r, gain):
    g = grad * gain
    return r * (
        g
        - jnp.mean(g, axis=-1, keepdims=True)
        - xhat * jnp.mean(g * xhat, axis=-1, keepdims=True)
    )


def column_sum(v):
    return jnp.sum(v, axis=0, keepdims=True)


def add_tiles(ref, at, landing, landing_at, count):
    step = max(k for k in range(1, 17) if count % k == 0)

    @pl.loop(0, count // step)
    def _(i):
        rows = pl.ds(at + i * step, step)
        total = ref[rows].astype(F32) + landing[pl.ds(landing_at + i * step, step)].astype(F32)
        ref[rows] = total.astype(ref.dtype)


def store_tiles(ref, at, value):
    rows, lanes = value.shape
    per = rows // TILE_ROWS
    for j in range(-(-lanes // LANES)):
        part = value[:, j * LANES : min((j + 1) * LANES, lanes)]
        if part.shape[1] < LANES:
            part = jnp.concatenate(
                [part, jnp.zeros((rows, LANES - part.shape[1]), part.dtype)], axis=1
            )
        ref[at + j * per : at + (j + 1) * per] = part.astype(BF16).reshape(per, TILE_ROWS, LANES)


def block_kernel(
    tok_ref,
    cot_ref,
    vec_ref,
    w_qkv_ref,
    qkv_bias_ref,
    w_out_ref,
    w_in_ref,
    in_bias_ref,
    w_exp_ref,
    exp_bias_ref,
    route_col_ref,
    route_row_ref,
    block_ref,
    grad_tok_ref,
    sum_ref,
    small_out,
    held,
    landing,
    small_held,
    small_landing,
    normed,
    cots,
    moes,
    ghs,
    att_part,
    mix_part,
    gmoe_part,
    gate_part,
    gnorm_part,
    q_all,
    k_all,
    v_all,
    probs,
    ctx,
    gproj,
    slot_in,
    slot_cot,
    act_all,
    gpre_all,
    scaled_all,
    gslot_all,
    gback_all,
    attn_xhat,
    moe_xhat,
    hidden_ref,
    pair_send,
    pair_recv,
    send_sem,
    recv_sem,
    back_send,
    back_recv,
    small_send,
    small_recv,
):
    who = partners()
    barrier = pltpu.get_barrier_semaphore()
    for device, _ in who.values():
        pl.semaphore_signal(barrier, inc=1, device_id=device, device_id_type=MESH)

    def remote(src, dst, send, recv, name):
        copy = pltpu.make_async_remote_copy(
            src_ref=src,
            dst_ref=dst,
            send_sem=send,
            recv_sem=recv,
            device_id=who[name][0],
            device_id_type=MESH,
        )
        copy.start()
        return copy

    unsent = []

    def exchange(i, src, dst):
        copy = remote(src, dst, pair_send.at[i], pair_recv.at[i], "pair")
        unsent.append(copy)
        return copy

    spots = [0]

    class Chain:
        def __init__(self, c):
            self.c, self.order = c, ORDERS[c % len(ORDERS)]
            self.base, self.size, self.k = sum(CHAINS[:c]), CHAINS[c], 0

        def send(self):
            c, k = self.c, self.k
            name = self.order[k]
            give = self.base
            if k < HALVINGS:
                self.size //= 2
                bit = who[name][1]
                give = self.base + (1 - bit) * self.size
                self.base = self.base + bit * self.size
            self.spot = spots[0]
            spots[0] += self.size
            self.copy = remote(
                held.at[pl.ds(give, self.size)],
                landing.at[pl.ds(self.spot, self.size)],
                send_sem.at[c, k],
                recv_sem.at[c, k],
                name,
            )

        def send_back(self, k):
            self.back = k
            part = sum_ref.at[pl.ds(self.base, self.size)]
            self.copy = remote(
                part, part, back_send.at[self.c, k], back_recv.at[self.c, k], self.order[k]
            )
            unsent.append(self.copy)

        def advance(self):
            if self.k < STEPS:
                self.copy.wait_recv()
                if self.k < HALVINGS:
                    unsent.append(self.copy)
                else:
                    self.copy.wait_send()
                add_tiles(held, self.base, landing, self.spot, self.size)
                self.k += 1
                if self.k < STEPS:
                    self.send()
                    return
                step = max(k for k in range(1, 17) if self.size % k == 0)

                @pl.loop(0, self.size // step)
                def _(i):
                    rows = pl.ds(self.base + i * step, step)
                    sum_ref[rows] = held[rows]

                self.send_back(HALVINGS - 1)
            elif self.back >= 0:
                self.copy.wait_recv()
                self.base = self.base - who[self.order[self.back]][1] * self.size
                self.size = self.size * 2
                if self.back:
                    self.send_back(self.back - 1)
                else:
                    self.back = -1

    def small_step(k):
        rows = SHARED_ROWS if k == 0 else SMALL_ROWS
        copy = remote(
            small_held.at[k, pl.ds(0, rows)],
            small_landing.at[k, pl.ds(0, rows)],
            small_send.at[k],
            small_recv.at[k],
            SMALL_ORDER[k],
        )
        unsent.append(copy)
        return copy

    attn_gain, attn_shift = vec_ref[0:1], vec_ref[1:2]
    moe_gain, moe_shift, out_bias = vec_ref[2:3], vec_ref[3:4], vec_ref[4:5]

    tok = tok_ref[...].astype(F32)
    xhat, attn_r = normalize(tok)
    attn_xhat[...] = xhat
    normed[0] = (xhat * attn_gain + attn_shift).astype(BF16)
    pl.semaphore_wait(barrier, len(who))
    normed_copy = exchange(0, normed.at[0], normed.at[1])
    cot_copy = exchange(1, cot_ref, cots.at[1])
    cots[0] = cot_ref[...]

    key_mask = lax.broadcasted_iota(jnp.int32, (ROWS, ROWS), 1) < SEQ

    def project(i):
        proj = dot(normed[i], w_qkv_ref[...]) + qkv_bias_ref[...]
        for h in range(HEADS):
            at = h * 3 * HD
            q_all[i, h] = proj[:, at : at + HD].astype(BF16)
            k_all[i, h] = proj[:, at + HD : at + 2 * HD].astype(BF16)
            v_all[i, h] = proj[:, at + 2 * HD : at + 3 * HD].astype(BF16)

    def attend(i):
        total = jnp.zeros((ROWS, D), F32)
        for h in range(HEADS):
            scores = dot(q_all[i, h], k_all[i, h], LAST) * (1.0 / math.sqrt(HD))
            scores = jnp.where(key_mask, scores, -1e30)
            weights = jnp.exp(scores - jnp.max(scores, axis=-1, keepdims=True))
            p = weights / jnp.sum(weights, axis=-1, keepdims=True)
            probs[i, h] = p
            c = dot(p.astype(BF16), v_all[i, h]).astype(BF16)
            ctx[h, i] = c
            total += dot(c, w_out_ref[h * HD : (h + 1) * HD])
        return total

    tensor = lax.axis_index("tensor")
    before = (
        lax.broadcasted_iota(jnp.int32, (ROWS, ROWS), 1)
        < lax.broadcasted_iota(jnp.int32, (ROWS, ROWS), 0)
    ).astype(BF16)
    lane = lax.broadcasted_iota(jnp.int32, (ROWS, LANES), 1)
    sub = lax.broadcasted_iota(jnp.int32, (8, ROWS), 0)
    slot_lane = lax.broadcasted_iota(jnp.int32, (ROWS, CAP), 1).astype(F32)
    slot_sub = lax.broadcasted_iota(jnp.int32, (CAP, ROWS), 0).astype(F32)
    pos_col, pos_row = [], []
    for i in range(2):
        mine = tensor == i
        col = jnp.where(mine, route_col_ref[0], route_col_ref[1])
        row = jnp.where(mine, route_row_ref[0], route_row_ref[1])
        a0, a1 = col[:, 0:1] == lane, col[:, 1:2] == lane
        f0, f1 = a0.astype(F32), a1.astype(F32)
        c0 = dot(before, f0.astype(BF16))
        c1 = dot(before, f1.astype(BF16)) + column_sum(f0)
        pos_col.append(jnp.where(a0, c0, jnp.where(a1, c1, -1.0)))
        a0, a1 = row[0:1] == sub, row[1:2] == sub
        f0, f1 = a0.astype(F32), a1.astype(F32)
        c0 = dot(f0.astype(BF16), before, LAST)
        c1 = dot(f1.astype(BF16), before, LAST) + jnp.sum(f0, axis=1, keepdims=True)
        pos_row.append(jnp.where(a0, c0, jnp.where(a1, c1, -1.0)))
    kept_row = [((p >= 0.0) & (p < CAP)).astype(F32) for p in pos_row]

    def dispatch(i, e):
        return (pos_col[i][:, e : e + 1] == slot_lane).astype(F32)

    def dispatch_t(i, e):
        return (pos_row[i][e : e + 1] == slot_sub).astype(F32)

    project(0)
    normed_copy.wait_recv()
    project(1)
    att_part[0] = attend(1).astype(BF16)
    att_copy = exchange(2, att_part.at[0], att_part.at[1])
    own_part = attend(0)
    cot_copy.wait_recv()
    for i in range(2):
        for e in range(EXPERTS):
            slot_cot[e, i * CAP : (i + 1) * CAP] = dot(
                dispatch_t(i, e).astype(BF16), cots[i]
            ).astype(BF16)
    att_copy.wait_recv()
    hidden = tok + (own_part.astype(BF16).astype(F32) + att_part[1].astype(F32)) + out_bias
    hidden_ref[...] = hidden
    xhat, moe_r = normalize(hidden)
    moe_xhat[...] = xhat
    moes[0] = (xhat * moe_gain + moe_shift).astype(BF16)
    moe_copy = exchange(3, moes.at[0], moes.at[1])

    router = vec_ref[8:16].astype(BF16)
    expert_rows = sub < EXPERTS

    def gate(i):
        logits = jnp.where(expert_rows, dot(router, moes[i], LAST), -1e30)
        weights = jnp.exp(logits - jnp.max(logits, axis=0, keepdims=True))
        return weights / column_sum(weights)

    gates, slot_weight = [None, None], [[None] * EXPERTS, [None] * EXPERTS]

    def fill_slots(i):
        gates[i] = gate(i)
        for e in range(EXPERTS):
            pick = dispatch_t(i, e)
            slot_in[e, i * CAP : (i + 1) * CAP] = dot(pick.astype(BF16), moes[i]).astype(BF16)
            slot_weight[i][e] = jnp.sum(pick * gates[i][e : e + 1], axis=1, keepdims=True)

    fill_slots(0)
    moe_copy.wait_recv()
    fill_slots(1)

    gate_rows = [[None] * EXPERTS, [None] * EXPERTS]
    small_held[0] = jnp.zeros((SMALL_ROWS, D), F32)
    for e in range(EXPERTS):
        weight = jnp.concatenate([slot_weight[0][e], slot_weight[1][e]], axis=0)
        pre = dot(slot_in[e], w_in_ref[e]) + in_bias_ref[e : e + 1].astype(F32)
        half = 0.5 * (1.0 + lax.erf(pre * (1.0 / math.sqrt(2.0))))
        act_all[e] = (pre * half).astype(BF16)
        slope = half + pre * jnp.exp(-0.5 * pre * pre) * (1.0 / math.sqrt(2.0 * math.pi))
        g = slot_cot[e].astype(F32)
        gs = (g * weight).astype(BF16)
        gslot_all[e] = gs
        gpre = (dot(gs, w_exp_ref[e], LAST) * slope).astype(BF16)
        gpre_all[e] = gpre
        gback_all[e] = dot(gpre, w_in_ref[e], LAST).astype(BF16)
        slot_out = dot(act_all[e], w_exp_ref[e])
        scaled_all[e] = (slot_out * weight).astype(BF16)
        slot_gate = jnp.sum(slot_out * g, axis=1, keepdims=True)
        for i in range(2):
            gate_rows[i][e] = column_sum(
                dispatch_t(i, e) * slot_gate[i * CAP : (i + 1) * CAP]
            )

    def combine(i, ref):
        total = jnp.zeros((ROWS, D), F32)
        for e in range(EXPERTS):
            total += dot(dispatch(i, e).astype(BF16), ref[e, i * CAP : (i + 1) * CAP])
        return total

    def gate_grads(i):
        return jnp.concatenate(gate_rows[i] + [jnp.zeros((8 - EXPERTS, ROWS), F32)], axis=0)

    gmoe_part[0] = combine(1, gback_all).astype(BF16)
    gmoe_copy = exchange(4, gmoe_part.at[0], gmoe_part.at[1])
    gate_part[0] = gate_grads(1)
    gate_copy = exchange(5, gate_part.at[0], gate_part.at[1])
    mix_part[0] = combine(1, scaled_all).astype(BF16)
    mix_copy = exchange(6, mix_part.at[0], mix_part.at[1])

    for e in range(EXPERTS):
        at = e * (IN_TILES + EXP_TILES)
        store_tiles(held, at, dot(slot_in[e], gpre_all[e], FIRST))
        store_tiles(held, at + IN_TILES, dot(act_all[e], gslot_all[e], FIRST))
        bias = column_sum(gpre_all[e].astype(F32))
        for j in range(FF // D):
            small_held[0, 16 + 2 * e + j : 17 + 2 * e + j] = bias[:, j * D : (j + 1) * D]
    chains = [Chain(c) for c in range(len(CHAINS))]
    moe_chains = chains[: len(MOE_CHAINS)]
    attn_chains = chains[len(MOE_CHAINS) :]
    for chain in moe_chains:
        chain.send()

    own_gmoe = combine(0, gback_all).astype(BF16).astype(F32)
    own_mix = combine(0, scaled_all).astype(BF16).astype(F32)
    own_gate = gate_grads(0)
    cot = cot_ref[...].astype(F32)
    bias_rows = jnp.concatenate(
        [exp_bias_ref[...], jnp.zeros((8 - EXPERTS, D), BF16)], axis=0
    )
    share = gates[0] * kept_row[0]
    bias_grad = dot(bias_rows, cot_ref[...], LAST)
    gate_copy.wait_recv()
    grad_gates = (own_gate + gate_part[1] + bias_grad) * kept_row[0]
    grad_logits = gates[0] * (grad_gates - column_sum(gates[0] * grad_gates))
    small_held[0, 5:8] = dot(grad_logits, moes[0].astype(F32), precision=HIGHEST)[:EXPERTS]
    small_held[0, 8:11] = dot(share, cot, precision=HIGHEST)[:EXPERTS]
    router_back = dot(grad_logits, vec_ref[8:16], FIRST, HIGHEST)
    gmoe_copy.wait_recv()
    gmoe = own_gmoe + gmoe_part[1].astype(F32) + router_back
    grad_hidden = cot + norm_back(gmoe, moe_xhat[...], moe_r, moe_gain)
    ghs[0] = grad_hidden.astype(BF16)
    gh_copy = exchange(7, ghs.at[0], ghs.at[1])
    small_held[0, 2:3] = column_sum(grad_hidden)
    small_held[0, 3:4] = column_sum(gmoe * moe_xhat[...])
    small_held[0, 4:5] = column_sum(gmoe)
    mix_copy.wait_recv()
    block_ref[...] = (
        hidden_ref[...]
        + (own_mix + mix_part[1].astype(F32))
        + dot(share, bias_rows.astype(F32), FIRST, HIGHEST)
    ).astype(BF16)
    for chain in moe_chains:
        chain.advance()

    def attend_back(i):
        for h in range(HEADS):
            q, k, v, p = q_all[i, h], k_all[i, h], v_all[i, h], probs[i, h]
            gc = dot(ghs[i], w_out_ref[h * HD : (h + 1) * HD], LAST).astype(BF16)
            gp = dot(gc, v, LAST)
            row_dot = jnp.sum(gp * p, axis=-1, keepdims=True)
            graw = (p * (gp - row_dot) * (1.0 / math.sqrt(HD))).astype(BF16)
            at = h * 3 * HD
            gproj[i, :, at : at + HD] = dot(graw, k).astype(BF16)
            gproj[i, :, at + HD : at + 2 * HD] = dot(graw, q, FIRST).astype(BF16)
            gproj[i, :, at + 2 * HD : at + 3 * HD] = dot(p.astype(BF16), gc, FIRST).astype(BF16)

    attend_back(0)
    gh_copy.wait_recv()
    attend_back(1)
    gnorm_part[0] = dot(gproj[1], w_qkv_ref[...], LAST).astype(BF16)
    gnorm_copy = exchange(8, gnorm_part.at[0], gnorm_part.at[1])

    both = gproj[...].reshape(2 * ROWS, QKV)
    at = MOE_TILES
    store_tiles(held, at, dot(normed[...].reshape(2 * ROWS, D), both, FIRST))
    at += QKV_TILES
    gh_both = ghs[...].reshape(2 * ROWS, D)
    for h in range(HEADS):
        grad = dot(ctx[h].reshape(2 * ROWS, HD), gh_both, FIRST)
        for j in range(D // LANES):
            tiles = grad[:, j * LANES : (j + 1) * LANES].astype(BF16)
            spot = at + j * (OUT_TILES // 3) + h * (HD // TILE_ROWS)
            held[spot : spot + HD // TILE_ROWS] = tiles.reshape(HD // TILE_ROWS, TILE_ROWS, LANES)
    at += OUT_TILES
    held[at:TILES] = jnp.zeros((TILES - at, TILE_ROWS, LANES), BF16)
    for chain in attn_chains:
        chain.send()
    bias = column_sum(both.astype(F32))
    small_held[0, 22:23] = bias[:, :D]
    small_held[0, 23:24, 0 : QKV - D] = bias[:, D:]
    for chain in moe_chains:
        chain.advance()

    own_gnorm = dot(gproj[0], w_qkv_ref[...], LAST).astype(BF16).astype(F32)
    gnorm_copy.wait_recv()
    gnorm = own_gnorm + gnorm_part[1].astype(F32)
    xhat = attn_xhat[...]
    small_held[0, 0:1] = column_sum(gnorm * xhat)
    small_held[0, 1:2] = column_sum(gnorm)
    small_copy = small_step(0)
    grad_tok_ref[...] = (grad_hidden + norm_back(gnorm, xhat, attn_r, attn_gain)).astype(BF16)

    for k in range(STEPS + HALVINGS):
        for chain in attn_chains:
            chain.advance()
        for chain in moe_chains:
            chain.advance()
        if k < len(SMALL_ORDER):
            small_copy.wait_recv()
            if k == 0:
                small_held[1, :SHARED_ROWS] = (
                    small_held[0, :SHARED_ROWS] + small_landing[0, :SHARED_ROWS]
                )
                small_held[1, SHARED_ROWS:] = small_held[0, SHARED_ROWS:]
            elif k < len(SMALL_ORDER) - 1:
                small_held[k + 1] = small_held[k] + small_landing[k]
            else:
                small_out[...] = small_held[k] + small_landing[k]
            if k < len(SMALL_ORDER) - 1:
                small_copy = small_step(k + 1)
    for copy in unsent:
        copy.wait_send()


def run_block(*args):
    def bf(*shape):
        return pltpu.VMEM(shape, BF16)

    def fl(*shape):
        return pltpu.VMEM(shape, F32)

    dma = pltpu.SemaphoreType.DMA
    count = len(CHAINS)
    slots = 2 * CAP
    return pl.pallas_call(
        block_kernel,
        out_shape=(
            jax.ShapeDtypeStruct((ROWS, D), BF16),
            jax.ShapeDtypeStruct((ROWS, D), BF16),
            jax.ShapeDtypeStruct((TILES, TILE_ROWS, LANES), BF16),
            jax.ShapeDtypeStruct((SMALL_ROWS, D), F32),
        ),
        in_specs=[pl.BlockSpec(memory_space=pltpu.VMEM)] * len(args),
        out_specs=[pl.BlockSpec(memory_space=pltpu.VMEM)] * 4,
        scratch_shapes=[
            bf(TILES, TILE_ROWS, LANES),
            bf(LANDING, TILE_ROWS, LANES),
            fl(STEPS + 1, SMALL_ROWS, D),
            fl(STEPS + 1, SMALL_ROWS, D),
            bf(2, ROWS, D),
            bf(2, ROWS, D),
            bf(2, ROWS, D),
            bf(2, ROWS, D),
            bf(2, ROWS, D),
            bf(2, ROWS, D),
            bf(2, ROWS, D),
            fl(2, 8, ROWS),
            bf(2, ROWS, D),
            bf(2, HEADS, ROWS, HD),
            bf(2, HEADS, ROWS, HD),
            bf(2, HEADS, ROWS, HD),
            fl(2, HEADS, ROWS, ROWS),
            bf(HEADS, 2, ROWS, HD),
            bf(2, ROWS, QKV),
            bf(EXPERTS, slots, D),
            bf(EXPERTS, slots, D),
            bf(EXPERTS, slots, FF),
            bf(EXPERTS, slots, FF),
            bf(EXPERTS, slots, D),
            bf(EXPERTS, slots, D),
            bf(EXPERTS, slots, D),
            fl(ROWS, D),
            fl(ROWS, D),
            fl(ROWS, D),
            dma((9,)),
            dma((9,)),
            dma((count, STEPS)),
            dma((count, STEPS)),
            dma((count, HALVINGS)),
            dma((count, HALVINGS)),
            dma((STEPS + 1,)),
            dma((STEPS + 1,)),
        ],
        compiler_params=pltpu.CompilerParams(
            collective_id=0, has_side_effects=True, vmem_limit_bytes=56 * 1024 * 1024
        ),
    )(*args)


def unpack_kernel(sum_ref, w_qkv_ref, w_out_ref, w_in_ref, w_exp_ref):
    def spread(at, rows, out, lanes):
        per = rows // TILE_ROWS
        for j in range(-(-lanes // LANES)):
            width = min(LANES, lanes - j * LANES)
            part = sum_ref[at + j * per : at + (j + 1) * per].reshape(rows, LANES)
            out[:, j * LANES : j * LANES + width] = part[:, :width].astype(F32)

    for e in range(EXPERTS):
        at = e * (IN_TILES + EXP_TILES)
        spread(at, D, w_in_ref.at[e], FF)
        spread(at + IN_TILES, FF, w_exp_ref.at[e], D)
    spread(MOE_TILES, D, w_qkv_ref, QKV)
    spread(MOE_TILES + QKV_TILES, HEADS * HD, w_out_ref, D)


def unpack(sums):
    return pl.pallas_call(
        unpack_kernel,
        out_shape=(
            jax.ShapeDtypeStruct((D, QKV), F32),
            jax.ShapeDtypeStruct((HEADS * HD, D), F32),
            jax.ShapeDtypeStruct((EXPERTS, D, FF), F32),
            jax.ShapeDtypeStruct((EXPERTS, FF, D), F32),
        ),
        in_specs=[pl.BlockSpec(memory_space=pltpu.VMEM)],
        out_specs=[pl.BlockSpec(memory_space=pltpu.VMEM)] * 4,
        compiler_params=pltpu.CompilerParams(vmem_limit_bytes=32 * 1024 * 1024),
    )(sums)


def on_device(
    tokens,
    attn_gain,
    attn_shift,
    w_qkv,
    qv_bias,
    w_out,
    out_bias,
    moe_gain,
    moe_shift,
    router,
    w_in,
    in_bias,
    w_exp,
    exp_bias,
    routes,
    cotangent,
):
    pad = ROWS - SEQ
    tok = jnp.pad(tokens[0], ((0, pad), (0, 0)))
    cot = jnp.pad(cotangent[0], ((0, pad), (0, 0)))
    zero = jnp.zeros((3, D), F32)
    vec = jnp.concatenate(
        [
            jnp.stack([attn_gain, attn_shift, moe_gain, moe_shift, out_bias.astype(F32)]),
            zero,
            router.astype(F32).T,
            jnp.zeros((5, D), F32),
        ]
    )
    qkv_bias = (
        jnp.pad(qv_bias.astype(F32).reshape(HEADS, 2, HD), ((0, 0), (0, 1), (0, 0)))[
            :, jnp.array([0, 2, 1])
        ]
    ).reshape(1, QKV)
    routes = jnp.pad(routes, ((0, 0), (0, pad), (0, 0)), constant_values=-1)
    block, grad_tok, sums, small = run_block(
        tok,
        cot,
        vec,
        w_qkv.reshape(D, QKV),
        qkv_bias,
        w_out.reshape(HEADS * HD, D),
        w_in,
        in_bias,
        w_exp,
        exp_bias,
        routes,
        jnp.transpose(routes, (0, 2, 1)),
    )
    grad_w_qkv, grad_w_out, grad_w_in, grad_w_exp = unpack(sums)
    flat_bias = small[22:24].reshape(-1)[:QKV].reshape(HEADS, 3, HD)
    return (
        block[None, :SEQ],
        grad_tok[None, :SEQ],
        small[0],
        small[1],
        grad_w_qkv.reshape(D, HEADS, 3 * HD),
        jnp.concatenate([flat_bias[:, 0], flat_bias[:, 2]], axis=-1),
        grad_w_out.reshape(HEADS, HD, D),
        small[2],
        small[3],
        small[4],
        small[5:8].T,
        grad_w_in,
        small[16:22].reshape(EXPERTS, FF),
        grad_w_exp,
        small[8:11],
    )


def solution(mesh):
    placed = (
        P(("dp", "tensor"), None, None),
        P(),
        P(),
        P(None, "tensor", None),
        P("tensor", None),
        P("tensor", None, None),
        P(),
        P(),
        P(),
        P(),
        P(None, None, "tensor"),
        P(None, "tensor"),
        P(None, "tensor", None),
        P(),
        P("dp", None, None),
        P(("dp", "tensor"), None, None),
    )
    return jax.shard_map(
        on_device,
        mesh=mesh,
        in_specs=placed,
        out_specs=(
            P(("dp", "tensor"), None, None),
            P(("dp", "tensor"), None, None),
            P(),
            P(),
            P(None, "tensor", None),
            P("tensor", None),
            P("tensor", None, None),
            P(),
            P(),
            P(),
            P(),
            P(None, None, "tensor"),
            P(None, "tensor"),
            P(None, "tensor", None),
            P(),
        ),
        check_vma=False,
    )
```

```python
import functools
import math

import jax
import jax.numpy as jnp
from jax import lax
from jax.experimental import pallas as pl
from jax.experimental.pallas import tpu as pltpu
from jax.sharding import PartitionSpec as P

MESH = pl.DeviceIdType.MESH
RING = 4
D, SEQ, HEADS, HD, FF, EXPERTS, CAP = 384, 197, 3, 64, 768, 3, 128
ROWS = 208
QKV = 3 * HEADS * HD
TILE_ROWS = 16
LANES = 128
IN_TILES = (D // TILE_ROWS) * (FF // LANES)
EXP_TILES = (FF // TILE_ROWS) * (D // LANES)
MOE_TILES = EXPERTS * (IN_TILES + EXP_TILES)
QKV_TILES = (QKV // TILE_ROWS) * (D // LANES)
OUT_TILES = (HEADS * HD // TILE_ROWS) * (D // LANES)
MOE_CHAINS = (224, 224, 224, 192)
ATTN_CHAINS = (64, 32, 32, 32)
CHAINS = MOE_CHAINS + ATTN_CHAINS
TILES = sum(CHAINS)
ORDERS = (
    ("core", "xa", "xb", "ya", "yb", "za", "zb"),
    ("core", "xb", "xa", "yb", "ya", "zb", "za"),
    ("core", "ya", "yb", "xa", "xb", "za", "zb"),
    ("core", "yb", "ya", "xb", "xa", "zb", "za"),
)
HALVINGS = 5
STEPS = 7
LANDING = sum(c // 2 + c // 4 + c // 8 + c // 16 + 3 * (c // 32) for c in CHAINS)
SMALL_ORDER = ("pair", "core", "xa", "xb", "ya", "yb", "za", "zb")
SMALL_ROWS = 24
SHARED_ROWS = 16
F32 = jnp.float32
BF16 = jnp.bfloat16
HIGHEST = lax.Precision.HIGHEST


def partners():
    me = lax.axis_index("dp")
    core = me % 2
    x = (me // 2) % RING
    z = (me // (2 * RING)) % RING
    y = me // (2 * RING * RING)

    def dp_index(y, z, x, core):
        return ((y * RING + z) * RING + x) * 2 + core

    def swap(v):
        return v + 1 - 2 * (v % 2)

    return {
        "core": ({"dp": dp_index(y, z, x, 1 - core)}, core),
        "xa": ({"dp": dp_index(y, z, swap(x), core)}, (x + 1) // 2 % 2),
        "xb": ({"dp": dp_index(y, z, RING - 1 - x, core)}, x // 2),
        "ya": ({"dp": dp_index(swap(y), z, x, core)}, (y + 1) // 2 % 2),
        "yb": ({"dp": dp_index(RING - 1 - y, z, x, core)}, y // 2),
        "za": ({"dp": dp_index(y, swap(z), x, core)}, (z + 1) // 2 % 2),
        "zb": ({"dp": dp_index(y, RING - 1 - z, x, core)}, z // 2),
        "pair": ({"tensor": 1 - lax.axis_index("tensor")}, lax.axis_index("tensor")),
    }


def dot(a, b, dims=((1,), (0,)), precision=None):
    return lax.dot_general(
        a, b, (dims, ((), ())), precision=precision, preferred_element_type=F32
    )


LAST = ((1,), (1,))
FIRST = ((0,), (0,))


def normalize(v):
    centre = v - jnp.mean(v, axis=-1, keepdims=True)
    r = lax.rsqrt(jnp.mean(centre * centre, axis=-1, keepdims=True) + 1e-06)
    return centre * r, r


def norm_back(grad, xhat, r, gain):
    g = grad * gain
    return r * (
        g
        - jnp.mean(g, axis=-1, keepdims=True)
        - xhat * jnp.mean(g * xhat, axis=-1, keepdims=True)
    )


def column_sum(v):
    return jnp.sum(v, axis=0, keepdims=True)


def add_tiles(ref, at, landing, landing_at, count):
    step = max(k for k in range(1, 17) if count % k == 0)

    @pl.loop(0, count // step)
    def _(i):
        rows = pl.ds(at + i * step, step)
        total = ref[rows].astype(F32) + landing[pl.ds(landing_at + i * step, step)].astype(F32)
        ref[rows] = total.astype(ref.dtype)


def store_tiles(ref, at, value):
    rows, lanes = value.shape
    per = rows // TILE_ROWS
    for j in range(-(-lanes // LANES)):
        part = value[:, j * LANES : min((j + 1) * LANES, lanes)]
        if part.shape[1] < LANES:
            part = jnp.concatenate(
                [part, jnp.zeros((rows, LANES - part.shape[1]), part.dtype)], axis=1
            )
        ref[at + j * per : at + (j + 1) * per] = part.astype(BF16).reshape(per, TILE_ROWS, LANES)


def block_kernel(
    tok_ref,
    attn_gain_ref,
    attn_shift_ref,
    w_qkv_ref,
    qv_bias_ref,
    w_out_ref,
    out_bias_ref,
    moe_gain_ref,
    moe_shift_ref,
    router_ref,
    w_in_ref,
    in_bias_ref,
    w_exp_ref,
    exp_bias_ref,
    route_ref,
    cot_ref,
    block_ref,
    grad_tok_ref,
    sum_ref,
    small_out,
    held,
    landing,
    small_held,
    small_landing,
    normed,
    cots,
    moes,
    ghs,
    att_part,
    mix_part,
    gmoe_part,
    gate_part,
    gnorm_part,
    q_all,
    k_all,
    v_all,
    probs,
    ctx,
    gproj,
    slot_in,
    slot_cot,
    act_all,
    gpre_all,
    scaled_all,
    gslot_all,
    gback_all,
    attn_xhat,
    moe_xhat,
    hidden_ref,
    padded,
    route_pad,
    pair_send,
    pair_recv,
    send_sem,
    recv_sem,
    back_send,
    back_recv,
    small_send,
    small_recv,
):
    who = partners()
    barrier = pltpu.get_barrier_semaphore()
    for device, _ in who.values():
        pl.semaphore_signal(barrier, inc=1, device_id=device, device_id_type=MESH)

    def remote(src, dst, send, recv, name):
        copy = pltpu.make_async_remote_copy(
            src_ref=src,
            dst_ref=dst,
            send_sem=send,
            recv_sem=recv,
            device_id=who[name][0],
            device_id_type=MESH,
        )
        copy.start()
        return copy

    unsent = []

    def exchange(i, src, dst):
        copy = remote(src, dst, pair_send.at[i], pair_recv.at[i], "pair")
        unsent.append(copy)
        return copy

    spots = [0]

    class Chain:
        def __init__(self, c):
            self.c, self.order = c, ORDERS[c % len(ORDERS)]
            self.base, self.size, self.k = sum(CHAINS[:c]), CHAINS[c], 0

        def send(self):
            c, k = self.c, self.k
            name = self.order[k]
            give = self.base
            if k < HALVINGS:
                self.size //= 2
                bit = who[name][1]
                give = self.base + (1 - bit) * self.size
                self.base = self.base + bit * self.size
            self.spot = spots[0]
            spots[0] += self.size
            self.copy = remote(
                held.at[pl.ds(give, self.size)],
                landing.at[pl.ds(self.spot, self.size)],
                send_sem.at[c, k],
                recv_sem.at[c, k],
                name,
            )

        def send_back(self, k):
            self.back = k
            part = sum_ref.at[pl.ds(self.base, self.size)]
            self.copy = remote(
                part, part, back_send.at[self.c, k], back_recv.at[self.c, k], self.order[k]
            )
            unsent.append(self.copy)

        def advance(self):
            if self.k < STEPS:
                self.copy.wait_recv()
                if self.k < HALVINGS:
                    unsent.append(self.copy)
                else:
                    self.copy.wait_send()
                add_tiles(held, self.base, landing, self.spot, self.size)
                self.k += 1
                if self.k < STEPS:
                    self.send()
                    return
                step = max(k for k in range(1, 17) if self.size % k == 0)

                @pl.loop(0, self.size // step)
                def _(i):
                    rows = pl.ds(self.base + i * step, step)
                    sum_ref[rows] = held[rows]

                self.send_back(HALVINGS - 1)
            elif self.back >= 0:
                self.copy.wait_recv()
                self.base = self.base - who[self.order[self.back]][1] * self.size
                self.size = self.size * 2
                if self.back:
                    self.send_back(self.back - 1)
                else:
                    self.back = -1

    def small_step(k):
        rows = SHARED_ROWS if k == 0 else SMALL_ROWS
        copy = remote(
            small_held.at[k, pl.ds(0, rows)],
            small_landing.at[k, pl.ds(0, rows)],
            small_send.at[k],
            small_recv.at[k],
            SMALL_ORDER[k],
        )
        unsent.append(copy)
        return copy

    def row_of(ref):
        return ref[...].astype(F32).reshape(1, D)

    attn_gain, attn_shift = row_of(attn_gain_ref), row_of(attn_shift_ref)
    moe_gain, moe_shift = row_of(moe_gain_ref), row_of(moe_shift_ref)
    out_bias = row_of(out_bias_ref)

    padded[:, SEQ - 5 :] = jnp.zeros((2, ROWS - SEQ + 5, D), F32)
    padded[0, :SEQ] = tok_ref[0].astype(F32)
    padded[1, :SEQ] = cot_ref[0].astype(F32)
    tok = padded[0]
    xhat, attn_r = normalize(tok)
    attn_xhat[...] = xhat
    normed[0] = (xhat * attn_gain + attn_shift).astype(BF16)
    cots[0] = padded[1].astype(BF16)
    pl.semaphore_wait(barrier, len(who))
    normed_copy = exchange(0, normed.at[0], normed.at[1])
    cot_copy = exchange(1, cots.at[0], cots.at[1])

    key_mask = lax.broadcasted_iota(jnp.int32, (ROWS, ROWS), 1) < SEQ

    def project(i):
        proj = dot(normed[i], w_qkv_ref[...], LAST)
        bias = qv_bias_ref[...].astype(F32)
        for h in range(HEADS):
            at = h * 3 * HD
            q_all[i, h] = (proj[:, at : at + HD] + bias[h : h + 1, :HD]).astype(BF16)
            k_all[i, h] = proj[:, at + HD : at + 2 * HD].astype(BF16)
            v_all[i, h] = (proj[:, at + 2 * HD : at + 3 * HD] + bias[h : h + 1, HD:]).astype(BF16)

    def attend(i):
        total = jnp.zeros((ROWS, D), F32)
        for h in range(HEADS):
            scores = dot(q_all[i, h], k_all[i, h], LAST) * (1.0 / math.sqrt(HD))
            scores = jnp.where(key_mask, scores, -1e30)
            weights = jnp.exp(scores - jnp.max(scores, axis=-1, keepdims=True))
            p = weights / jnp.sum(weights, axis=-1, keepdims=True)
            probs[i, h] = p
            c = dot(p.astype(BF16), v_all[i, h]).astype(BF16)
            ctx[h, i] = c
            total += dot(c, w_out_ref[h * HD : (h + 1) * HD])
        return total

    tensor = lax.axis_index("tensor")
    before = (
        lax.broadcasted_iota(jnp.int32, (ROWS, ROWS), 1)
        < lax.broadcasted_iota(jnp.int32, (ROWS, ROWS), 0)
    ).astype(BF16)
    lane = lax.broadcasted_iota(jnp.int32, (ROWS, LANES), 1).astype(F32)
    sub = lax.broadcasted_iota(jnp.int32, (8, ROWS), 0).astype(F32)
    slot_lane = lax.broadcasted_iota(jnp.int32, (ROWS, CAP), 1).astype(F32)
    slot_sub = lax.broadcasted_iota(jnp.int32, (CAP, ROWS), 0).astype(F32)
    same = (
        lax.broadcasted_iota(jnp.int32, (ROWS, ROWS), 0)
        == lax.broadcasted_iota(jnp.int32, (ROWS, ROWS), 1)
    ).astype(BF16)
    pos_col, pos_row = [], []
    for i in range(2):
        route_pad[i] = jnp.full((2, ROWS), -1.0, F32)
        first, second = route_ref[0].astype(F32), route_ref[1].astype(F32)
        route_pad[i, :, :SEQ] = jnp.where(tensor == i, first, second)
        row = route_pad[i]
        col = dot(same, row.astype(BF16), LAST)
        a0, a1 = col[:, 0:1] == lane, col[:, 1:2] == lane
        f0, f1 = a0.astype(F32), a1.astype(F32)
        c0 = dot(before, f0.astype(BF16))
        c1 = dot(before, f1.astype(BF16)) + column_sum(f0)
        pos_col.append(jnp.where(a0, c0, jnp.where(a1, c1, -1.0)))
        a0, a1 = row[0:1] == sub, row[1:2] == sub
        f0, f1 = a0.astype(F32), a1.astype(F32)
        c0 = dot(f0.astype(BF16), before, LAST)
        c1 = dot(f1.astype(BF16), before, LAST) + jnp.sum(f0, axis=1, keepdims=True)
        pos_row.append(jnp.where(a0, c0, jnp.where(a1, c1, -1.0)))
    kept_row = [((p >= 0.0) & (p < CAP)).astype(F32) for p in pos_row]

    def dispatch(i, e):
        return (pos_col[i][:, e : e + 1] == slot_lane).astype(F32)

    def dispatch_t(i, e):
        return (pos_row[i][e : e + 1] == slot_sub).astype(F32)

    project(0)
    normed_copy.wait_recv()
    project(1)
    att_part[0] = attend(1).astype(BF16)
    att_copy = exchange(2, att_part.at[0], att_part.at[1])
    own_part = attend(0)
    cot_copy.wait_recv()
    for i in range(2):
        for e in range(EXPERTS):
            slot_cot[e, i * CAP : (i + 1) * CAP] = dot(
                dispatch_t(i, e).astype(BF16), cots[i]
            ).astype(BF16)
    att_copy.wait_recv()
    hidden = tok + (own_part.astype(BF16).astype(F32) + att_part[1].astype(F32)) + out_bias
    hidden_ref[...] = hidden
    xhat, moe_r = normalize(hidden)
    moe_xhat[...] = xhat
    moes[0] = (xhat * moe_gain + moe_shift).astype(BF16)
    moe_copy = exchange(3, moes.at[0], moes.at[1])

    router_rows = jnp.concatenate(
        [router_ref[...].astype(F32), jnp.zeros((8 - EXPERTS, D), F32)], axis=0
    )
    router = router_rows.astype(BF16)
    expert_rows = sub < EXPERTS

    def gate(i):
        logits = jnp.where(expert_rows, dot(router, moes[i], LAST), -1e30)
        weights = jnp.exp(logits - jnp.max(logits, axis=0, keepdims=True))
        return weights / column_sum(weights)

    gates, slot_weight = [None, None], [[None] * EXPERTS, [None] * EXPERTS]

    def fill_slots(i):
        gates[i] = gate(i)
        for e in range(EXPERTS):
            pick = dispatch_t(i, e)
            slot_in[e, i * CAP : (i + 1) * CAP] = dot(pick.astype(BF16), moes[i]).astype(BF16)
            slot_weight[i][e] = jnp.sum(pick * gates[i][e : e + 1], axis=1, keepdims=True)

    fill_slots(0)
    moe_copy.wait_recv()
    fill_slots(1)

    gate_rows = [[None] * EXPERTS, [None] * EXPERTS]
    small_held[0] = jnp.zeros((SMALL_ROWS, D), F32)
    for e in range(EXPERTS):
        weight = jnp.concatenate([slot_weight[0][e], slot_weight[1][e]], axis=0)
        pre = dot(slot_in[e], w_in_ref[e]) + in_bias_ref[e : e + 1].astype(F32)
        half = 0.5 * (1.0 + lax.erf(pre * (1.0 / math.sqrt(2.0))))
        act_all[e] = (pre * half).astype(BF16)
        slope = half + pre * jnp.exp(-0.5 * pre * pre) * (1.0 / math.sqrt(2.0 * math.pi))
        g = slot_cot[e].astype(F32)
        gs = (g * weight).astype(BF16)
        gslot_all[e] = gs
        gpre = (dot(gs, w_exp_ref[e], LAST) * slope).astype(BF16)
        gpre_all[e] = gpre
        gback_all[e] = dot(gpre, w_in_ref[e], LAST).astype(BF16)
        slot_out = dot(act_all[e], w_exp_ref[e])
        scaled_all[e] = (slot_out * weight).astype(BF16)
        slot_gate = jnp.sum(slot_out * g, axis=1, keepdims=True)
        for i in range(2):
            gate_rows[i][e] = column_sum(
                dispatch_t(i, e) * slot_gate[i * CAP : (i + 1) * CAP]
            )

    def combine(i, ref):
        total = jnp.zeros((ROWS, D), F32)
        for e in range(EXPERTS):
            total += dot(dispatch(i, e).astype(BF16), ref[e, i * CAP : (i + 1) * CAP])
        return total

    def gate_grads(i):
        return jnp.concatenate(gate_rows[i] + [jnp.zeros((8 - EXPERTS, ROWS), F32)], axis=0)

    gmoe_part[0] = combine(1, gback_all).astype(BF16)
    gmoe_copy = exchange(4, gmoe_part.at[0], gmoe_part.at[1])
    gate_part[0] = gate_grads(1)
    gate_copy = exchange(5, gate_part.at[0], gate_part.at[1])
    mix_part[0] = combine(1, scaled_all).astype(BF16)
    mix_copy = exchange(6, mix_part.at[0], mix_part.at[1])

    for e in range(EXPERTS):
        at = e * (IN_TILES + EXP_TILES)
        store_tiles(held, at, dot(slot_in[e], gpre_all[e], FIRST))
        store_tiles(held, at + IN_TILES, dot(act_all[e], gslot_all[e], FIRST))
        bias = column_sum(gpre_all[e].astype(F32))
        for j in range(FF // D):
            small_held[0, 16 + 2 * e + j : 17 + 2 * e + j] = bias[:, j * D : (j + 1) * D]
    chains = [Chain(c) for c in range(len(CHAINS))]
    moe_chains = chains[: len(MOE_CHAINS)]
    attn_chains = chains[len(MOE_CHAINS) :]
    for chain in moe_chains:
        chain.send()

    own_gmoe = combine(0, gback_all).astype(BF16).astype(F32)
    own_mix = combine(0, scaled_all).astype(BF16).astype(F32)
    own_gate = gate_grads(0)
    cot = padded[1]
    bias_rows = jnp.concatenate(
        [exp_bias_ref[...], jnp.zeros((8 - EXPERTS, D), BF16)], axis=0
    )
    share = gates[0] * kept_row[0]
    bias_grad = dot(bias_rows, cots[0], LAST)
    gate_copy.wait_recv()
    grad_gates = (own_gate + gate_part[1] + bias_grad) * kept_row[0]
    grad_logits = gates[0] * (grad_gates - column_sum(gates[0] * grad_gates))
    small_held[0, 5:8] = dot(grad_logits, moes[0].astype(F32), precision=HIGHEST)[:EXPERTS]
    small_held[0, 8:11] = dot(share, cot, precision=HIGHEST)[:EXPERTS]
    router_back = dot(grad_logits, router_rows, FIRST, HIGHEST)
    gmoe_copy.wait_recv()
    gmoe = own_gmoe + gmoe_part[1].astype(F32) + router_back
    grad_hidden = cot + norm_back(gmoe, moe_xhat[...], moe_r, moe_gain)
    ghs[0] = grad_hidden.astype(BF16)
    gh_copy = exchange(7, ghs.at[0], ghs.at[1])
    small_held[0, 2:3] = column_sum(grad_hidden)
    small_held[0, 3:4] = column_sum(gmoe * moe_xhat[...])
    small_held[0, 4:5] = column_sum(gmoe)
    mix_copy.wait_recv()
    block_ref[...] = (
        hidden_ref[...]
        + (own_mix + mix_part[1].astype(F32))
        + dot(share, bias_rows.astype(F32), FIRST, HIGHEST)
    ).astype(BF16)
    for chain in moe_chains:
        chain.advance()

    def attend_back(i):
        for h in range(HEADS):
            q, k, v, p = q_all[i, h], k_all[i, h], v_all[i, h], probs[i, h]
            gc = dot(ghs[i], w_out_ref[h * HD : (h + 1) * HD], LAST).astype(BF16)
            gp = dot(gc, v, LAST)
            row_dot = jnp.sum(gp * p, axis=-1, keepdims=True)
            graw = (p * (gp - row_dot) * (1.0 / math.sqrt(HD))).astype(BF16)
            at = h * 3 * HD
            gproj[i, :, at : at + HD] = dot(graw, k).astype(BF16)
            gproj[i, :, at + HD : at + 2 * HD] = dot(graw, q, FIRST).astype(BF16)
            gproj[i, :, at + 2 * HD : at + 3 * HD] = dot(p.astype(BF16), gc, FIRST).astype(BF16)

    attend_back(0)
    gh_copy.wait_recv()
    attend_back(1)
    gnorm_part[0] = dot(gproj[1], w_qkv_ref[...]).astype(BF16)
    gnorm_copy = exchange(8, gnorm_part.at[0], gnorm_part.at[1])

    both = gproj[...].reshape(2 * ROWS, QKV)
    at = MOE_TILES
    store_tiles(held, at, dot(both, normed[...].reshape(2 * ROWS, D), FIRST))
    at += QKV_TILES
    gh_both = ghs[...].reshape(2 * ROWS, D)
    for h in range(HEADS):
        grad = dot(ctx[h].reshape(2 * ROWS, HD), gh_both, FIRST)
        for j in range(D // LANES):
            tiles = grad[:, j * LANES : (j + 1) * LANES].astype(BF16)
            spot = at + j * (OUT_TILES // 3) + h * (HD // TILE_ROWS)
            held[spot : spot + HD // TILE_ROWS] = tiles.reshape(HD // TILE_ROWS, TILE_ROWS, LANES)
    at += OUT_TILES
    held[at:TILES] = jnp.zeros((TILES - at, TILE_ROWS, LANES), BF16)
    for chain in attn_chains:
        chain.send()
    bias = column_sum(both.astype(F32))
    small_held[0, 22:23] = bias[:, :D]
    small_held[0, 23:24, 0 : QKV - D] = bias[:, D:]
    for chain in moe_chains:
        chain.advance()

    own_gnorm = dot(gproj[0], w_qkv_ref[...]).astype(BF16).astype(F32)
    gnorm_copy.wait_recv()
    gnorm = own_gnorm + gnorm_part[1].astype(F32)
    xhat = attn_xhat[...]
    small_held[0, 0:1] = column_sum(gnorm * xhat)
    small_held[0, 1:2] = column_sum(gnorm)
    small_copy = small_step(0)
    grad_tok_ref[...] = (grad_hidden + norm_back(gnorm, xhat, attn_r, attn_gain)).astype(BF16)

    for k in range(STEPS + HALVINGS):
        for chain in attn_chains:
            chain.advance()
        for chain in moe_chains:
            chain.advance()
        if k < len(SMALL_ORDER):
            small_copy.wait_recv()
            if k == 0:
                small_held[1, :SHARED_ROWS] = (
                    small_held[0, :SHARED_ROWS] + small_landing[0, :SHARED_ROWS]
                )
                small_held[1, SHARED_ROWS:] = small_held[0, SHARED_ROWS:]
            elif k < len(SMALL_ORDER) - 1:
                small_held[k + 1] = small_held[k] + small_landing[k]
            else:
                small_out[...] = small_held[k] + small_landing[k]
            if k < len(SMALL_ORDER) - 1:
                small_copy = small_step(k + 1)
    for copy in unsent:
        copy.wait_send()


def run_block(*args):
    def bf(*shape):
        return pltpu.VMEM(shape, BF16)

    def fl(*shape):
        return pltpu.VMEM(shape, F32)

    dma = pltpu.SemaphoreType.DMA
    count = len(CHAINS)
    slots = 2 * CAP
    return pl.pallas_call(
        block_kernel,
        out_shape=(
            jax.ShapeDtypeStruct((ROWS, D), BF16),
            jax.ShapeDtypeStruct((ROWS, D), BF16),
            jax.ShapeDtypeStruct((TILES, TILE_ROWS, LANES), BF16),
            jax.ShapeDtypeStruct((SMALL_ROWS, D), F32),
        ),
        in_specs=[pl.BlockSpec(memory_space=pltpu.VMEM)] * len(args),
        out_specs=[pl.BlockSpec(memory_space=pltpu.VMEM)] * 4,
        scratch_shapes=[
            bf(TILES, TILE_ROWS, LANES),
            bf(LANDING, TILE_ROWS, LANES),
            fl(STEPS + 1, SMALL_ROWS, D),
            fl(STEPS + 1, SMALL_ROWS, D),
            bf(2, ROWS, D),
            bf(2, ROWS, D),
            bf(2, ROWS, D),
            bf(2, ROWS, D),
            bf(2, ROWS, D),
            bf(2, ROWS, D),
            bf(2, ROWS, D),
            fl(2, 8, ROWS),
            bf(2, ROWS, D),
            bf(2, HEADS, ROWS, HD),
            bf(2, HEADS, ROWS, HD),
            bf(2, HEADS, ROWS, HD),
            fl(2, HEADS, ROWS, ROWS),
            bf(HEADS, 2, ROWS, HD),
            bf(2, ROWS, QKV),
            bf(EXPERTS, slots, D),
            bf(EXPERTS, slots, D),
            bf(EXPERTS, slots, FF),
            bf(EXPERTS, slots, FF),
            bf(EXPERTS, slots, D),
            bf(EXPERTS, slots, D),
            bf(EXPERTS, slots, D),
            fl(ROWS, D),
            fl(ROWS, D),
            fl(ROWS, D),
            fl(2, ROWS, D),
            fl(2, 2, ROWS),
            dma((9,)),
            dma((9,)),
            dma((count, STEPS)),
            dma((count, STEPS)),
            dma((count, HALVINGS)),
            dma((count, HALVINGS)),
            dma((STEPS + 1,)),
            dma((STEPS + 1,)),
        ],
        compiler_params=pltpu.CompilerParams(
            collective_id=0, has_side_effects=True, vmem_limit_bytes=56 * 1024 * 1024
        ),
    )(*args)


def unpack_kernel(
    block_ref,
    grad_tok_ref,
    sum_ref,
    small_ref,
    block_out,
    grad_tok_out,
    attn_gain,
    attn_shift,
    w_qkv_out,
    qv_bias,
    w_out_out,
    out_bias,
    moe_gain,
    moe_shift,
    router,
    w_in_out,
    in_bias,
    w_exp_out,
    exp_bias,
    sums,
    w_qkv,
    w_out,
    w_in,
    w_exp,
    in_sem,
    out_sem,
):
    pieces = []
    for e in range(EXPERTS):
        at = e * (IN_TILES + EXP_TILES)
        pieces.append((at, IN_TILES, D, FF, w_in.at[e], w_in_out.at[e]))
        pieces.append((at + IN_TILES, EXP_TILES, FF, D, w_exp.at[e], w_exp_out.at[e]))
    at = MOE_TILES
    pieces.append((at, QKV_TILES, QKV, D, w_qkv, w_qkv_out))
    pieces.append((at + QKV_TILES, OUT_TILES, HEADS * HD, D, w_out, w_out_out))
    arriving = []
    for i, (at, tiles, *_) in enumerate(pieces):
        rows = pl.ds(at, tiles)
        arriving.append(pltpu.make_async_copy(sum_ref.at[rows], sums.at[rows], in_sem.at[i]))
        arriving[-1].start()
    block_out[0] = block_ref[:SEQ]
    grad_tok_out[0] = grad_tok_ref[:SEQ]
    small = small_ref[...]
    for ref, row in zip((attn_gain, attn_shift, out_bias, moe_gain, moe_shift), range(5)):
        ref[...] = small[row]
    router[...] = small[5:8]
    exp_bias[...] = small[8:11]
    for e in range(EXPERTS):
        for j in range(FF // D):
            in_bias[e : e + 1, j * D : (j + 1) * D] = small[16 + 2 * e + j : 17 + 2 * e + j]
    bias = jnp.concatenate([small[22:23], small[23:24]], axis=1)
    for h in range(HEADS):
        at = 3 * h * HD
        qv_bias[h : h + 1, :HD] = bias[:, at : at + HD]
        qv_bias[h : h + 1, HD:] = bias[:, at + 2 * HD : at + 3 * HD]
    leaving = []
    for i, (at, tiles, rows, lanes, held, out) in enumerate(pieces):
        arriving[i].wait()
        per = rows // TILE_ROWS
        for j in range(-(-lanes // LANES)):
            width = min(LANES, lanes - j * LANES)
            part = sums[at + j * per : at + (j + 1) * per].reshape(rows, LANES)
            held[:, j * LANES : j * LANES + width] = part[:, :width].astype(F32)
        leaving.append(pltpu.make_async_copy(held, out, out_sem.at[i]))
        leaving[-1].start()
    for copy in leaving:
        copy.wait()


def unpack(*args):
    def out(shape, dtype=F32):
        return jax.ShapeDtypeStruct(shape, dtype)

    vmem = pl.BlockSpec(memory_space=pltpu.VMEM)
    anywhere = pl.BlockSpec(memory_space=pl.ANY)
    wide = (4, 6, 11, 13)
    shapes = (
        out((1, SEQ, D), BF16),
        out((1, SEQ, D), BF16),
        out((D,)),
        out((D,)),
        out((QKV, D)),
        out((HEADS, 2 * HD)),
        out((HEADS * HD, D)),
        out((D,)),
        out((D,)),
        out((D,)),
        out((EXPERTS, D)),
        out((EXPERTS, D, FF)),
        out((EXPERTS, FF)),
        out((EXPERTS, FF, D)),
        out((EXPERTS, D)),
    )
    return pl.pallas_call(
        unpack_kernel,
        out_shape=shapes,
        in_specs=[vmem, vmem, anywhere, vmem],
        out_specs=[anywhere if i in wide else vmem for i in range(len(shapes))],
        scratch_shapes=[
            pltpu.VMEM((TILES, TILE_ROWS, LANES), BF16),
            pltpu.VMEM((QKV, D), F32),
            pltpu.VMEM((HEADS * HD, D), F32),
            pltpu.VMEM((EXPERTS, D, FF), F32),
            pltpu.VMEM((EXPERTS, FF, D), F32),
            pltpu.SemaphoreType.DMA((8,)),
            pltpu.SemaphoreType.DMA((8,)),
        ],
        compiler_params=pltpu.CompilerParams(vmem_limit_bytes=40 * 1024 * 1024),
    )(*args)


def on_device(
    tokens,
    attn_gain,
    attn_shift,
    w_qkv,
    qv_bias,
    w_out,
    out_bias,
    moe_gain,
    moe_shift,
    router,
    w_in,
    in_bias,
    w_exp,
    exp_bias,
    routes,
    cotangent,
):
    outs = list(
        unpack(
            *run_block(
                tokens,
                attn_gain,
                attn_shift,
                jnp.transpose(w_qkv, (1, 2, 0)).reshape(QKV, D),
                qv_bias,
                w_out.reshape(HEADS * HD, D),
                out_bias,
                moe_gain,
                moe_shift,
                router.T,
                w_in,
                in_bias,
                w_exp,
                exp_bias,
                jnp.transpose(routes, (0, 2, 1)),
                cotangent,
            )
        )
    )
    outs[4] = jnp.transpose(outs[4].reshape(HEADS, 3 * HD, D), (2, 0, 1))
    outs[10] = outs[10].T
    outs[6] = outs[6].reshape(HEADS, HD, D)
    return tuple(outs)


def solution(mesh):
    placed = (
        P(("dp", "tensor"), None, None),
        P(),
        P(),
        P(None, "tensor", None),
        P("tensor", None),
        P("tensor", None, None),
        P(),
        P(),
        P(),
        P(),
        P(None, None, "tensor"),
        P(None, "tensor"),
        P(None, "tensor", None),
        P(),
        P("dp", None, None),
        P(("dp", "tensor"), None, None),
    )
    return jax.shard_map(
        on_device,
        mesh=mesh,
        in_specs=placed,
        out_specs=(
            P(("dp", "tensor"), None, None),
            P(("dp", "tensor"), None, None),
            P(),
            P(),
            P(None, "tensor", None),
            P("tensor", None),
            P("tensor", None, None),
            P(),
            P(),
            P(),
            P(),
            P(None, None, "tensor"),
            P(None, "tensor"),
            P(None, "tensor", None),
            P(),
        ),
        check_vma=False,
    )
```

```python
import functools
import math

import jax
import jax.numpy as jnp
from jax import lax
from jax.experimental import pallas as pl
from jax.experimental.pallas import tpu as pltpu
from jax.sharding import PartitionSpec as P

MESH = pl.DeviceIdType.MESH
RING = 4
D, SEQ, HEADS, HD, FF, EXPERTS, CAP = 384, 197, 3, 64, 768, 3, 128
ROWS = 208
QKV = 3 * HEADS * HD
TILE_ROWS = 16
LANES = 128
IN_TILES = (D // TILE_ROWS) * (FF // LANES)
EXP_TILES = (FF // TILE_ROWS) * (D // LANES)
MOE_TILES = EXPERTS * (IN_TILES + EXP_TILES)
QKV_TILES = (QKV // TILE_ROWS) * (D // LANES)
OUT_TILES = (HEADS * HD // TILE_ROWS) * (D // LANES)
BATCHES = ((128, 160),) * EXPERTS + ((64, 96),)
CHAIN_COUNT = 2 * len(BATCHES)
TILES = sum(sum(batch) for batch in BATCHES)
ORDERS = (("core", "x", "y", "z"), ("core", "y", "x", "z"))
GROUP = {"pair": 2, "core": 2, "x": RING, "y": RING, "z": RING}
PHASES = 4
LANDING = sum(c // 2 + 3 * (c // 8) + 7 * (c // 32) for batch in BATCHES for c in batch)
SMALL_ORDER = ("pair", "core", "x", "y", "z")
EARLY_ROWS, LATE_ROWS = 24, 16
SHARED_ROWS = (16, 8)
F32 = jnp.float32
BF16 = jnp.bfloat16
HIGHEST = lax.Precision.HIGHEST


def places():
    me = lax.axis_index("dp")
    tensor = lax.axis_index("tensor")
    at = {
        "pair": tensor,
        "core": me % 2,
        "x": (me // 2) % RING,
        "z": (me // (2 * RING)) % RING,
        "y": me // (2 * RING * RING),
    }

    def ahead(axis, distance):
        if axis == "pair":
            return {"tensor": 1 - tensor}
        to = dict(at)
        to[axis] = (at[axis] + distance) % GROUP[axis]
        return {"dp": ((to["y"] * RING + to["z"]) * RING + to["x"]) * 2 + to["core"]}

    return at, ahead


def dot(a, b, dims=((1,), (0,)), precision=None):
    return lax.dot_general(
        a, b, (dims, ((), ())), precision=precision, preferred_element_type=F32
    )


LAST = ((1,), (1,))
FIRST = ((0,), (0,))


def normalize(v):
    centre = v - jnp.mean(v, axis=-1, keepdims=True)
    r = lax.rsqrt(jnp.mean(centre * centre, axis=-1, keepdims=True) + 1e-06)
    return centre * r, r


def norm_back(grad, xhat, r, gain):
    g = grad * gain
    return r * (
        g
        - jnp.mean(g, axis=-1, keepdims=True)
        - xhat * jnp.mean(g * xhat, axis=-1, keepdims=True)
    )


def column_sum(v):
    return jnp.sum(v, axis=0, keepdims=True)


def add_tiles(out, at, count, parts):
    step = max(k for k in range(1, 17) if count % k == 0)

    @pl.loop(0, count // step)
    def _(i):
        total = None
        for ref, start in parts:
            piece = ref[pl.ds(start + i * step, step)].astype(F32)
            total = piece if total is None else total + piece
        out[pl.ds(at + i * step, step)] = total.astype(out.dtype)


def store_tiles(ref, at, value):
    rows, lanes = value.shape
    per = rows // TILE_ROWS
    for j in range(-(-lanes // LANES)):
        part = value[:, j * LANES : min((j + 1) * LANES, lanes)]
        if part.shape[1] < LANES:
            part = jnp.concatenate(
                [part, jnp.zeros((rows, LANES - part.shape[1]), part.dtype)], axis=1
            )
        ref[at + j * per : at + (j + 1) * per] = part.astype(BF16).reshape(per, TILE_ROWS, LANES)


def block_kernel(
    tok_ref,
    attn_gain_ref,
    attn_shift_ref,
    w_qkv_hbm,
    qv_bias_ref,
    w_out_hbm,
    out_bias_ref,
    moe_gain_ref,
    moe_shift_ref,
    router_ref,
    w_in_hbm,
    in_bias_ref,
    w_exp_hbm,
    exp_bias_ref,
    route_ref,
    cot_ref,
    block_ref,
    grad_tok_ref,
    sum_out,
    small_out,
    w_qkv_ref,
    w_out_ref,
    w_in_ref,
    w_exp_ref,
    held,
    landing,
    sum_ref,
    early_held,
    early_landing,
    late_held,
    late_landing,
    normed,
    cots,
    moes,
    ghs,
    att_part,
    mix_part,
    gmoe_part,
    gate_part,
    gnorm_part,
    q_all,
    k_all,
    v_all,
    probs,
    ctx,
    gproj,
    slot_in,
    slot_cot,
    act_all,
    gpre_all,
    scaled_all,
    gslot_all,
    gback_all,
    attn_xhat,
    moe_xhat,
    hidden_ref,
    padded,
    route_pad,
    pair_send,
    pair_recv,
    send_sem,
    recv_sem,
    back_send,
    back_recv,
    small_send,
    small_recv,
    load_sem,
    store_sem,
):
    place, ahead = places()
    barrier = pltpu.get_barrier_semaphore()
    peers = [(axis, d) for axis, group in GROUP.items() for d in range(1, group)]
    for axis, d in peers:
        pl.semaphore_signal(barrier, inc=1, device_id=ahead(axis, d), device_id_type=MESH)
    loads = []
    for src, dst in (
        (w_qkv_hbm, w_qkv_ref),
        (w_out_hbm, w_out_ref),
        (w_in_hbm, w_in_ref),
        (w_exp_hbm, w_exp_ref),
    ):
        loads.append(pltpu.make_async_copy(src, dst, load_sem.at[len(loads)]))
        loads[-1].start()

    def remote(src, dst, send, recv, axis, distance=1):
        copy = pltpu.make_async_remote_copy(
            src_ref=src,
            dst_ref=dst,
            send_sem=send,
            recv_sem=recv,
            device_id=ahead(axis, distance),
            device_id_type=MESH,
        )
        copy.start()
        return copy

    unsent = []

    def exchange(i, src, dst):
        copy = remote(src, dst, pair_send.at[i], pair_recv.at[i], "pair")
        unsent.append(copy)
        return copy

    spots = [0]
    stores = []

    class Chain:
        def __init__(self, c, base, size):
            self.c, self.base, self.size, self.order = c, base, size, ORDERS[c % 2]
            self.first, self.whole = base, size
            self.k, self.back, self.copies = 0, PHASES - 1, []

        def send(self):
            axis = self.order[self.k]
            group, index = GROUP[axis], place[axis]
            self.spot, earlier, self.copies = spots[0], self.copies, []
            if axis == "z":
                n = self.size
                add_tiles(landing, self.spot + index * n, n, [(held, self.base)])
                spots[0] += group * n
            else:
                n = self.size // group
                spots[0] += (group - 1) * n
            for d in range(1, group):
                if axis == "z":
                    src, dst = self.base, self.spot + index * n
                else:
                    src, dst = self.base + (index + d) % group * n, self.spot + (d - 1) * n
                self.copies.append(
                    remote(
                        held.at[pl.ds(src, n)],
                        landing.at[pl.ds(dst, n)],
                        send_sem.at[self.c, self.k, d - 1],
                        recv_sem.at[self.c, self.k, d - 1],
                        axis,
                        d,
                    )
                )
            if axis != "z":
                self.base, self.size = self.base + index * n, n
            for copy in earlier:
                copy.wait_send()

        def send_back(self):
            axis = self.order[self.back]
            earlier, self.copies = self.copies, []
            part = sum_ref.at[pl.ds(self.base, self.size)]
            for d in range(1, GROUP[axis]):
                self.copies.append(
                    remote(
                        part,
                        part,
                        back_send.at[self.c, self.back, d - 1],
                        back_recv.at[self.c, self.back, d - 1],
                        axis,
                        d,
                    )
                )
            for copy in earlier:
                copy.wait_send()

        def advance(self):
            for copy in self.copies:
                copy.wait_recv()
            if self.k < PHASES:
                axis = self.order[self.k]
                n = self.size
                if axis == "z":
                    parts = [(landing, self.spot + j * n) for j in range(GROUP[axis])]
                    add_tiles(sum_ref, self.base, n, parts)
                else:
                    parts = [(landing, self.spot + j * n) for j in range(GROUP[axis] - 1)]
                    add_tiles(held, self.base, n, [(held, self.base)] + parts)
                self.k += 1
                if self.k < PHASES:
                    self.send()
                    return
            else:
                axis = self.order[self.back]
                self.base = self.base - place[axis] * self.size
                self.size = self.size * GROUP[axis]
            self.back -= 1
            if self.back >= 0:
                self.send_back()
                return
            rows = pl.ds(self.first, self.whole)
            copy = pltpu.make_async_copy(
                sum_ref.at[rows], sum_out.at[rows], store_sem.at[self.c]
            )
            copy.start()
            stores.append(copy)
            for copy in self.copies:
                copy.wait_send()

    class Small:
        def __init__(self, b, held, landing, rows):
            self.b, self.held, self.landing, self.rows = b, held, landing, rows
            self.k, self.copies = 0, []

        def send(self):
            k, axis = self.k, SMALL_ORDER[self.k]
            group, index = GROUP[axis], place[axis]
            n = SHARED_ROWS[self.b] if axis == "pair" else self.rows
            earlier, self.copies = self.copies, []
            slot = 0
            if group > 2:
                slot = index
                self.landing[k, slot] = self.held[k]
            for d in range(1, group):
                self.copies.append(
                    remote(
                        self.held.at[k, pl.ds(0, n)],
                        self.landing.at[k, slot, pl.ds(0, n)],
                        small_send.at[self.b, k, d - 1],
                        small_recv.at[self.b, k, d - 1],
                        axis,
                        d,
                    )
                )
            for copy in earlier:
                copy.wait_send()

        def advance(self):
            for copy in self.copies:
                copy.wait_recv()
            k, axis = self.k, SMALL_ORDER[self.k]
            held, landing = self.held, self.landing
            if axis == "pair":
                n = SHARED_ROWS[self.b]
                held[k + 1, :n] = held[k, :n] + landing[k, 0, :n]
                held[k + 1, n:] = held[k, n:]
            elif GROUP[axis] == 2:
                held[k + 1] = held[k] + landing[k, 0]
            else:
                held[k + 1] = landing[k, 0] + landing[k, 1] + landing[k, 2] + landing[k, 3]
            self.k += 1
            if self.k < len(SMALL_ORDER):
                self.send()
                return
            small_out[EARLY_ROWS * self.b : EARLY_ROWS * self.b + self.rows] = held[self.k]
            for copy in self.copies:
                copy.wait_send()

    early = Small(0, early_held, early_landing, EARLY_ROWS)
    late = Small(1, late_held, late_landing, LATE_ROWS)
    batches, start = [], 0
    for batch in BATCHES:
        batches.append([])
        for size in batch:
            batches[-1].append(Chain(2 * len(batches) - 2 + len(batches[-1]), start, size))
            start += size

    def send_batch(b):
        for chain in batches[b]:
            chain.send()

    def advance_batch(b):
        for chain in batches[b]:
            chain.advance()

    def row_of(ref):
        return ref[...].astype(F32).reshape(1, D)

    attn_gain, attn_shift = row_of(attn_gain_ref), row_of(attn_shift_ref)
    moe_gain, moe_shift = row_of(moe_gain_ref), row_of(moe_shift_ref)
    out_bias = row_of(out_bias_ref)

    padded[:, SEQ - 5 :] = jnp.zeros((2, ROWS - SEQ + 5, D), F32)
    padded[0, :SEQ] = tok_ref[0].astype(F32)
    padded[1, :SEQ] = cot_ref[0].astype(F32)
    tok = padded[0]
    xhat, attn_r = normalize(tok)
    attn_xhat[...] = xhat
    normed[0] = (xhat * attn_gain + attn_shift).astype(BF16)
    cots[0] = padded[1].astype(BF16)
    pl.semaphore_wait(barrier, len(peers))
    normed_copy = exchange(0, normed.at[0], normed.at[1])
    cot_copy = exchange(1, cots.at[0], cots.at[1])

    key_mask = lax.broadcasted_iota(jnp.int32, (ROWS, ROWS), 1) < SEQ

    def project(i):
        proj = dot(normed[i], w_qkv_ref[...], LAST)
        bias = qv_bias_ref[...].astype(F32)
        for h in range(HEADS):
            at = h * 3 * HD
            q_all[i, h] = (proj[:, at : at + HD] + bias[h : h + 1, :HD]).astype(BF16)
            k_all[i, h] = proj[:, at + HD : at + 2 * HD].astype(BF16)
            v_all[i, h] = (proj[:, at + 2 * HD : at + 3 * HD] + bias[h : h + 1, HD:]).astype(BF16)

    def attend(i):
        total = jnp.zeros((ROWS, D), F32)
        for h in range(HEADS):
            scores = dot(q_all[i, h], k_all[i, h], LAST) * (1.0 / math.sqrt(HD))
            scores = jnp.where(key_mask, scores, -1e30)
            weights = jnp.exp(scores - jnp.max(scores, axis=-1, keepdims=True))
            p = weights / jnp.sum(weights, axis=-1, keepdims=True)
            probs[i, h] = p
            c = dot(p.astype(BF16), v_all[i, h]).astype(BF16)
            ctx[h, i] = c
            total += dot(c, w_out_ref[h * HD : (h + 1) * HD])
        return total

    tensor = lax.axis_index("tensor")
    before = (
        lax.broadcasted_iota(jnp.int32, (ROWS, ROWS), 1)
        < lax.broadcasted_iota(jnp.int32, (ROWS, ROWS), 0)
    ).astype(BF16)
    lane = lax.broadcasted_iota(jnp.int32, (ROWS, LANES), 1).astype(F32)
    sub = lax.broadcasted_iota(jnp.int32, (8, ROWS), 0).astype(F32)
    slot_lane = lax.broadcasted_iota(jnp.int32, (ROWS, CAP), 1).astype(F32)
    slot_sub = lax.broadcasted_iota(jnp.int32, (CAP, ROWS), 0).astype(F32)
    same = (
        lax.broadcasted_iota(jnp.int32, (ROWS, ROWS), 0)
        == lax.broadcasted_iota(jnp.int32, (ROWS, ROWS), 1)
    ).astype(BF16)
    pos_col, pos_row = [], []
    for i in range(2):
        route_pad[i] = jnp.full((2, ROWS), -1.0, F32)
        first, second = route_ref[0].astype(F32), route_ref[1].astype(F32)
        route_pad[i, :, :SEQ] = jnp.where(tensor == i, first, second)
        row = route_pad[i]
        col = dot(same, row.astype(BF16), LAST)
        a0, a1 = col[:, 0:1] == lane, col[:, 1:2] == lane
        f0, f1 = a0.astype(F32), a1.astype(F32)
        c0 = dot(before, f0.astype(BF16))
        c1 = dot(before, f1.astype(BF16)) + column_sum(f0)
        pos_col.append(jnp.where(a0, c0, jnp.where(a1, c1, -1.0)))
        a0, a1 = row[0:1] == sub, row[1:2] == sub
        f0, f1 = a0.astype(F32), a1.astype(F32)
        c0 = dot(f0.astype(BF16), before, LAST)
        c1 = dot(f1.astype(BF16), before, LAST) + jnp.sum(f0, axis=1, keepdims=True)
        pos_row.append(jnp.where(a0, c0, jnp.where(a1, c1, -1.0)))
    kept_row = [((p >= 0.0) & (p < CAP)).astype(F32) for p in pos_row]

    def dispatch(i, e):
        return (pos_col[i][:, e : e + 1] == slot_lane).astype(F32)

    def dispatch_t(i, e):
        return (pos_row[i][e : e + 1] == slot_sub).astype(F32)

    loads[0].wait()
    loads[1].wait()
    project(0)
    normed_copy.wait_recv()
    project(1)
    att_part[0] = attend(1).astype(BF16)
    att_copy = exchange(2, att_part.at[0], att_part.at[1])
    own_part = attend(0)
    cot_copy.wait_recv()
    for i in range(2):
        for e in range(EXPERTS):
            slot_cot[e, i * CAP : (i + 1) * CAP] = dot(
                dispatch_t(i, e).astype(BF16), cots[i]
            ).astype(BF16)
    att_copy.wait_recv()
    hidden = tok + (own_part.astype(BF16).astype(F32) + att_part[1].astype(F32)) + out_bias
    hidden_ref[...] = hidden
    xhat, moe_r = normalize(hidden)
    moe_xhat[...] = xhat
    moes[0] = (xhat * moe_gain + moe_shift).astype(BF16)
    moe_copy = exchange(3, moes.at[0], moes.at[1])

    router_rows = jnp.concatenate(
        [router_ref[...].astype(F32), jnp.zeros((8 - EXPERTS, D), F32)], axis=0
    )
    router = router_rows.astype(BF16)
    expert_rows = sub < EXPERTS

    def gate(i):
        logits = jnp.where(expert_rows, dot(router, moes[i], LAST), -1e30)
        weights = jnp.exp(logits - jnp.max(logits, axis=0, keepdims=True))
        return weights / column_sum(weights)

    gates, slot_weight = [None, None], [[None] * EXPERTS, [None] * EXPERTS]

    def fill_slots(i):
        gates[i] = gate(i)
        for e in range(EXPERTS):
            pick = dispatch_t(i, e)
            slot_in[e, i * CAP : (i + 1) * CAP] = dot(pick.astype(BF16), moes[i]).astype(BF16)
            slot_weight[i][e] = jnp.sum(pick * gates[i][e : e + 1], axis=1, keepdims=True)

    fill_slots(0)
    moe_copy.wait_recv()
    fill_slots(1)

    gate_rows = [[None] * EXPERTS, [None] * EXPERTS]
    early_held[0] = jnp.zeros((EARLY_ROWS, D), F32)
    loads[2].wait()
    loads[3].wait()
    for e in range(EXPERTS):
        weight = jnp.concatenate([slot_weight[0][e], slot_weight[1][e]], axis=0)
        pre = dot(slot_in[e], w_in_ref[e]) + in_bias_ref[e : e + 1].astype(F32)
        half = 0.5 * (1.0 + lax.erf(pre * (1.0 / math.sqrt(2.0))))
        act_all[e] = (pre * half).astype(BF16)
        slope = half + pre * jnp.exp(-0.5 * pre * pre) * (1.0 / math.sqrt(2.0 * math.pi))
        g = slot_cot[e].astype(F32)
        gs = (g * weight).astype(BF16)
        gslot_all[e] = gs
        gpre = (dot(gs, w_exp_ref[e], LAST) * slope).astype(BF16)
        gpre_all[e] = gpre
        gback_all[e] = dot(gpre, w_in_ref[e], LAST).astype(BF16)
        slot_out = dot(act_all[e], w_exp_ref[e])
        scaled_all[e] = (slot_out * weight).astype(BF16)
        slot_gate = jnp.sum(slot_out * g, axis=1, keepdims=True)
        for i in range(2):
            gate_rows[i][e] = column_sum(
                dispatch_t(i, e) * slot_gate[i * CAP : (i + 1) * CAP]
            )

        at = e * (IN_TILES + EXP_TILES)
        store_tiles(held, at, dot(slot_in[e], gpre_all[e], FIRST))
        store_tiles(held, at + IN_TILES, dot(act_all[e], gslot_all[e], FIRST))
        bias = column_sum(gpre_all[e].astype(F32))
        for j in range(FF // D):
            early_held[0, 16 + 2 * e + j : 17 + 2 * e + j] = bias[:, j * D : (j + 1) * D]
        send_batch(e)

    def combine(i, ref):
        total = jnp.zeros((ROWS, D), F32)
        for e in range(EXPERTS):
            total += dot(dispatch(i, e).astype(BF16), ref[e, i * CAP : (i + 1) * CAP])
        return total

    def gate_grads(i):
        return jnp.concatenate(gate_rows[i] + [jnp.zeros((8 - EXPERTS, ROWS), F32)], axis=0)

    gmoe_part[0] = combine(1, gback_all).astype(BF16)
    gmoe_copy = exchange(4, gmoe_part.at[0], gmoe_part.at[1])
    gate_part[0] = gate_grads(1)
    gate_copy = exchange(5, gate_part.at[0], gate_part.at[1])
    mix_part[0] = combine(1, scaled_all).astype(BF16)
    mix_copy = exchange(6, mix_part.at[0], mix_part.at[1])

    for e in range(EXPERTS):
        advance_batch(e)

    own_gmoe = combine(0, gback_all).astype(BF16).astype(F32)
    own_mix = combine(0, scaled_all).astype(BF16).astype(F32)
    own_gate = gate_grads(0)
    cot = padded[1]
    bias_rows = jnp.concatenate(
        [exp_bias_ref[...], jnp.zeros((8 - EXPERTS, D), BF16)], axis=0
    )
    share = gates[0] * kept_row[0]
    bias_grad = dot(bias_rows, cots[0], LAST)
    gate_copy.wait_recv()
    grad_gates = (own_gate + gate_part[1] + bias_grad) * kept_row[0]
    grad_logits = gates[0] * (grad_gates - column_sum(gates[0] * grad_gates))
    early_held[0, 3:6] = dot(grad_logits, moes[0].astype(F32), precision=HIGHEST)[:EXPERTS]
    early_held[0, 6:9] = dot(share, cot, precision=HIGHEST)[:EXPERTS]
    router_back = dot(grad_logits, router_rows, FIRST, HIGHEST)
    gmoe_copy.wait_recv()
    gmoe = own_gmoe + gmoe_part[1].astype(F32) + router_back
    grad_hidden = cot + norm_back(gmoe, moe_xhat[...], moe_r, moe_gain)
    ghs[0] = grad_hidden.astype(BF16)
    gh_copy = exchange(7, ghs.at[0], ghs.at[1])
    early_held[0, 0:1] = column_sum(grad_hidden)
    early_held[0, 1:2] = column_sum(gmoe * moe_xhat[...])
    early_held[0, 2:3] = column_sum(gmoe)
    early.send()
    mix_copy.wait_recv()
    block_ref[...] = (
        hidden_ref[...]
        + (own_mix + mix_part[1].astype(F32))
        + dot(share, bias_rows.astype(F32), FIRST, HIGHEST)
    ).astype(BF16)

    def attend_back(i):
        for h in range(HEADS):
            q, k, v, p = q_all[i, h], k_all[i, h], v_all[i, h], probs[i, h]
            gc = dot(ghs[i], w_out_ref[h * HD : (h + 1) * HD], LAST).astype(BF16)
            gp = dot(gc, v, LAST)
            row_dot = jnp.sum(gp * p, axis=-1, keepdims=True)
            graw = (p * (gp - row_dot) * (1.0 / math.sqrt(HD))).astype(BF16)
            at = h * 3 * HD
            gproj[i, :, at : at + HD] = dot(graw, k).astype(BF16)
            gproj[i, :, at + HD : at + 2 * HD] = dot(graw, q, FIRST).astype(BF16)
            gproj[i, :, at + 2 * HD : at + 3 * HD] = dot(p.astype(BF16), gc, FIRST).astype(BF16)

    attend_back(0)
    gh_copy.wait_recv()
    attend_back(1)
    gnorm_part[0] = dot(gproj[1], w_qkv_ref[...]).astype(BF16)
    gnorm_copy = exchange(8, gnorm_part.at[0], gnorm_part.at[1])

    both = gproj[...].reshape(2 * ROWS, QKV)
    at = MOE_TILES
    store_tiles(held, at, dot(both, normed[...].reshape(2 * ROWS, D), FIRST))
    at += QKV_TILES
    gh_both = ghs[...].reshape(2 * ROWS, D)
    for h in range(HEADS):
        grad = dot(ctx[h].reshape(2 * ROWS, HD), gh_both, FIRST)
        for j in range(D // LANES):
            tiles = grad[:, j * LANES : (j + 1) * LANES].astype(BF16)
            spot = at + j * (OUT_TILES // 3) + h * (HD // TILE_ROWS)
            held[spot : spot + HD // TILE_ROWS] = tiles.reshape(HD // TILE_ROWS, TILE_ROWS, LANES)
    at += OUT_TILES
    held[at:TILES] = jnp.zeros((TILES - at, TILE_ROWS, LANES), BF16)
    send_batch(EXPERTS)
    late_held[0] = jnp.zeros((LATE_ROWS, D), F32)
    bias = column_sum(both.astype(F32))
    late_held[0, 8:9] = bias[:, :D]
    late_held[0, 9:10, 0 : QKV - D] = bias[:, D:]
    for e in range(EXPERTS):
        advance_batch(e)
    early.advance()

    own_gnorm = dot(gproj[0], w_qkv_ref[...]).astype(BF16).astype(F32)
    gnorm_copy.wait_recv()
    gnorm = own_gnorm + gnorm_part[1].astype(F32)
    xhat = attn_xhat[...]
    late_held[0, 0:1] = column_sum(gnorm * xhat)
    late_held[0, 1:2] = column_sum(gnorm)
    late.send()
    grad_tok_ref[...] = (grad_hidden + norm_back(gnorm, xhat, attn_r, attn_gain)).astype(BF16)

    for k in range(2 * PHASES - 1):
        if k < 2 * PHASES - 3:
            for e in range(EXPERTS):
                advance_batch(e)
        advance_batch(EXPERTS)
        if k < len(SMALL_ORDER) - 1:
            early.advance()
        if k < len(SMALL_ORDER):
            late.advance()
    for copy in stores:
        copy.wait()
    for copy in unsent:
        copy.wait_send()


def run_block(*args):
    def bf(*shape):
        return pltpu.VMEM(shape, BF16)

    def fl(*shape):
        return pltpu.VMEM(shape, F32)

    dma = pltpu.SemaphoreType.DMA
    slots = 2 * CAP
    steps = len(SMALL_ORDER)
    vmem = pl.BlockSpec(memory_space=pltpu.VMEM)
    anywhere = pl.BlockSpec(memory_space=pl.ANY)
    return pl.pallas_call(
        block_kernel,
        out_shape=(
            jax.ShapeDtypeStruct((ROWS, D), BF16),
            jax.ShapeDtypeStruct((ROWS, D), BF16),
            jax.ShapeDtypeStruct((TILES, TILE_ROWS, LANES), BF16),
            jax.ShapeDtypeStruct((EARLY_ROWS + LATE_ROWS, D), F32),
        ),
        in_specs=[anywhere if i in (3, 5, 10, 12) else vmem for i in range(len(args))],
        out_specs=[vmem, vmem, anywhere, vmem],
        scratch_shapes=[
            bf(QKV, D),
            bf(HEADS * HD, D),
            bf(EXPERTS, D, FF),
            bf(EXPERTS, FF, D),
            bf(TILES, TILE_ROWS, LANES),
            bf(LANDING, TILE_ROWS, LANES),
            bf(TILES, TILE_ROWS, LANES),
            fl(steps + 1, EARLY_ROWS, D),
            fl(steps, RING, EARLY_ROWS, D),
            fl(steps + 1, LATE_ROWS, D),
            fl(steps, RING, LATE_ROWS, D),
            bf(2, ROWS, D),
            bf(2, ROWS, D),
            bf(2, ROWS, D),
            bf(2, ROWS, D),
            bf(2, ROWS, D),
            bf(2, ROWS, D),
            bf(2, ROWS, D),
            fl(2, 8, ROWS),
            bf(2, ROWS, D),
            bf(2, HEADS, ROWS, HD),
            bf(2, HEADS, ROWS, HD),
            bf(2, HEADS, ROWS, HD),
            fl(2, HEADS, ROWS, ROWS),
            bf(HEADS, 2, ROWS, HD),
            bf(2, ROWS, QKV),
            bf(EXPERTS, slots, D),
            bf(EXPERTS, slots, D),
            bf(EXPERTS, slots, FF),
            bf(EXPERTS, slots, FF),
            bf(EXPERTS, slots, D),
            bf(EXPERTS, slots, D),
            bf(EXPERTS, slots, D),
            fl(ROWS, D),
            fl(ROWS, D),
            fl(ROWS, D),
            fl(2, ROWS, D),
            fl(2, 2, ROWS),
            dma((9,)),
            dma((9,)),
            dma((CHAIN_COUNT, PHASES, RING - 1)),
            dma((CHAIN_COUNT, PHASES, RING - 1)),
            dma((CHAIN_COUNT, PHASES - 1, RING - 1)),
            dma((CHAIN_COUNT, PHASES - 1, RING - 1)),
            dma((2, steps, RING - 1)),
            dma((2, steps, RING - 1)),
            dma((4,)),
            dma((CHAIN_COUNT,)),
        ],
        compiler_params=pltpu.CompilerParams(
            collective_id=0, has_side_effects=True, vmem_limit_bytes=56 * 1024 * 1024
        ),
    )(*args)


def unpack_kernel(
    block_ref,
    grad_tok_ref,
    sum_ref,
    small_ref,
    block_out,
    grad_tok_out,
    attn_gain,
    attn_shift,
    w_qkv_out,
    qv_bias,
    w_out_out,
    out_bias,
    moe_gain,
    moe_shift,
    router,
    w_in_out,
    in_bias,
    w_exp_out,
    exp_bias,
    sums,
    w_qkv,
    w_out,
    w_in,
    w_exp,
    in_sem,
    out_sem,
):
    pieces = []
    for e in range(EXPERTS):
        at = e * (IN_TILES + EXP_TILES)
        pieces.append((at, IN_TILES, D, FF, w_in.at[e], w_in_out.at[e]))
        pieces.append((at + IN_TILES, EXP_TILES, FF, D, w_exp.at[e], w_exp_out.at[e]))
    at = MOE_TILES
    pieces.append((at, QKV_TILES, QKV, D, w_qkv, w_qkv_out))
    pieces.append((at + QKV_TILES, OUT_TILES, HEADS * HD, D, w_out, w_out_out))
    arriving = []
    for i, (at, tiles, *_) in enumerate(pieces):
        rows = pl.ds(at, tiles)
        arriving.append(pltpu.make_async_copy(sum_ref.at[rows], sums.at[rows], in_sem.at[i]))
        arriving[-1].start()
    block_out[0] = block_ref[:SEQ]
    grad_tok_out[0] = grad_tok_ref[:SEQ]
    small = small_ref[...]
    rows = (24, 25, 0, 1, 2)
    for ref, row in zip((attn_gain, attn_shift, out_bias, moe_gain, moe_shift), rows):
        ref[...] = small[row]
    router[...] = small[3:6]
    exp_bias[...] = small[6:9]
    for e in range(EXPERTS):
        for j in range(FF // D):
            in_bias[e : e + 1, j * D : (j + 1) * D] = small[16 + 2 * e + j : 17 + 2 * e + j]
    bias = jnp.concatenate([small[32:33], small[33:34]], axis=1)
    for h in range(HEADS):
        at = 3 * h * HD
        qv_bias[h : h + 1, :HD] = bias[:, at : at + HD]
        qv_bias[h : h + 1, HD:] = bias[:, at + 2 * HD : at + 3 * HD]
    leaving = []
    for i, (at, tiles, rows, lanes, held, out) in enumerate(pieces):
        arriving[i].wait()
        per = rows // TILE_ROWS
        for j in range(-(-lanes // LANES)):
            width = min(LANES, lanes - j * LANES)
            part = sums[at + j * per : at + (j + 1) * per].reshape(rows, LANES)
            held[:, j * LANES : j * LANES + width] = part[:, :width].astype(F32)
        leaving.append(pltpu.make_async_copy(held, out, out_sem.at[i]))
        leaving[-1].start()
    for copy in leaving:
        copy.wait()


def unpack(*args):
    def out(shape, dtype=F32):
        return jax.ShapeDtypeStruct(shape, dtype)

    vmem = pl.BlockSpec(memory_space=pltpu.VMEM)
    anywhere = pl.BlockSpec(memory_space=pl.ANY)
    wide = (4, 6, 11, 13)
    shapes = (
        out((1, SEQ, D), BF16),
        out((1, SEQ, D), BF16),
        out((D,)),
        out((D,)),
        out((QKV, D)),
        out((HEADS, 2 * HD)),
        out((HEADS * HD, D)),
        out((D,)),
        out((D,)),
        out((D,)),
        out((EXPERTS, D)),
        out((EXPERTS, D, FF)),
        out((EXPERTS, FF)),
        out((EXPERTS, FF, D)),
        out((EXPERTS, D)),
    )
    return pl.pallas_call(
        unpack_kernel,
        out_shape=shapes,
        in_specs=[vmem, vmem, anywhere, vmem],
        out_specs=[anywhere if i in wide else vmem for i in range(len(shapes))],
        scratch_shapes=[
            pltpu.VMEM((TILES, TILE_ROWS, LANES), BF16),
            pltpu.VMEM((QKV, D), F32),
            pltpu.VMEM((HEADS * HD, D), F32),
            pltpu.VMEM((EXPERTS, D, FF), F32),
            pltpu.VMEM((EXPERTS, FF, D), F32),
            pltpu.SemaphoreType.DMA((8,)),
            pltpu.SemaphoreType.DMA((8,)),
        ],
        compiler_params=pltpu.CompilerParams(vmem_limit_bytes=58 * 1024 * 1024),
    )(*args)


def on_device(
    tokens,
    attn_gain,
    attn_shift,
    w_qkv,
    qv_bias,
    w_out,
    out_bias,
    moe_gain,
    moe_shift,
    router,
    w_in,
    in_bias,
    w_exp,
    exp_bias,
    routes,
    cotangent,
):
    outs = list(
        unpack(
            *run_block(
                tokens,
                attn_gain,
                attn_shift,
                jnp.transpose(w_qkv, (1, 2, 0)).reshape(QKV, D),
                qv_bias,
                w_out.reshape(HEADS * HD, D),
                out_bias,
                moe_gain,
                moe_shift,
                router.T,
                w_in,
                in_bias,
                w_exp,
                exp_bias,
                jnp.transpose(routes, (0, 2, 1)),
                cotangent,
            )
        )
    )
    outs[4] = jnp.transpose(outs[4].reshape(HEADS, 3 * HD, D), (2, 0, 1))
    outs[10] = outs[10].T
    outs[6] = outs[6].reshape(HEADS, HD, D)
    return tuple(outs)


def solution(mesh):
    placed = (
        P(("dp", "tensor"), None, None),
        P(),
        P(),
        P(None, "tensor", None),
        P("tensor", None),
        P("tensor", None, None),
        P(),
        P(),
        P(),
        P(),
        P(None, None, "tensor"),
        P(None, "tensor"),
        P(None, "tensor", None),
        P(),
        P("dp", None, None),
        P(("dp", "tensor"), None, None),
    )
    return jax.shard_map(
        on_device,
        mesh=mesh,
        in_specs=placed,
        out_specs=(
            P(("dp", "tensor"), None, None),
            P(("dp", "tensor"), None, None),
            P(),
            P(),
            P(None, "tensor", None),
            P("tensor", None),
            P("tensor", None, None),
            P(),
            P(),
            P(),
            P(),
            P(None, None, "tensor"),
            P(None, "tensor"),
            P(None, "tensor", None),
            P(),
        ),
        check_vma=False,
    )
```

```python
import functools
import math

import jax
import jax.numpy as jnp
from jax import lax
from jax.experimental import pallas as pl
from jax.experimental.pallas import tpu as pltpu
from jax.sharding import PartitionSpec as P

MESH = pl.DeviceIdType.MESH
RING = 4
D, SEQ, HEADS, HD, FF, EXPERTS, CAP = 384, 197, 3, 64, 768, 3, 128
ROWS = 208
QKV = 3 * HEADS * HD
TILE_ROWS = 16
LANES = 128
IN_TILES = (D // TILE_ROWS) * (FF // LANES)
EXP_TILES = (FF // TILE_ROWS) * (D // LANES)
MOE_TILES = EXPERTS * (IN_TILES + EXP_TILES)
QKV_TILES = (QKV // TILE_ROWS) * (D // LANES)
OUT_TILES = (HEADS * HD // TILE_ROWS) * (D // LANES)
BATCHES = ((128, 160),) * EXPERTS + ((64, 96),)
CHAIN_COUNT = 2 * len(BATCHES)
TILES = sum(sum(batch) for batch in BATCHES)
ORDERS = (("core", "x", "y", "z"), ("core", "y", "x", "z"))
GROUP = {"pair": 2, "core": 2, "x": RING, "y": RING, "z": RING}
PHASES = 4
LANDING = sum(c // 2 + 3 * (c // 8) + 7 * (c // 32) for batch in BATCHES for c in batch)
SMALL_ORDER = ("pair", "core", "x", "y", "z")
EARLY_ROWS, LATE_ROWS = 16, 8
SHARED_ROWS = (9, 2)
F32 = jnp.float32
BF16 = jnp.bfloat16
HIGHEST = lax.Precision.HIGHEST


def places():
    me = lax.axis_index("dp")
    tensor = lax.axis_index("tensor")
    at = {
        "pair": tensor,
        "core": me % 2,
        "x": (me // 2) % RING,
        "z": (me // (2 * RING)) % RING,
        "y": me // (2 * RING * RING),
    }

    def ahead(axis, distance):
        if axis == "pair":
            return {"tensor": 1 - tensor}
        to = dict(at)
        to[axis] = (at[axis] + distance) % GROUP[axis]
        return {"dp": ((to["y"] * RING + to["z"]) * RING + to["x"]) * 2 + to["core"]}

    return at, ahead


def dot(a, b, dims=((1,), (0,)), precision=None):
    return lax.dot_general(
        a, b, (dims, ((), ())), precision=precision, preferred_element_type=F32
    )


LAST = ((1,), (1,))
FIRST = ((0,), (0,))


def normalize(v):
    centre = v - jnp.mean(v, axis=-1, keepdims=True)
    r = lax.rsqrt(jnp.mean(centre * centre, axis=-1, keepdims=True) + 1e-06)
    return centre * r, r


def norm_back(grad, xhat, r, gain):
    g = grad * gain
    return r * (
        g
        - jnp.mean(g, axis=-1, keepdims=True)
        - xhat * jnp.mean(g * xhat, axis=-1, keepdims=True)
    )


def column_sum(v):
    return jnp.sum(v, axis=0, keepdims=True)


def add_tiles(out, at, count, parts):
    step = max(k for k in range(1, 17) if count % k == 0)

    @pl.loop(0, count // step)
    def _(i):
        total = None
        for ref, start in parts:
            piece = ref[pl.ds(start + i * step, step)].astype(F32)
            total = piece if total is None else total + piece
        out[pl.ds(at + i * step, step)] = total.astype(out.dtype)


def store_tiles(ref, at, value):
    rows, lanes = value.shape
    per = rows // TILE_ROWS
    for j in range(-(-lanes // LANES)):
        part = value[:, j * LANES : min((j + 1) * LANES, lanes)]
        if part.shape[1] < LANES:
            part = jnp.concatenate(
                [part, jnp.zeros((rows, LANES - part.shape[1]), part.dtype)], axis=1
            )
        ref[at + j * per : at + (j + 1) * per] = part.astype(BF16).reshape(per, TILE_ROWS, LANES)


def block_kernel(*refs):
    count = 16
    sources, (block_out, grad_tok_out, sum_out, small_hbm) = refs[:count], refs[count : count + 4]
    inputs = refs[count + 4 : 2 * count + 4]
    results = refs[2 * count + 4 : 2 * count + 7]
    work = refs[2 * count + 7 : -2]
    load_sem, result_sem = refs[-2:]
    loads = [
        pltpu.make_async_copy(src, dst, load_sem.at[i])
        for i, (src, dst) in enumerate(zip(sources, inputs))
    ]
    stores = []

    def store(i, out):
        copy = pltpu.make_async_copy(results[i], out, result_sem.at[i])
        copy.start()
        stores.append(copy)

    finish = (
        lambda: store(0, block_out),
        lambda: store(1, grad_tok_out),
        lambda: store(2, small_hbm),
    )
    block_body(loads, stores, finish, *inputs, *results[:2], sum_out, results[2], *work)


def block_body(
    loads,
    stores,
    finish,
    tok_ref,
    attn_gain_ref,
    attn_shift_ref,
    w_qkv_ref,
    qv_bias_ref,
    w_out_ref,
    out_bias_ref,
    moe_gain_ref,
    moe_shift_ref,
    router_ref,
    w_in_ref,
    in_bias_ref,
    w_exp_ref,
    exp_bias_ref,
    route_ref,
    cot_ref,
    block_ref,
    grad_tok_ref,
    sum_out,
    small_out,
    held,
    landing,
    sum_ref,
    early_held,
    early_landing,
    late_held,
    late_landing,
    toks,
    normed,
    cots,
    moes,
    ghs,
    att_part,
    att_other,
    mix_part,
    gmoe_part,
    gmoe_other,
    gate_part,
    gate_other,
    gnorm_part,
    q_all,
    k_all,
    v_all,
    probs,
    ctx,
    gproj,
    slot_in,
    slot_cot,
    act_all,
    gpre_all,
    scaled_all,
    gslot_all,
    gback_all,
    attn_xhat,
    moe_xhat,
    hidden_ref,
    gh_ref,
    padded,
    route_pad,
    pair_send,
    pair_recv,
    send_sem,
    recv_sem,
    back_send,
    back_recv,
    small_send,
    small_recv,
    store_sem,
):
    place, ahead = places()
    barrier = pltpu.get_barrier_semaphore()
    peers = [(axis, d) for axis, group in GROUP.items() for d in range(1, group)]
    for axis, d in peers:
        pl.semaphore_signal(barrier, inc=1, device_id=ahead(axis, d), device_id_type=MESH)
    big = (3, 5, 10, 12)
    for i in [i for i in range(len(loads)) if i not in big] + list(big):
        loads[i].start()

    def remote(src, dst, send, recv, axis, distance=1):
        copy = pltpu.make_async_remote_copy(
            src_ref=src,
            dst_ref=dst,
            send_sem=send,
            recv_sem=recv,
            device_id=ahead(axis, distance),
            device_id_type=MESH,
        )
        copy.start()
        return copy

    unsent = []

    def exchange(i, src, dst):
        copy = remote(src, dst, pair_send.at[i], pair_recv.at[i], "pair")
        unsent.append(copy)
        return copy

    spots = [0]

    class Chain:
        def __init__(self, c, base, size):
            self.c, self.base, self.size, self.order = c, base, size, ORDERS[c % 2]
            self.first, self.whole = base, size
            self.k, self.back, self.copies = 0, PHASES - 1, []

        def send(self):
            axis = self.order[self.k]
            group, index = GROUP[axis], place[axis]
            self.spot, earlier, self.copies = spots[0], self.copies, []
            if axis == "z":
                n = self.size
                add_tiles(landing, self.spot + index * n, n, [(held, self.base)])
                spots[0] += group * n
            else:
                n = self.size // group
                spots[0] += (group - 1) * n
            for d in range(1, group):
                if axis == "z":
                    src, dst = self.base, self.spot + index * n
                else:
                    src, dst = self.base + (index + d) % group * n, self.spot + (d - 1) * n
                self.copies.append(
                    remote(
                        held.at[pl.ds(src, n)],
                        landing.at[pl.ds(dst, n)],
                        send_sem.at[self.c, self.k, d - 1],
                        recv_sem.at[self.c, self.k, d - 1],
                        axis,
                        d,
                    )
                )
            if axis != "z":
                self.base, self.size = self.base + index * n, n
            for copy in earlier:
                copy.wait_send()

        def send_back(self):
            axis = self.order[self.back]
            earlier, self.copies = self.copies, []
            part = sum_ref.at[pl.ds(self.base, self.size)]
            for d in range(1, GROUP[axis]):
                self.copies.append(
                    remote(
                        part,
                        part,
                        back_send.at[self.c, self.back, d - 1],
                        back_recv.at[self.c, self.back, d - 1],
                        axis,
                        d,
                    )
                )
            for copy in earlier:
                copy.wait_send()

        def advance(self):
            for copy in self.copies:
                copy.wait_recv()
            if self.k < PHASES:
                axis = self.order[self.k]
                n = self.size
                if axis == "z":
                    parts = [(landing, self.spot + j * n) for j in range(GROUP[axis])]
                    add_tiles(sum_ref, self.base, n, parts)
                else:
                    parts = [(landing, self.spot + j * n) for j in range(GROUP[axis] - 1)]
                    add_tiles(held, self.base, n, [(held, self.base)] + parts)
                self.k += 1
                if self.k < PHASES:
                    self.send()
                    return
            else:
                axis = self.order[self.back]
                self.base = self.base - place[axis] * self.size
                self.size = self.size * GROUP[axis]
            self.back -= 1
            if self.back >= 0:
                self.send_back()
                return
            rows = pl.ds(self.first, self.whole)
            copy = pltpu.make_async_copy(
                sum_ref.at[rows], sum_out.at[rows], store_sem.at[self.c]
            )
            copy.start()
            stores.append(copy)
            for copy in self.copies:
                copy.wait_send()

    class Small:
        def __init__(self, b, held, landing, rows):
            self.b, self.held, self.landing, self.rows = b, held, landing, rows
            self.k, self.copies = 0, []

        def send(self):
            k, axis = self.k, SMALL_ORDER[self.k]
            group, index = GROUP[axis], place[axis]
            earlier, self.copies = self.copies, []
            slot = 0
            if group > 2:
                slot = index
                self.landing[k, slot] = self.held[k]
            for d in range(1, group):
                self.copies.append(
                    remote(
                        self.held.at[k],
                        self.landing.at[k, slot],
                        small_send.at[self.b, k, d - 1],
                        small_recv.at[self.b, k, d - 1],
                        axis,
                        d,
                    )
                )
            for copy in earlier:
                copy.wait_send()

        def advance(self):
            for copy in self.copies:
                copy.wait_recv()
            k, axis = self.k, SMALL_ORDER[self.k]
            held, landing = self.held, self.landing
            if axis == "pair":
                row = lax.broadcasted_iota(jnp.int32, (self.rows, D), 0)
                other = jnp.where(row < SHARED_ROWS[self.b], landing[k, 0], 0.0)
                held[k + 1] = held[k] + other
            elif GROUP[axis] == 2:
                held[k + 1] = held[k] + landing[k, 0]
            else:
                held[k + 1] = landing[k, 0] + landing[k, 1] + landing[k, 2] + landing[k, 3]
            self.k += 1
            if self.k < len(SMALL_ORDER):
                self.send()
                return
            small_out[EARLY_ROWS * self.b : EARLY_ROWS * self.b + self.rows] = held[self.k]
            for copy in self.copies:
                copy.wait_send()

    early = Small(0, early_held, early_landing, EARLY_ROWS)
    late = Small(1, late_held, late_landing, LATE_ROWS)
    batches, start = [], 0
    for batch in BATCHES:
        batches.append([])
        for size in batch:
            batches[-1].append(Chain(2 * len(batches) - 2 + len(batches[-1]), start, size))
            start += size

    def send_batch(b):
        for chain in batches[b]:
            chain.send()

    def advance_batch(b):
        for chain in batches[b]:
            chain.advance()

    for i in range(len(loads)):
        if i not in big:
            loads[i].wait()

    def row_of(ref):
        return ref[...].astype(F32).reshape(1, D)

    attn_gain, attn_shift = row_of(attn_gain_ref), row_of(attn_shift_ref)
    moe_gain, moe_shift = row_of(moe_gain_ref), row_of(moe_shift_ref)
    out_bias = row_of(out_bias_ref)

    padded[:, SEQ - 5 :] = jnp.zeros((2, ROWS - SEQ + 5, D), F32)
    padded[0, :SEQ] = tok_ref[0].astype(F32)
    padded[1, :SEQ] = cot_ref[0].astype(F32)
    toks[0] = padded[0].astype(BF16)
    cots[0] = padded[1].astype(BF16)
    pl.semaphore_wait(barrier, len(peers))
    tok_copy = exchange(0, toks.at[0], toks.at[1])
    cot_copy = exchange(1, cots.at[0], cots.at[1])
    xhat, attn_r = normalize(padded[0])
    attn_xhat[...] = xhat
    normed[0] = (xhat * attn_gain + attn_shift).astype(BF16)

    key_mask = lax.broadcasted_iota(jnp.int32, (ROWS, ROWS), 1) < SEQ

    def project(i):
        proj = dot(normed[i], w_qkv_ref[...], LAST)
        bias = qv_bias_ref[...].astype(F32)
        for h in range(HEADS):
            at = h * 3 * HD
            q_all[i, h] = (proj[:, at : at + HD] + bias[h : h + 1, :HD]).astype(BF16)
            k_all[i, h] = proj[:, at + HD : at + 2 * HD].astype(BF16)
            v_all[i, h] = (proj[:, at + 2 * HD : at + 3 * HD] + bias[h : h + 1, HD:]).astype(BF16)

    def attend(i):
        total = jnp.zeros((ROWS, D), F32)
        for h in range(HEADS):
            scores = dot(q_all[i, h], k_all[i, h], LAST) * (1.0 / math.sqrt(HD))
            scores = jnp.where(key_mask, scores, -1e30)
            weights = jnp.exp(scores - jnp.max(scores, axis=-1, keepdims=True))
            p = weights / jnp.sum(weights, axis=-1, keepdims=True)
            probs[i, h] = p
            c = dot(p.astype(BF16), v_all[i, h]).astype(BF16)
            ctx[h, i] = c
            total += dot(c, w_out_ref[h * HD : (h + 1) * HD])
        return total

    tensor = lax.axis_index("tensor")
    before = (
        lax.broadcasted_iota(jnp.int32, (ROWS, ROWS), 1)
        < lax.broadcasted_iota(jnp.int32, (ROWS, ROWS), 0)
    ).astype(BF16)
    lane = lax.broadcasted_iota(jnp.int32, (ROWS, LANES), 1).astype(F32)
    sub = lax.broadcasted_iota(jnp.int32, (8, ROWS), 0).astype(F32)
    slot_lane = lax.broadcasted_iota(jnp.int32, (ROWS, CAP), 1).astype(F32)
    slot_sub = lax.broadcasted_iota(jnp.int32, (CAP, ROWS), 0).astype(F32)
    same = (
        lax.broadcasted_iota(jnp.int32, (ROWS, ROWS), 0)
        == lax.broadcasted_iota(jnp.int32, (ROWS, ROWS), 1)
    ).astype(BF16)
    pos_col, pos_row = [], []
    for i in range(2):
        route_pad[i] = jnp.full((2, ROWS), -1.0, F32)
        first, second = route_ref[0].astype(F32), route_ref[1].astype(F32)
        route_pad[i, :, :SEQ] = jnp.where(tensor == i, first, second)
        row = route_pad[i]
        col = dot(same, row.astype(BF16), LAST)
        a0, a1 = col[:, 0:1] == lane, col[:, 1:2] == lane
        f0, f1 = a0.astype(F32), a1.astype(F32)
        c0 = dot(before, f0.astype(BF16))
        c1 = dot(before, f1.astype(BF16)) + column_sum(f0)
        pos_col.append(jnp.where(a0, c0, jnp.where(a1, c1, -1.0)))
        a0, a1 = row[0:1] == sub, row[1:2] == sub
        f0, f1 = a0.astype(F32), a1.astype(F32)
        c0 = dot(f0.astype(BF16), before, LAST)
        c1 = dot(f1.astype(BF16), before, LAST) + jnp.sum(f0, axis=1, keepdims=True)
        pos_row.append(jnp.where(a0, c0, jnp.where(a1, c1, -1.0)))
    kept_row = [((p >= 0.0) & (p < CAP)).astype(F32) for p in pos_row]

    def dispatch(i, e):
        return (pos_col[i][:, e : e + 1] == slot_lane).astype(F32)

    def dispatch_t(i, e):
        return (pos_row[i][e : e + 1] == slot_sub).astype(F32)

    loads[3].wait()
    loads[5].wait()
    project(0)
    att_part[0] = attend(0).astype(BF16)
    att_copies = [exchange(2, att_part.at[0], att_other.at[1])]
    tok_copy.wait_recv()
    normed[1] = (normalize(toks[1].astype(F32))[0] * attn_gain + attn_shift).astype(BF16)
    project(1)
    att_part[1] = attend(1).astype(BF16)
    att_copies.append(exchange(3, att_part.at[1], att_other.at[0]))
    cot_copy.wait_recv()
    for i in range(2):
        for e in range(EXPERTS):
            slot_cot[e, i * CAP : (i + 1) * CAP] = dot(
                dispatch_t(i, e).astype(BF16), cots[i]
            ).astype(BF16)
    moe_r = [None, None]

    def norm_hidden(i):
        total = att_part[i].astype(F32) + att_other[i].astype(F32)
        hidden = toks[i].astype(F32) + total + out_bias
        if i == 0:
            hidden_ref[...] = hidden
        xhat, moe_r[i] = normalize(hidden)
        moe_xhat[i] = xhat
        moes[i] = (xhat * moe_gain + moe_shift).astype(BF16)

    router_rows = jnp.concatenate(
        [router_ref[...].astype(F32), jnp.zeros((8 - EXPERTS, D), F32)], axis=0
    )
    router = router_rows.astype(BF16)
    expert_rows = sub < EXPERTS

    def gate(i):
        logits = jnp.where(expert_rows, dot(router, moes[i], LAST), -1e30)
        weights = jnp.exp(logits - jnp.max(logits, axis=0, keepdims=True))
        return weights / column_sum(weights)

    gates, slot_weight = [None, None], [[None] * EXPERTS, [None] * EXPERTS]

    def fill_slots(i):
        gates[i] = gate(i)
        for e in range(EXPERTS):
            pick = dispatch_t(i, e)
            slot_in[e, i * CAP : (i + 1) * CAP] = dot(pick.astype(BF16), moes[i]).astype(BF16)
            slot_weight[i][e] = jnp.sum(pick * gates[i][e : e + 1], axis=1, keepdims=True)

    for i in (1, 0):
        att_copies[1 - i].wait_recv()
        norm_hidden(i)
        fill_slots(i)

    gate_rows = [[None] * EXPERTS, [None] * EXPERTS]
    early_held[0] = jnp.zeros((EARLY_ROWS, D), F32)
    loads[10].wait()
    loads[12].wait()
    for e in range(EXPERTS):
        weight = jnp.concatenate([slot_weight[0][e], slot_weight[1][e]], axis=0)
        pre = dot(slot_in[e], w_in_ref[e]) + in_bias_ref[e : e + 1].astype(F32)
        half = 0.5 * (1.0 + lax.erf(pre * (1.0 / math.sqrt(2.0))))
        act_all[e] = (pre * half).astype(BF16)
        slope = half + pre * jnp.exp(-0.5 * pre * pre) * (1.0 / math.sqrt(2.0 * math.pi))
        g = slot_cot[e].astype(F32)
        gs = (g * weight).astype(BF16)
        gslot_all[e] = gs
        gpre = (dot(gs, w_exp_ref[e], LAST) * slope).astype(BF16)
        gpre_all[e] = gpre
        gback_all[e] = dot(gpre, w_in_ref[e], LAST).astype(BF16)
        slot_out = dot(act_all[e], w_exp_ref[e])
        scaled_all[e] = (slot_out * weight).astype(BF16)
        slot_gate = jnp.sum(slot_out * g, axis=1, keepdims=True)
        for i in range(2):
            gate_rows[i][e] = column_sum(
                dispatch_t(i, e) * slot_gate[i * CAP : (i + 1) * CAP]
            )

        at = e * (IN_TILES + EXP_TILES)
        store_tiles(held, at, dot(slot_in[e], gpre_all[e], FIRST))
        store_tiles(held, at + IN_TILES, dot(act_all[e], gslot_all[e], FIRST))
        bias = column_sum(gpre_all[e].astype(F32))
        for j in range(FF // D):
            early_held[0, 9 + 2 * e + j : 10 + 2 * e + j] = bias[:, j * D : (j + 1) * D]
        send_batch(e)

    def combine(i, ref):
        total = jnp.zeros((ROWS, D), F32)
        for e in range(EXPERTS):
            total += dot(dispatch(i, e).astype(BF16), ref[e, i * CAP : (i + 1) * CAP])
        return total

    def gate_grads(i):
        return jnp.concatenate(gate_rows[i] + [jnp.zeros((8 - EXPERTS, ROWS), F32)], axis=0)

    gmoe_copies, gate_copies = [], []
    for i in range(2):
        gate_part[i] = gate_grads(i)
        gate_copies.append(exchange(4 + i, gate_part.at[i], gate_other.at[1 - i]))
        gmoe_part[i] = combine(i, gback_all).astype(BF16)
        gmoe_copies.append(exchange(6 + i, gmoe_part.at[i], gmoe_other.at[1 - i]))
    mix_part[0] = combine(1, scaled_all).astype(BF16)
    mix_copy = exchange(8, mix_part.at[0], mix_part.at[1])
    for e in range(EXPERTS):
        advance_batch(e)

    own_mix = combine(0, scaled_all).astype(BF16).astype(F32)
    bias_rows = jnp.concatenate(
        [exp_bias_ref[...], jnp.zeros((8 - EXPERTS, D), BF16)], axis=0
    )
    share = gates[0] * kept_row[0]

    def hidden_back(i):
        bias_grad = dot(bias_rows, cots[i], LAST)
        gate_copies[1 - i].wait_recv()
        grad_gates = (gate_part[i] + gate_other[i] + bias_grad) * kept_row[i]
        grad_logits = gates[i] * (grad_gates - column_sum(gates[i] * grad_gates))
        router_back = dot(grad_logits, router_rows, FIRST, HIGHEST)
        gmoe_copies[1 - i].wait_recv()
        gmoe = gmoe_part[i].astype(F32) + gmoe_other[i].astype(F32) + router_back
        grad = cots[i].astype(F32) + norm_back(gmoe, moe_xhat[i], moe_r[i], moe_gain)
        ghs[i] = grad.astype(BF16)
        if i == 0:
            gh_ref[...] = grad
            early_held[0, 0:1] = column_sum(grad)
            early_held[0, 1:2] = column_sum(gmoe * moe_xhat[0])
            early_held[0, 2:3] = column_sum(gmoe)
            early_held[0, 3:6] = dot(grad_logits, moes[0].astype(F32), precision=HIGHEST)[:EXPERTS]
            early_held[0, 6:9] = dot(share, padded[1], precision=HIGHEST)[:EXPERTS]
            early.send()

    def attend_back(i):
        for h in range(HEADS):
            q, k, v, p = q_all[i, h], k_all[i, h], v_all[i, h], probs[i, h]
            gc = dot(ghs[i], w_out_ref[h * HD : (h + 1) * HD], LAST).astype(BF16)
            gp = dot(gc, v, LAST)
            row_dot = jnp.sum(gp * p, axis=-1, keepdims=True)
            graw = (p * (gp - row_dot) * (1.0 / math.sqrt(HD))).astype(BF16)
            at = h * 3 * HD
            gproj[i, :, at : at + HD] = dot(graw, k).astype(BF16)
            gproj[i, :, at + HD : at + 2 * HD] = dot(graw, q, FIRST).astype(BF16)
            gproj[i, :, at + 2 * HD : at + 3 * HD] = dot(p.astype(BF16), gc, FIRST).astype(BF16)

    hidden_back(1)
    attend_back(1)
    gnorm_part[0] = dot(gproj[1], w_qkv_ref[...]).astype(BF16)
    gnorm_copy = exchange(9, gnorm_part.at[0], gnorm_part.at[1])
    hidden_back(0)
    attend_back(0)

    both = gproj[...].reshape(2 * ROWS, QKV)
    at = MOE_TILES
    store_tiles(held, at, dot(both, normed[...].reshape(2 * ROWS, D), FIRST))
    at += QKV_TILES
    gh_both = ghs[...].reshape(2 * ROWS, D)
    for h in range(HEADS):
        grad = dot(ctx[h].reshape(2 * ROWS, HD), gh_both, FIRST)
        for j in range(D // LANES):
            tiles = grad[:, j * LANES : (j + 1) * LANES].astype(BF16)
            spot = at + j * (OUT_TILES // 3) + h * (HD // TILE_ROWS)
            held[spot : spot + HD // TILE_ROWS] = tiles.reshape(HD // TILE_ROWS, TILE_ROWS, LANES)
    at += OUT_TILES
    held[at:TILES] = jnp.zeros((TILES - at, TILE_ROWS, LANES), BF16)
    send_batch(EXPERTS)
    late_held[0] = jnp.zeros((LATE_ROWS, D), F32)
    bias = column_sum(both.astype(F32))
    late_held[0, 2:3] = bias[:, :D]
    late_held[0, 3:4, 0 : QKV - D] = bias[:, D:]
    for e in range(EXPERTS):
        advance_batch(e)
    early.advance()
    mix_copy.wait_recv()
    block_ref[...] = (
        hidden_ref[...]
        + (own_mix + mix_part[1].astype(F32))
        + dot(share, bias_rows.astype(F32), FIRST, HIGHEST)
    ).astype(BF16)
    finish[0]()

    own_gnorm = dot(gproj[0], w_qkv_ref[...]).astype(BF16).astype(F32)
    gnorm_copy.wait_recv()
    gnorm = own_gnorm + gnorm_part[1].astype(F32)
    xhat = attn_xhat[...]
    late_held[0, 0:1] = column_sum(gnorm * xhat)
    late_held[0, 1:2] = column_sum(gnorm)
    late.send()
    grad_tok_ref[...] = (gh_ref[...] + norm_back(gnorm, xhat, attn_r, attn_gain)).astype(BF16)
    finish[1]()

    for k in range(2 * PHASES - 1):
        advance_batch(EXPERTS)
        if k < 2 * PHASES - 3:
            for e in range(EXPERTS):
                advance_batch(e)
        if k < len(SMALL_ORDER):
            late.advance()
        if k < len(SMALL_ORDER) - 1:
            early.advance()
    finish[2]()
    for copy in stores:
        copy.wait()
    for copy in unsent:
        copy.wait_send()


def run_block(*args):
    def bf(*shape):
        return pltpu.VMEM(shape, BF16)

    def fl(*shape):
        return pltpu.VMEM(shape, F32)

    dma = pltpu.SemaphoreType.DMA
    slots = 2 * CAP
    steps = len(SMALL_ORDER)
    anywhere = pl.BlockSpec(memory_space=pl.ANY)
    return pl.pallas_call(
        block_kernel,
        out_shape=(
            jax.ShapeDtypeStruct((ROWS, D), BF16),
            jax.ShapeDtypeStruct((ROWS, D), BF16),
            jax.ShapeDtypeStruct((TILES, TILE_ROWS, LANES), BF16),
            jax.ShapeDtypeStruct((EARLY_ROWS + LATE_ROWS, D), F32),
        ),
        in_specs=[anywhere] * len(args),
        out_specs=[anywhere] * 4,
        scratch_shapes=[
            *(pltpu.VMEM(arg.shape, arg.dtype) for arg in args),
            bf(ROWS, D),
            bf(ROWS, D),
            fl(EARLY_ROWS + LATE_ROWS, D),
            bf(TILES, TILE_ROWS, LANES),
            bf(LANDING, TILE_ROWS, LANES),
            bf(TILES, TILE_ROWS, LANES),
            fl(steps + 1, EARLY_ROWS, D),
            fl(steps, RING, EARLY_ROWS, D),
            fl(steps + 1, LATE_ROWS, D),
            fl(steps, RING, LATE_ROWS, D),
            bf(2, ROWS, D),
            bf(2, ROWS, D),
            bf(2, ROWS, D),
            bf(2, ROWS, D),
            bf(2, ROWS, D),
            bf(2, ROWS, D),
            bf(2, ROWS, D),
            bf(2, ROWS, D),
            bf(2, ROWS, D),
            bf(2, ROWS, D),
            fl(2, 8, ROWS),
            fl(2, 8, ROWS),
            bf(2, ROWS, D),
            bf(2, HEADS, ROWS, HD),
            bf(2, HEADS, ROWS, HD),
            bf(2, HEADS, ROWS, HD),
            fl(2, HEADS, ROWS, ROWS),
            bf(HEADS, 2, ROWS, HD),
            bf(2, ROWS, QKV),
            bf(EXPERTS, slots, D),
            bf(EXPERTS, slots, D),
            bf(EXPERTS, slots, FF),
            bf(EXPERTS, slots, FF),
            bf(EXPERTS, slots, D),
            bf(EXPERTS, slots, D),
            bf(EXPERTS, slots, D),
            fl(ROWS, D),
            fl(2, ROWS, D),
            fl(ROWS, D),
            fl(ROWS, D),
            fl(2, ROWS, D),
            fl(2, 2, ROWS),
            dma((10,)),
            dma((10,)),
            dma((CHAIN_COUNT, PHASES, RING - 1)),
            dma((CHAIN_COUNT, PHASES, RING - 1)),
            dma((CHAIN_COUNT, PHASES - 1, RING - 1)),
            dma((CHAIN_COUNT, PHASES - 1, RING - 1)),
            dma((2, steps, RING - 1)),
            dma((2, steps, RING - 1)),
            dma((CHAIN_COUNT,)),
            dma((len(args),)),
            dma((3,)),
        ],
        compiler_params=pltpu.CompilerParams(
            collective_id=0, has_side_effects=True, vmem_limit_bytes=56 * 1024 * 1024
        ),
    )(*args)


WIDE = (4, 6, 11, 13)


def unpack_kernel(*refs):
    sources, outs, held = refs[:4], refs[4:19], refs[19:38]
    in_sem, out_sem, rest_in, rest_out = refs[38:]
    block_ref, grad_tok_ref, sums, small_ref = held[:4]
    results = held[4:]
    block, grad_tok, attn_gain, attn_shift, w_qkv, qv_bias, w_out = results[:7]
    out_bias, moe_gain, moe_shift, router, w_in, in_bias, w_exp, exp_bias = results[7:]
    sum_ref = sources[2]
    w_qkv_out, w_out_out, w_in_out, w_exp_out = (outs[i] for i in WIDE)
    pieces = []
    for e in range(EXPERTS):
        at = e * (IN_TILES + EXP_TILES)
        pieces.append((at, IN_TILES, D, FF, w_in.at[e], w_in_out.at[e]))
        pieces.append((at + IN_TILES, EXP_TILES, FF, D, w_exp.at[e], w_exp_out.at[e]))
    at = MOE_TILES
    pieces.append((at, QKV_TILES, QKV, D, w_qkv, w_qkv_out))
    pieces.append((at + QKV_TILES, OUT_TILES, HEADS * HD, D, w_out, w_out_out))
    arriving = []
    for i, (at, tiles, *_) in enumerate(pieces):
        rows = pl.ds(at, tiles)
        arriving.append(pltpu.make_async_copy(sum_ref.at[rows], sums.at[rows], in_sem.at[i]))
        arriving[-1].start()
    narrow = [
        pltpu.make_async_copy(sources[i], held[i], rest_in.at[i]) for i in (0, 1, 3)
    ]
    for copy in narrow:
        copy.start()
    for copy in narrow:
        copy.wait()
    block[0] = block_ref[:SEQ]
    grad_tok[0] = grad_tok_ref[:SEQ]
    small = small_ref[...]
    rows = (16, 17, 0, 1, 2)
    for ref, row in zip((attn_gain, attn_shift, out_bias, moe_gain, moe_shift), rows):
        ref[...] = small[row]
    router[...] = small[3:6]
    exp_bias[...] = small[6:9]
    for e in range(EXPERTS):
        for j in range(FF // D):
            in_bias[e : e + 1, j * D : (j + 1) * D] = small[9 + 2 * e + j : 10 + 2 * e + j]
    bias = jnp.concatenate([small[18:19], small[19:20]], axis=1)
    for h in range(HEADS):
        at = 3 * h * HD
        qv_bias[h : h + 1, :HD] = bias[:, at : at + HD]
        qv_bias[h : h + 1, HD:] = bias[:, at + 2 * HD : at + 3 * HD]
    leaving = []
    for i in range(len(outs)):
        if i not in WIDE:
            leaving.append(pltpu.make_async_copy(results[i], outs[i], rest_out.at[i]))
            leaving[-1].start()
    for i, (at, tiles, rows, lanes, piece, out) in enumerate(pieces):
        arriving[i].wait()
        per = rows // TILE_ROWS
        for j in range(-(-lanes // LANES)):
            width = min(LANES, lanes - j * LANES)
            part = sums[at + j * per : at + (j + 1) * per].reshape(rows, LANES)
            piece[:, j * LANES : j * LANES + width] = part[:, :width].astype(F32)
        leaving.append(pltpu.make_async_copy(piece, out, out_sem.at[i]))
        leaving[-1].start()
    for copy in leaving:
        copy.wait()


def unpack(*args):
    def out(shape, dtype=F32):
        return jax.ShapeDtypeStruct(shape, dtype)

    anywhere = pl.BlockSpec(memory_space=pl.ANY)
    shapes = (
        out((1, SEQ, D), BF16),
        out((1, SEQ, D), BF16),
        out((D,)),
        out((D,)),
        out((QKV, D)),
        out((HEADS, 2 * HD)),
        out((HEADS * HD, D)),
        out((D,)),
        out((D,)),
        out((D,)),
        out((EXPERTS, D)),
        out((EXPERTS, D, FF)),
        out((EXPERTS, FF)),
        out((EXPERTS, FF, D)),
        out((EXPERTS, D)),
    )
    return pl.pallas_call(
        unpack_kernel,
        out_shape=shapes,
        in_specs=[anywhere] * 4,
        out_specs=[anywhere] * len(shapes),
        scratch_shapes=[
            *(pltpu.VMEM(leaf.shape, leaf.dtype) for leaf in args + shapes),
            pltpu.SemaphoreType.DMA((8,)),
            pltpu.SemaphoreType.DMA((8,)),
            pltpu.SemaphoreType.DMA((4,)),
            pltpu.SemaphoreType.DMA((len(shapes),)),
        ],
        compiler_params=pltpu.CompilerParams(vmem_limit_bytes=58 * 1024 * 1024),
    )(*args)


def on_device(
    tokens,
    attn_gain,
    attn_shift,
    w_qkv,
    qv_bias,
    w_out,
    out_bias,
    moe_gain,
    moe_shift,
    router,
    w_in,
    in_bias,
    w_exp,
    exp_bias,
    routes,
    cotangent,
):
    outs = list(
        unpack(
            *run_block(
                tokens,
                attn_gain,
                attn_shift,
                jnp.transpose(w_qkv, (1, 2, 0)).reshape(QKV, D),
                qv_bias,
                w_out.reshape(HEADS * HD, D),
                out_bias,
                moe_gain,
                moe_shift,
                router.T,
                w_in,
                in_bias,
                w_exp,
                exp_bias,
                jnp.transpose(routes, (0, 2, 1)),
                cotangent,
            )
        )
    )
    outs[4] = jnp.transpose(outs[4].reshape(HEADS, 3 * HD, D), (2, 0, 1))
    outs[10] = outs[10].T
    outs[6] = outs[6].reshape(HEADS, HD, D)
    return tuple(outs)


def solution(mesh):
    placed = (
        P(("dp", "tensor"), None, None),
        P(),
        P(),
        P(None, "tensor", None),
        P("tensor", None),
        P("tensor", None, None),
        P(),
        P(),
        P(),
        P(),
        P(None, None, "tensor"),
        P(None, "tensor"),
        P(None, "tensor", None),
        P(),
        P("dp", None, None),
        P(("dp", "tensor"), None, None),
    )
    return jax.shard_map(
        on_device,
        mesh=mesh,
        in_specs=placed,
        out_specs=(
            P(("dp", "tensor"), None, None),
            P(("dp", "tensor"), None, None),
            P(),
            P(),
            P(None, "tensor", None),
            P("tensor", None),
            P("tensor", None, None),
            P(),
            P(),
            P(),
            P(),
            P(None, None, "tensor"),
            P(None, "tensor"),
            P(None, "tensor", None),
            P(),
        ),
        check_vma=False,
    )
```

```python
import functools
import math

import jax
import jax.numpy as jnp
from jax import lax
from jax.experimental import pallas as pl
from jax.experimental.pallas import tpu as pltpu
from jax.sharding import PartitionSpec as P

MESH = pl.DeviceIdType.MESH
RING = 4
D, SEQ, HEADS, HD, FF, EXPERTS, CAP = 384, 197, 3, 64, 768, 3, 128
ROWS = 208
QKV = 3 * HEADS * HD
TILE_ROWS = 16
LANES = 128
IN_TILES = (D // TILE_ROWS) * (FF // LANES)
EXP_TILES = (FF // TILE_ROWS) * (D // LANES)
MOE_TILES = EXPERTS * (IN_TILES + EXP_TILES)
QKV_TILES = (QKV // TILE_ROWS) * (D // LANES)
OUT_TILES = (HEADS * HD // TILE_ROWS) * (D // LANES)
EXPERT_BATCHES = ((128, 160), (288, 288))
BATCHES = EXPERT_BATCHES + ((64, 96),)
READY = (0, None, 1)
CHAIN_COUNT = 2 * len(BATCHES)
TILES = sum(sum(batch) for batch in BATCHES)
ORDERS = (("core", "x", "y", "z"), ("core", "y", "x", "z"))
GROUP = {"pair": 2, "core": 2, "x": RING, "y": RING, "z": RING}
PHASES = 4
LANDING = sum(c // 2 + 3 * (c // 8) + 7 * (c // 32) for batch in BATCHES for c in batch)
SMALL_ORDER = ("pair", "core", "x", "y", "z")
EARLY_ROWS, LATE_ROWS = 16, 8
SHARED_ROWS = (9, 2)
F32 = jnp.float32
BF16 = jnp.bfloat16
HIGHEST = lax.Precision.HIGHEST


def places():
    me = lax.axis_index("dp")
    tensor = lax.axis_index("tensor")
    at = {
        "pair": tensor,
        "core": me % 2,
        "x": (me // 2) % RING,
        "z": (me // (2 * RING)) % RING,
        "y": me // (2 * RING * RING),
    }

    def ahead(axis, distance):
        if axis == "pair":
            return {"tensor": 1 - tensor}
        to = dict(at)
        to[axis] = (at[axis] + distance) % GROUP[axis]
        return {"dp": ((to["y"] * RING + to["z"]) * RING + to["x"]) * 2 + to["core"]}

    return at, ahead


def dot(a, b, dims=((1,), (0,)), precision=None):
    return lax.dot_general(
        a, b, (dims, ((), ())), precision=precision, preferred_element_type=F32
    )


LAST = ((1,), (1,))
FIRST = ((0,), (0,))


def normalize(v):
    centre = v - jnp.mean(v, axis=-1, keepdims=True)
    r = lax.rsqrt(jnp.mean(centre * centre, axis=-1, keepdims=True) + 1e-06)
    return centre * r, r


def norm_back(grad, xhat, r, gain):
    g = grad * gain
    return r * (
        g
        - jnp.mean(g, axis=-1, keepdims=True)
        - xhat * jnp.mean(g * xhat, axis=-1, keepdims=True)
    )


def column_sum(v):
    return jnp.sum(v, axis=0, keepdims=True)


def add_tiles(out, at, count, parts):
    step = max(k for k in range(1, 17) if count % k == 0)

    @pl.loop(0, count // step)
    def _(i):
        total = None
        for ref, start in parts:
            piece = ref[pl.ds(start + i * step, step)].astype(F32)
            total = piece if total is None else total + piece
        out[pl.ds(at + i * step, step)] = total.astype(out.dtype)


def store_tiles(ref, at, value):
    rows, lanes = value.shape
    per = rows // TILE_ROWS
    for j in range(-(-lanes // LANES)):
        part = value[:, j * LANES : min((j + 1) * LANES, lanes)]
        if part.shape[1] < LANES:
            part = jnp.concatenate(
                [part, jnp.zeros((rows, LANES - part.shape[1]), part.dtype)], axis=1
            )
        ref[at + j * per : at + (j + 1) * per] = part.astype(BF16).reshape(per, TILE_ROWS, LANES)


def block_kernel(*refs):
    count = 16
    sources, (block_out, grad_tok_out, sum_out, small_hbm) = refs[:count], refs[count : count + 4]
    inputs = refs[count + 4 : 2 * count + 4]
    results = refs[2 * count + 4 : 2 * count + 7]
    work = refs[2 * count + 7 : -2]
    load_sem, result_sem = refs[-2:]
    loads = [
        pltpu.make_async_copy(src, dst, load_sem.at[i])
        for i, (src, dst) in enumerate(zip(sources, inputs))
    ]
    stores = []

    def store(i, out):
        copy = pltpu.make_async_copy(results[i], out, result_sem.at[i])
        copy.start()
        stores.append(copy)

    finish = (
        lambda: store(0, block_out),
        lambda: store(1, grad_tok_out),
        lambda: store(2, small_hbm),
    )
    block_body(loads, stores, finish, *inputs, *results[:2], sum_out, results[2], *work)


def block_body(
    loads,
    stores,
    finish,
    tok_ref,
    attn_gain_ref,
    attn_shift_ref,
    w_qkv_ref,
    qv_bias_ref,
    w_out_ref,
    out_bias_ref,
    moe_gain_ref,
    moe_shift_ref,
    router_ref,
    w_in_ref,
    in_bias_ref,
    w_exp_ref,
    exp_bias_ref,
    route_ref,
    cot_ref,
    block_ref,
    grad_tok_ref,
    sum_out,
    small_out,
    held,
    landing,
    sum_ref,
    early_held,
    early_landing,
    late_held,
    late_landing,
    toks,
    normed,
    cots,
    moes,
    ghs,
    att_part,
    att_other,
    mix_part,
    gmoe_part,
    gmoe_other,
    gate_part,
    gate_other,
    gnorm_part,
    q_all,
    k_all,
    v_all,
    probs,
    ctx,
    gproj,
    slot_in,
    slot_cot,
    act_all,
    gpre_all,
    scaled_all,
    gslot_all,
    gback_all,
    attn_xhat,
    moe_xhat,
    hidden_ref,
    gh_ref,
    padded,
    route_pad,
    pair_send,
    pair_recv,
    send_sem,
    recv_sem,
    back_send,
    back_recv,
    small_send,
    small_recv,
    store_sem,
):
    place, ahead = places()
    barrier = pltpu.get_barrier_semaphore()
    peers = [(axis, d) for axis, group in GROUP.items() for d in range(1, group)]
    for axis, d in peers:
        pl.semaphore_signal(barrier, inc=1, device_id=ahead(axis, d), device_id_type=MESH)
    big = (3, 5, 10, 12)
    for i in [i for i in range(len(loads)) if i not in big] + list(big):
        loads[i].start()

    def remote(src, dst, send, recv, axis, distance=1):
        copy = pltpu.make_async_remote_copy(
            src_ref=src,
            dst_ref=dst,
            send_sem=send,
            recv_sem=recv,
            device_id=ahead(axis, distance),
            device_id_type=MESH,
        )
        copy.start()
        return copy

    unsent = []

    def exchange(i, src, dst):
        copy = remote(src, dst, pair_send.at[i], pair_recv.at[i], "pair")
        unsent.append(copy)
        return copy

    spots = [0]

    class Chain:
        def __init__(self, c, base, size):
            self.c, self.base, self.size, self.order = c, base, size, ORDERS[c % 2]
            self.first, self.whole = base, size
            self.k, self.back, self.copies = 0, PHASES - 1, []

        def send(self):
            axis = self.order[self.k]
            group, index = GROUP[axis], place[axis]
            self.spot, earlier, self.copies = spots[0], self.copies, []
            if axis == "z":
                n = self.size
                add_tiles(landing, self.spot + index * n, n, [(held, self.base)])
                spots[0] += group * n
            else:
                n = self.size // group
                spots[0] += (group - 1) * n
            for d in range(1, group):
                if axis == "z":
                    src, dst = self.base, self.spot + index * n
                else:
                    src, dst = self.base + (index + d) % group * n, self.spot + (d - 1) * n
                self.copies.append(
                    remote(
                        held.at[pl.ds(src, n)],
                        landing.at[pl.ds(dst, n)],
                        send_sem.at[self.c, self.k, d - 1],
                        recv_sem.at[self.c, self.k, d - 1],
                        axis,
                        d,
                    )
                )
            if axis != "z":
                self.base, self.size = self.base + index * n, n
            for copy in earlier:
                copy.wait_send()

        def send_back(self):
            axis = self.order[self.back]
            earlier, self.copies = self.copies, []
            part = sum_ref.at[pl.ds(self.base, self.size)]
            for d in range(1, GROUP[axis]):
                self.copies.append(
                    remote(
                        part,
                        part,
                        back_send.at[self.c, self.back, d - 1],
                        back_recv.at[self.c, self.back, d - 1],
                        axis,
                        d,
                    )
                )
            for copy in earlier:
                copy.wait_send()

        def advance(self):
            for copy in self.copies:
                copy.wait_recv()
            if self.k < PHASES:
                axis = self.order[self.k]
                n = self.size
                if axis == "z":
                    parts = [(landing, self.spot + j * n) for j in range(GROUP[axis])]
                    add_tiles(sum_ref, self.base, n, parts)
                else:
                    parts = [(landing, self.spot + j * n) for j in range(GROUP[axis] - 1)]
                    add_tiles(held, self.base, n, [(held, self.base)] + parts)
                self.k += 1
                if self.k < PHASES:
                    self.send()
                    return
            else:
                axis = self.order[self.back]
                self.base = self.base - place[axis] * self.size
                self.size = self.size * GROUP[axis]
            self.back -= 1
            if self.back >= 0:
                self.send_back()
                return
            rows = pl.ds(self.first, self.whole)
            copy = pltpu.make_async_copy(
                sum_ref.at[rows], sum_out.at[rows], store_sem.at[self.c]
            )
            copy.start()
            stores.append(copy)
            for copy in self.copies:
                copy.wait_send()

    class Small:
        def __init__(self, b, held, landing, rows):
            self.b, self.held, self.landing, self.rows = b, held, landing, rows
            self.k, self.copies = 0, []

        def send(self):
            k, axis = self.k, SMALL_ORDER[self.k]
            group, index = GROUP[axis], place[axis]
            earlier, self.copies = self.copies, []
            slot = 0
            if group > 2:
                slot = index
                self.landing[k, slot] = self.held[k]
            for d in range(1, group):
                self.copies.append(
                    remote(
                        self.held.at[k],
                        self.landing.at[k, slot],
                        small_send.at[self.b, k, d - 1],
                        small_recv.at[self.b, k, d - 1],
                        axis,
                        d,
                    )
                )
            for copy in earlier:
                copy.wait_send()

        def advance(self):
            for copy in self.copies:
                copy.wait_recv()
            k, axis = self.k, SMALL_ORDER[self.k]
            held, landing = self.held, self.landing
            if axis == "pair":
                row = lax.broadcasted_iota(jnp.int32, (self.rows, D), 0)
                other = jnp.where(row < SHARED_ROWS[self.b], landing[k, 0], 0.0)
                held[k + 1] = held[k] + other
            elif GROUP[axis] == 2:
                held[k + 1] = held[k] + landing[k, 0]
            else:
                held[k + 1] = landing[k, 0] + landing[k, 1] + landing[k, 2] + landing[k, 3]
            self.k += 1
            if self.k < len(SMALL_ORDER):
                self.send()
                return
            small_out[EARLY_ROWS * self.b : EARLY_ROWS * self.b + self.rows] = held[self.k]
            for copy in self.copies:
                copy.wait_send()

    early = Small(0, early_held, early_landing, EARLY_ROWS)
    late = Small(1, late_held, late_landing, LATE_ROWS)
    batches, start = [], 0
    for batch in BATCHES:
        batches.append([])
        for size in batch:
            batches[-1].append(Chain(2 * len(batches) - 2 + len(batches[-1]), start, size))
            start += size

    def send_batch(b):
        for chain in batches[b]:
            chain.send()

    def advance_batch(b):
        for chain in batches[b]:
            chain.advance()

    for i in range(len(loads)):
        if i not in big:
            loads[i].wait()

    def row_of(ref):
        return ref[...].astype(F32).reshape(1, D)

    attn_gain, attn_shift = row_of(attn_gain_ref), row_of(attn_shift_ref)
    moe_gain, moe_shift = row_of(moe_gain_ref), row_of(moe_shift_ref)
    out_bias = row_of(out_bias_ref)

    padded[:, SEQ - 5 :] = jnp.zeros((2, ROWS - SEQ + 5, D), F32)
    padded[0, :SEQ] = tok_ref[0].astype(F32)
    padded[1, :SEQ] = cot_ref[0].astype(F32)
    toks[0] = padded[0].astype(BF16)
    cots[0] = padded[1].astype(BF16)
    pl.semaphore_wait(barrier, len(peers))
    tok_copy = exchange(0, toks.at[0], toks.at[1])
    cot_copy = exchange(1, cots.at[0], cots.at[1])
    xhat, attn_r = normalize(padded[0])
    attn_xhat[...] = xhat
    normed[0] = (xhat * attn_gain + attn_shift).astype(BF16)

    key_mask = lax.broadcasted_iota(jnp.int32, (ROWS, ROWS), 1) < SEQ

    def project(i):
        proj = dot(normed[i], w_qkv_ref[...], LAST)
        bias = qv_bias_ref[...].astype(F32)
        for h in range(HEADS):
            at = h * 3 * HD
            q_all[i, h] = (proj[:, at : at + HD] + bias[h : h + 1, :HD]).astype(BF16)
            k_all[i, h] = proj[:, at + HD : at + 2 * HD].astype(BF16)
            v_all[i, h] = (proj[:, at + 2 * HD : at + 3 * HD] + bias[h : h + 1, HD:]).astype(BF16)

    def attend(i):
        total = jnp.zeros((ROWS, D), F32)
        for h in range(HEADS):
            scores = dot(q_all[i, h], k_all[i, h], LAST) * (1.0 / math.sqrt(HD))
            scores = jnp.where(key_mask, scores, -1e30)
            weights = jnp.exp(scores - jnp.max(scores, axis=-1, keepdims=True))
            p = weights / jnp.sum(weights, axis=-1, keepdims=True)
            probs[i, h] = p
            c = dot(p.astype(BF16), v_all[i, h]).astype(BF16)
            ctx[h, i] = c
            total += dot(c, w_out_ref[h * HD : (h + 1) * HD])
        return total

    tensor = lax.axis_index("tensor")
    before = (
        lax.broadcasted_iota(jnp.int32, (ROWS, ROWS), 1)
        < lax.broadcasted_iota(jnp.int32, (ROWS, ROWS), 0)
    ).astype(BF16)
    lane = lax.broadcasted_iota(jnp.int32, (ROWS, LANES), 1).astype(F32)
    sub = lax.broadcasted_iota(jnp.int32, (8, ROWS), 0).astype(F32)
    slot_lane = lax.broadcasted_iota(jnp.int32, (ROWS, CAP), 1).astype(F32)
    slot_sub = lax.broadcasted_iota(jnp.int32, (CAP, ROWS), 0).astype(F32)
    same = (
        lax.broadcasted_iota(jnp.int32, (ROWS, ROWS), 0)
        == lax.broadcasted_iota(jnp.int32, (ROWS, ROWS), 1)
    ).astype(BF16)
    pos_col, pos_row = [], []
    for i in range(2):
        route_pad[i] = jnp.full((2, ROWS), -1.0, F32)
        first, second = route_ref[0].astype(F32), route_ref[1].astype(F32)
        route_pad[i, :, :SEQ] = jnp.where(tensor == i, first, second)
        row = route_pad[i]
        col = dot(same, row.astype(BF16), LAST)
        a0, a1 = col[:, 0:1] == lane, col[:, 1:2] == lane
        f0, f1 = a0.astype(F32), a1.astype(F32)
        c0 = dot(before, f0.astype(BF16))
        c1 = dot(before, f1.astype(BF16)) + column_sum(f0)
        pos_col.append(jnp.where(a0, c0, jnp.where(a1, c1, -1.0)))
        a0, a1 = row[0:1] == sub, row[1:2] == sub
        f0, f1 = a0.astype(F32), a1.astype(F32)
        c0 = dot(f0.astype(BF16), before, LAST)
        c1 = dot(f1.astype(BF16), before, LAST) + jnp.sum(f0, axis=1, keepdims=True)
        pos_row.append(jnp.where(a0, c0, jnp.where(a1, c1, -1.0)))
    kept_row = [((p >= 0.0) & (p < CAP)).astype(F32) for p in pos_row]

    def dispatch(i, e):
        return (pos_col[i][:, e : e + 1] == slot_lane).astype(F32)

    def dispatch_t(i, e):
        return (pos_row[i][e : e + 1] == slot_sub).astype(F32)

    loads[3].wait()
    loads[5].wait()
    project(0)
    att_part[0] = attend(0).astype(BF16)
    att_copies = [exchange(2, att_part.at[0], att_other.at[1])]
    tok_copy.wait_recv()
    normed[1] = (normalize(toks[1].astype(F32))[0] * attn_gain + attn_shift).astype(BF16)
    project(1)
    att_part[1] = attend(1).astype(BF16)
    att_copies.append(exchange(3, att_part.at[1], att_other.at[0]))
    cot_copy.wait_recv()
    for i in range(2):
        for e in range(EXPERTS):
            slot_cot[e, i * CAP : (i + 1) * CAP] = dot(
                dispatch_t(i, e).astype(BF16), cots[i]
            ).astype(BF16)
    moe_r = [None, None]

    def norm_hidden(i):
        total = att_part[i].astype(F32) + att_other[i].astype(F32)
        hidden = toks[i].astype(F32) + total + out_bias
        if i == 0:
            hidden_ref[...] = hidden
        xhat, moe_r[i] = normalize(hidden)
        moe_xhat[i] = xhat
        moes[i] = (xhat * moe_gain + moe_shift).astype(BF16)

    router_rows = jnp.concatenate(
        [router_ref[...].astype(F32), jnp.zeros((8 - EXPERTS, D), F32)], axis=0
    )
    router = router_rows.astype(BF16)
    expert_rows = sub < EXPERTS

    def gate(i):
        logits = jnp.where(expert_rows, dot(router, moes[i], LAST), -1e30)
        weights = jnp.exp(logits - jnp.max(logits, axis=0, keepdims=True))
        return weights / column_sum(weights)

    gates, slot_weight = [None, None], [[None] * EXPERTS, [None] * EXPERTS]

    def fill_slots(i):
        gates[i] = gate(i)
        for e in range(EXPERTS):
            pick = dispatch_t(i, e)
            slot_in[e, i * CAP : (i + 1) * CAP] = dot(pick.astype(BF16), moes[i]).astype(BF16)
            slot_weight[i][e] = jnp.sum(pick * gates[i][e : e + 1], axis=1, keepdims=True)

    for i in (1, 0):
        att_copies[1 - i].wait_recv()
        norm_hidden(i)
        fill_slots(i)

    gate_rows = [[None] * EXPERTS, [None] * EXPERTS]
    early_held[0] = jnp.zeros((EARLY_ROWS, D), F32)
    loads[10].wait()
    loads[12].wait()
    for e in range(EXPERTS):
        weight = jnp.concatenate([slot_weight[0][e], slot_weight[1][e]], axis=0)
        pre = dot(slot_in[e], w_in_ref[e]) + in_bias_ref[e : e + 1].astype(F32)
        half = 0.5 * (1.0 + lax.erf(pre * (1.0 / math.sqrt(2.0))))
        act_all[e] = (pre * half).astype(BF16)
        slope = half + pre * jnp.exp(-0.5 * pre * pre) * (1.0 / math.sqrt(2.0 * math.pi))
        g = slot_cot[e].astype(F32)
        gs = (g * weight).astype(BF16)
        gslot_all[e] = gs
        gpre = (dot(gs, w_exp_ref[e], LAST) * slope).astype(BF16)
        gpre_all[e] = gpre
        gback_all[e] = dot(gpre, w_in_ref[e], LAST).astype(BF16)
        slot_out = dot(act_all[e], w_exp_ref[e])
        scaled_all[e] = (slot_out * weight).astype(BF16)
        slot_gate = jnp.sum(slot_out * g, axis=1, keepdims=True)
        for i in range(2):
            gate_rows[i][e] = column_sum(
                dispatch_t(i, e) * slot_gate[i * CAP : (i + 1) * CAP]
            )

        at = e * (IN_TILES + EXP_TILES)
        store_tiles(held, at, dot(slot_in[e], gpre_all[e], FIRST))
        store_tiles(held, at + IN_TILES, dot(act_all[e], gslot_all[e], FIRST))
        bias = column_sum(gpre_all[e].astype(F32))
        for j in range(FF // D):
            early_held[0, 9 + 2 * e + j : 10 + 2 * e + j] = bias[:, j * D : (j + 1) * D]
        if READY[e] is not None:
            send_batch(READY[e])

    def combine(i, ref):
        total = jnp.zeros((ROWS, D), F32)
        for e in range(EXPERTS):
            total += dot(dispatch(i, e).astype(BF16), ref[e, i * CAP : (i + 1) * CAP])
        return total

    def gate_grads(i):
        return jnp.concatenate(gate_rows[i] + [jnp.zeros((8 - EXPERTS, ROWS), F32)], axis=0)

    gmoe_copies, gate_copies = [], []
    for i in range(2):
        gate_part[i] = gate_grads(i)
        gate_copies.append(exchange(4 + i, gate_part.at[i], gate_other.at[1 - i]))
        gmoe_part[i] = combine(i, gback_all).astype(BF16)
        gmoe_copies.append(exchange(6 + i, gmoe_part.at[i], gmoe_other.at[1 - i]))
    mix_part[0] = combine(1, scaled_all).astype(BF16)
    mix_copy = exchange(8, mix_part.at[0], mix_part.at[1])
    for b in range(len(EXPERT_BATCHES)):
        advance_batch(b)

    own_mix = combine(0, scaled_all).astype(BF16).astype(F32)
    bias_rows = jnp.concatenate(
        [exp_bias_ref[...], jnp.zeros((8 - EXPERTS, D), BF16)], axis=0
    )
    share = gates[0] * kept_row[0]

    def hidden_back(i):
        bias_grad = dot(bias_rows, cots[i], LAST)
        gate_copies[1 - i].wait_recv()
        grad_gates = (gate_part[i] + gate_other[i] + bias_grad) * kept_row[i]
        grad_logits = gates[i] * (grad_gates - column_sum(gates[i] * grad_gates))
        router_back = dot(grad_logits, router_rows, FIRST, HIGHEST)
        gmoe_copies[1 - i].wait_recv()
        gmoe = gmoe_part[i].astype(F32) + gmoe_other[i].astype(F32) + router_back
        grad = cots[i].astype(F32) + norm_back(gmoe, moe_xhat[i], moe_r[i], moe_gain)
        ghs[i] = grad.astype(BF16)
        if i == 0:
            gh_ref[...] = grad
            early_held[0, 0:1] = column_sum(grad)
            early_held[0, 1:2] = column_sum(gmoe * moe_xhat[0])
            early_held[0, 2:3] = column_sum(gmoe)
            early_held[0, 3:6] = dot(grad_logits, moes[0].astype(F32), precision=HIGHEST)[:EXPERTS]
            early_held[0, 6:9] = dot(share, padded[1], precision=HIGHEST)[:EXPERTS]
            early.send()

    def attend_back(i):
        for h in range(HEADS):
            q, k, v, p = q_all[i, h], k_all[i, h], v_all[i, h], probs[i, h]
            gc = dot(ghs[i], w_out_ref[h * HD : (h + 1) * HD], LAST).astype(BF16)
            gp = dot(gc, v, LAST)
            row_dot = jnp.sum(gp * p, axis=-1, keepdims=True)
            graw = (p * (gp - row_dot) * (1.0 / math.sqrt(HD))).astype(BF16)
            at = h * 3 * HD
            gproj[i, :, at : at + HD] = dot(graw, k).astype(BF16)
            gproj[i, :, at + HD : at + 2 * HD] = dot(graw, q, FIRST).astype(BF16)
            gproj[i, :, at + 2 * HD : at + 3 * HD] = dot(p.astype(BF16), gc, FIRST).astype(BF16)

    hidden_back(1)
    attend_back(1)
    gnorm_part[0] = dot(gproj[1], w_qkv_ref[...]).astype(BF16)
    gnorm_copy = exchange(9, gnorm_part.at[0], gnorm_part.at[1])
    hidden_back(0)
    attend_back(0)

    both = gproj[...].reshape(2 * ROWS, QKV)
    at = MOE_TILES
    store_tiles(held, at, dot(both, normed[...].reshape(2 * ROWS, D), FIRST))
    at += QKV_TILES
    gh_both = ghs[...].reshape(2 * ROWS, D)
    for h in range(HEADS):
        grad = dot(ctx[h].reshape(2 * ROWS, HD), gh_both, FIRST)
        for j in range(D // LANES):
            tiles = grad[:, j * LANES : (j + 1) * LANES].astype(BF16)
            spot = at + j * (OUT_TILES // 3) + h * (HD // TILE_ROWS)
            held[spot : spot + HD // TILE_ROWS] = tiles.reshape(HD // TILE_ROWS, TILE_ROWS, LANES)
    at += OUT_TILES
    held[at:TILES] = jnp.zeros((TILES - at, TILE_ROWS, LANES), BF16)
    send_batch(len(EXPERT_BATCHES))
    late_held[0] = jnp.zeros((LATE_ROWS, D), F32)
    bias = column_sum(both.astype(F32))
    late_held[0, 2:3] = bias[:, :D]
    late_held[0, 3:4, 0 : QKV - D] = bias[:, D:]
    for b in range(len(EXPERT_BATCHES)):
        advance_batch(b)
    early.advance()
    mix_copy.wait_recv()
    block_ref[...] = (
        hidden_ref[...]
        + (own_mix + mix_part[1].astype(F32))
        + dot(share, bias_rows.astype(F32), FIRST, HIGHEST)
    ).astype(BF16)
    finish[0]()

    own_gnorm = dot(gproj[0], w_qkv_ref[...]).astype(BF16).astype(F32)
    gnorm_copy.wait_recv()
    gnorm = own_gnorm + gnorm_part[1].astype(F32)
    xhat = attn_xhat[...]
    late_held[0, 0:1] = column_sum(gnorm * xhat)
    late_held[0, 1:2] = column_sum(gnorm)
    late.send()
    grad_tok_ref[...] = (gh_ref[...] + norm_back(gnorm, xhat, attn_r, attn_gain)).astype(BF16)
    finish[1]()

    for k in range(2 * PHASES - 1):
        advance_batch(len(EXPERT_BATCHES))
        if k < len(SMALL_ORDER):
            late.advance()
        if k < 2 * PHASES - 3:
            for b in range(len(EXPERT_BATCHES)):
                advance_batch(b)
        if k < len(SMALL_ORDER) - 1:
            early.advance()
    finish[2]()
    for copy in stores:
        copy.wait()
    for copy in unsent:
        copy.wait_send()


def run_block(*args):
    def bf(*shape):
        return pltpu.VMEM(shape, BF16)

    def fl(*shape):
        return pltpu.VMEM(shape, F32)

    dma = pltpu.SemaphoreType.DMA
    slots = 2 * CAP
    steps = len(SMALL_ORDER)
    anywhere = pl.BlockSpec(memory_space=pl.ANY)
    return pl.pallas_call(
        block_kernel,
        out_shape=(
            jax.ShapeDtypeStruct((ROWS, D), BF16),
            jax.ShapeDtypeStruct((ROWS, D), BF16),
            jax.ShapeDtypeStruct((TILES, TILE_ROWS, LANES), BF16),
            jax.ShapeDtypeStruct((EARLY_ROWS + LATE_ROWS, D), F32),
        ),
        in_specs=[anywhere] * len(args),
        out_specs=[anywhere] * 4,
        scratch_shapes=[
            *(pltpu.VMEM(arg.shape, arg.dtype) for arg in args),
            bf(ROWS, D),
            bf(ROWS, D),
            fl(EARLY_ROWS + LATE_ROWS, D),
            bf(TILES, TILE_ROWS, LANES),
            bf(LANDING, TILE_ROWS, LANES),
            bf(TILES, TILE_ROWS, LANES),
            fl(steps + 1, EARLY_ROWS, D),
            fl(steps, RING, EARLY_ROWS, D),
            fl(steps + 1, LATE_ROWS, D),
            fl(steps, RING, LATE_ROWS, D),
            bf(2, ROWS, D),
            bf(2, ROWS, D),
            bf(2, ROWS, D),
            bf(2, ROWS, D),
            bf(2, ROWS, D),
            bf(2, ROWS, D),
            bf(2, ROWS, D),
            bf(2, ROWS, D),
            bf(2, ROWS, D),
            bf(2, ROWS, D),
            fl(2, 8, ROWS),
            fl(2, 8, ROWS),
            bf(2, ROWS, D),
            bf(2, HEADS, ROWS, HD),
            bf(2, HEADS, ROWS, HD),
            bf(2, HEADS, ROWS, HD),
            fl(2, HEADS, ROWS, ROWS),
            bf(HEADS, 2, ROWS, HD),
            bf(2, ROWS, QKV),
            bf(EXPERTS, slots, D),
            bf(EXPERTS, slots, D),
            bf(EXPERTS, slots, FF),
            bf(EXPERTS, slots, FF),
            bf(EXPERTS, slots, D),
            bf(EXPERTS, slots, D),
            bf(EXPERTS, slots, D),
            fl(ROWS, D),
            fl(2, ROWS, D),
            fl(ROWS, D),
            fl(ROWS, D),
            fl(2, ROWS, D),
            fl(2, 2, ROWS),
            dma((10,)),
            dma((10,)),
            dma((CHAIN_COUNT, PHASES, RING - 1)),
            dma((CHAIN_COUNT, PHASES, RING - 1)),
            dma((CHAIN_COUNT, PHASES - 1, RING - 1)),
            dma((CHAIN_COUNT, PHASES - 1, RING - 1)),
            dma((2, steps, RING - 1)),
            dma((2, steps, RING - 1)),
            dma((CHAIN_COUNT,)),
            dma((len(args),)),
            dma((3,)),
        ],
        compiler_params=pltpu.CompilerParams(
            collective_id=0, has_side_effects=True, vmem_limit_bytes=56 * 1024 * 1024
        ),
    )(*args)


WIDE = (4, 6, 11, 13)


def unpack_kernel(*refs):
    sources, outs, held = refs[:4], refs[4:19], refs[19:38]
    in_sem, out_sem, rest_in, rest_out = refs[38:]
    block_ref, grad_tok_ref, sums, small_ref = held[:4]
    results = held[4:]
    block, grad_tok, attn_gain, attn_shift, w_qkv, qv_bias, w_out = results[:7]
    out_bias, moe_gain, moe_shift, router, w_in, in_bias, w_exp, exp_bias = results[7:]
    sum_ref = sources[2]
    w_qkv_out, w_out_out, w_in_out, w_exp_out = (outs[i] for i in WIDE)
    pieces = []
    for e in range(EXPERTS):
        at = e * (IN_TILES + EXP_TILES)
        pieces.append((at, IN_TILES, D, FF, w_in.at[e], w_in_out.at[e]))
        pieces.append((at + IN_TILES, EXP_TILES, FF, D, w_exp.at[e], w_exp_out.at[e]))
    at = MOE_TILES
    pieces.append((at, QKV_TILES, QKV, D, w_qkv, w_qkv_out))
    pieces.append((at + QKV_TILES, OUT_TILES, HEADS * HD, D, w_out, w_out_out))
    arriving = []
    for i, (at, tiles, *_) in enumerate(pieces):
        rows = pl.ds(at, tiles)
        arriving.append(pltpu.make_async_copy(sum_ref.at[rows], sums.at[rows], in_sem.at[i]))
        arriving[-1].start()
    narrow = [
        pltpu.make_async_copy(sources[i], held[i], rest_in.at[i]) for i in (0, 1, 3)
    ]
    for copy in narrow:
        copy.start()
    for copy in narrow:
        copy.wait()
    block[0] = block_ref[:SEQ]
    grad_tok[0] = grad_tok_ref[:SEQ]
    small = small_ref[...]
    rows = (16, 17, 0, 1, 2)
    for ref, row in zip((attn_gain, attn_shift, out_bias, moe_gain, moe_shift), rows):
        ref[...] = small[row]
    router[...] = small[3:6]
    exp_bias[...] = small[6:9]
    for e in range(EXPERTS):
        for j in range(FF // D):
            in_bias[e : e + 1, j * D : (j + 1) * D] = small[9 + 2 * e + j : 10 + 2 * e + j]
    bias = jnp.concatenate([small[18:19], small[19:20]], axis=1)
    for h in range(HEADS):
        at = 3 * h * HD
        qv_bias[h : h + 1, :HD] = bias[:, at : at + HD]
        qv_bias[h : h + 1, HD:] = bias[:, at + 2 * HD : at + 3 * HD]
    leaving = []
    for i in range(len(outs)):
        if i not in WIDE:
            leaving.append(pltpu.make_async_copy(results[i], outs[i], rest_out.at[i]))
            leaving[-1].start()
    for i, (at, tiles, rows, lanes, piece, out) in enumerate(pieces):
        arriving[i].wait()
        per = rows // TILE_ROWS
        for j in range(-(-lanes // LANES)):
            width = min(LANES, lanes - j * LANES)
            part = sums[at + j * per : at + (j + 1) * per].reshape(rows, LANES)
            piece[:, j * LANES : j * LANES + width] = part[:, :width].astype(F32)
        leaving.append(pltpu.make_async_copy(piece, out, out_sem.at[i]))
        leaving[-1].start()
    for copy in leaving:
        copy.wait()


def unpack(*args):
    def out(shape, dtype=F32):
        return jax.ShapeDtypeStruct(shape, dtype)

    anywhere = pl.BlockSpec(memory_space=pl.ANY)
    shapes = (
        out((1, SEQ, D), BF16),
        out((1, SEQ, D), BF16),
        out((D,)),
        out((D,)),
        out((QKV, D)),
        out((HEADS, 2 * HD)),
        out((HEADS * HD, D)),
        out((D,)),
        out((D,)),
        out((D,)),
        out((EXPERTS, D)),
        out((EXPERTS, D, FF)),
        out((EXPERTS, FF)),
        out((EXPERTS, FF, D)),
        out((EXPERTS, D)),
    )
    return pl.pallas_call(
        unpack_kernel,
        out_shape=shapes,
        in_specs=[anywhere] * 4,
        out_specs=[anywhere] * len(shapes),
        scratch_shapes=[
            *(pltpu.VMEM(leaf.shape, leaf.dtype) for leaf in args + shapes),
            pltpu.SemaphoreType.DMA((8,)),
            pltpu.SemaphoreType.DMA((8,)),
            pltpu.SemaphoreType.DMA((4,)),
            pltpu.SemaphoreType.DMA((len(shapes),)),
        ],
        compiler_params=pltpu.CompilerParams(vmem_limit_bytes=58 * 1024 * 1024),
    )(*args)


def on_device(
    tokens,
    attn_gain,
    attn_shift,
    w_qkv,
    qv_bias,
    w_out,
    out_bias,
    moe_gain,
    moe_shift,
    router,
    w_in,
    in_bias,
    w_exp,
    exp_bias,
    routes,
    cotangent,
):
    outs = list(
        unpack(
            *run_block(
                tokens,
                attn_gain,
                attn_shift,
                jnp.transpose(w_qkv, (1, 2, 0)).reshape(QKV, D),
                qv_bias,
                w_out.reshape(HEADS * HD, D),
                out_bias,
                moe_gain,
                moe_shift,
                router.T,
                w_in,
                in_bias,
                w_exp,
                exp_bias,
                jnp.transpose(routes, (0, 2, 1)),
                cotangent,
            )
        )
    )
    outs[4] = jnp.transpose(outs[4].reshape(HEADS, 3 * HD, D), (2, 0, 1))
    outs[10] = outs[10].T
    outs[6] = outs[6].reshape(HEADS, HD, D)
    return tuple(outs)


def solution(mesh):
    placed = (
        P(("dp", "tensor"), None, None),
        P(),
        P(),
        P(None, "tensor", None),
        P("tensor", None),
        P("tensor", None, None),
        P(),
        P(),
        P(),
        P(),
        P(None, None, "tensor"),
        P(None, "tensor"),
        P(None, "tensor", None),
        P(),
        P("dp", None, None),
        P(("dp", "tensor"), None, None),
    )
    return jax.shard_map(
        on_device,
        mesh=mesh,
        in_specs=placed,
        out_specs=(
            P(("dp", "tensor"), None, None),
            P(("dp", "tensor"), None, None),
            P(),
            P(),
            P(None, "tensor", None),
            P("tensor", None),
            P("tensor", None, None),
            P(),
            P(),
            P(),
            P(),
            P(None, None, "tensor"),
            P(None, "tensor"),
            P(None, "tensor", None),
            P(),
        ),
        check_vma=False,
    )
```
